256 devices in a mesh: row: 16 (over x, y), col: 16 (over z, core).
Axes of the slice: x: 4, y: 4, z: 8, core: 2. Of those that a mesh axis runs over, the one named last changes fastest.
Arguments:
- diag_tiles: float32 [1, 16, 1024, 1024], P(None, 'row', 'col')
- left_factors: bfloat16 [1, 16, 1, 16, 1024, 256], P(None, 'row', None, 'col'), as said below
- right_factors: bfloat16 [1, 16, 1, 16, 1024, 256], P(None, 'row', None, 'col'), as said below
- ranks: int32 [1, 16, 1, 16], P(None, 'row', None, 'col'), may hold values from 32 to 256, as said below
Outputs:
- new_diag: float32 [1, 16, 1024, 1024], P(None, 'row', 'col')
- updates: bfloat16 [1, 16, 1, 16, 1024, 768], P(None, 'row', None, 'col')
The draws below stay inside these ranges and needn't reach their ends.
Inputs may be any that keep to these rules, and one draw needn't show every extreme that they name: `ranks`: every tile (i, i - 1) has rank 256. `left_factors`: columns at or beyond a tile's rank hold values that are not read. `right_factors`: columns at or beyond a tile's rank hold values that are not read.
All inputs are finite; a program needn't handle non-finite values.
Results may differ from the reference program's by a relative error of at most 0.014.
Values may be sent and summed in bfloat16 or wider, within the bound.
No kernel may reach another device: no remote copies, remote signals or barrier semaphores. Data moves between devices by JAX's collectives and lax.ppermute only.
A program may use at most 128 MiB of HBM per device.

```python
import jax
import jax.numpy as jnp
from jax import lax

NB = 1024
R = 256
MT = 16
TA = 1
TB = 1
N_ROW = 16
N_COL = 16


def basis_tiles(key):
    sign_key, freq_key = jax.random.split(key)
    signs = jax.random.randint(sign_key, (MT, MT, NB, 1), 0, 2, dtype=jnp.int32) * 2 - 1
    tile_keys = jax.random.split(freq_key, MT * MT)
    freqs = jax.vmap(lambda one: jax.random.permutation(one, NB - 1)[:R] + 1)(tile_keys)
    freqs = freqs.reshape(MT, MT, 1, R).astype(jnp.int32)
    odd_rows = (2 * jnp.arange(NB, dtype=jnp.int32) + 1).reshape(1, 1, NB, 1)
    phase = odd_rows * freqs % (4 * NB)
    angle = phase.astype(jnp.float32) * (jnp.pi / (2.0 * NB))
    return signs.astype(jnp.float32) * jnp.cos(angle) * (2.0 / NB) ** 0.5


def draw_diag_tiles(key, part):
    key = jax.random.fold_in(key, 11)
    first_key, second_key = jax.random.split(key)
    raw = jax.random.normal(first_key, (MT, NB, NB), jnp.float32)
    heights = jax.random.uniform(second_key, (MT, 1, NB), jnp.float32, 4.8, 5.2)
    symmetric = (raw + jnp.swapaxes(raw, 1, 2)) * (1.0 / (2.0 * NB) ** 0.5)
    tiles = symmetric + jnp.eye(NB, dtype=jnp.float32)[None] * heights
    return tiles.reshape(TA, N_ROW, NB, NB)


def draw_left_factors(key, part):
    key = jax.random.fold_in(key, 31)
    basis_key, scale_key = jax.random.split(key)
    basis = basis_tiles(basis_key)
    scales = jax.random.uniform(scale_key, (MT, MT, 1, R), jnp.float32, 0.95, 1.0)
    tiles = basis * scales * 2.0 ** 0.5
    return tiles.reshape(TA, N_ROW, TB, N_COL, NB, R).astype(jnp.bfloat16)


def draw_right_factors(key, part):
    key = jax.random.fold_in(key, 37)
    basis_key, scale_key = jax.random.split(key)
    basis = basis_tiles(basis_key)
    column = jnp.arange(R, dtype=jnp.float32).reshape(1, 1, 1, R) / R
    scales = jax.random.uniform(scale_key, (MT, MT, 1, R), jnp.float32, 0.95, 1.0) * (1.0 - 0.1 * column)
    tiles = basis * scales * 2.75 ** 0.5
    return tiles.reshape(TA, N_ROW, TB, N_COL, NB, R).astype(jnp.bfloat16)


def draw_ranks(key, part):
    key = jax.random.fold_in(key, 23)
    drawn = jax.random.randint(key, (MT, MT), R // 8, R + 1, dtype=jnp.int32)
    rows_at = jnp.arange(MT, dtype=jnp.int32)[:, None]
    cols_at = jnp.arange(MT, dtype=jnp.int32)[None, :]
    drawn = jnp.where(rows_at == cols_at + 1, R, drawn)
    return drawn.reshape(TA, N_ROW, TB, N_COL)


def setup_inputs(seed: int = 0) -> dict:
    splits = jax.random.split(jax.random.key(seed), 5)
    return {
        "diag_tiles": draw_diag_tiles(jax.random.fold_in(splits[4], 71), 0),
        "left_factors": draw_left_factors(jax.random.fold_in(splits[4], 71), 0),
        "right_factors": draw_right_factors(jax.random.fold_in(splits[4], 71), 0),
        "ranks": draw_ranks(jax.random.fold_in(splits[4], 71), 0),
    }


def lower_solve(low_b, rhs):
    low = low_b.astype(jnp.float32)
    count, order, width = rhs.shape
    flat = jnp.transpose(rhs, (1, 0, 2)).reshape(order, count * width)
    solved = lax.linalg.triangular_solve(low, flat, left_side=True, lower=True)
    return jnp.transpose(solved.reshape(order, count, width), (1, 0, 2))

def reference(diag_tiles, left_factors, right_factors, ranks):
    diag = diag_tiles.reshape(MT, NB, NB)
    left = left_factors.reshape(MT, MT, NB, R)
    right = right_factors.reshape(MT, MT, NB, R)
    rank_grid = ranks.reshape(MT, MT)
    keep = jnp.arange(R)[None, None, None, :] < rank_grid[:, :, None, None]
    left_kept = jnp.where(keep, left, jnp.zeros((), jnp.bfloat16))
    right_kept = jnp.where(keep, right, jnp.zeros((), jnp.bfloat16))
    index = jnp.arange(MT)
    low0 = jnp.linalg.cholesky(diag[0])
    low0_b = low0.astype(jnp.bfloat16)
    panel0 = lower_solve(low0_b, right_kept[:, 0].astype(jnp.float32))
    panel0 = jnp.where((index > 0)[:, None, None], panel0, 0.0).astype(jnp.bfloat16)
    inner0 = jnp.einsum('inr,jns->ijrs', panel0.astype(jnp.float32), panel0.astype(jnp.float32)).astype(jnp.bfloat16)
    corr0 = jnp.einsum('inr,ijrs->ijns', left_kept[:, 0].astype(jnp.float32), inner0.astype(jnp.float32)).astype(jnp.bfloat16)
    self0 = corr0[index, index]
    diag1 = diag - jnp.einsum('inr,imr->inm', self0.astype(jnp.float32), left_kept[:, 0].astype(jnp.float32))
    low1 = jnp.linalg.cholesky(diag1[1])
    low1_b = low1.astype(jnp.bfloat16)
    left1 = jnp.concatenate([left_kept[:, 1], -corr0[:, 1]], axis=-1)
    shared = jnp.broadcast_to(left_kept[1, 0][None], (MT, NB, R))
    right1 = jnp.concatenate([right_kept[:, 1], shared], axis=-1)
    panel1 = lower_solve(low1_b, right1.astype(jnp.float32))
    panel1 = jnp.where((index > 1)[:, None, None], panel1, 0.0).astype(jnp.bfloat16)
    inner1 = jnp.einsum('inr,jns->ijrs', panel1.astype(jnp.float32), panel1.astype(jnp.float32)).astype(jnp.bfloat16)
    corr1 = jnp.einsum('inr,ijrs->ijns', left1.astype(jnp.float32), inner1.astype(jnp.float32)).astype(jnp.bfloat16)
    self1 = corr1[index, index]
    diag2 = diag1 - jnp.einsum('inr,imr->inm', self1.astype(jnp.float32), left1.astype(jnp.float32))
    new_diag = diag2.at[0].set(low0).at[1].set(low1)
    rows_at = index[:, None]
    cols_at = index[None, :]
    zero_b = jnp.zeros((), jnp.bfloat16)
    first = jnp.where((cols_at == 0)[:, :, None, None], panel0[:, None], jnp.where(((rows_at > cols_at) & (cols_at > 0))[:, :, None, None], corr0, zero_b))
    second = jnp.where((cols_at == 1)[:, :, None, None], panel1[:, None], jnp.where(((rows_at > cols_at) & (cols_at > 1))[:, :, None, None], corr1, zero_b))
    updates = jnp.concatenate([first, second], axis=-1).reshape(MT // N_ROW, N_ROW, MT // N_COL, N_COL, NB, 3 * R)
    return (new_diag.reshape(MT // N_ROW, N_ROW, NB, NB), updates)
```

```python
import functools

import jax
import jax.numpy as jnp
from jax import lax
from jax.experimental import pallas as pl
from jax.experimental.pallas import tpu as pltpu
from jax.sharding import PartitionSpec as P

F32 = jnp.float32
BF16 = jnp.bfloat16
NB = 1024
RANK = 256
BLK = 128
NBLK = NB // BLK
BAND = 5 * BLK
TN = (((0,), (0,)), ((), ()))
NT = (((1,), (1,)), ((), ()))
VMEM = pl.BlockSpec(memory_space=pltpu.VMEM)
SMEM = pl.BlockSpec(memory_space=pltpu.SMEM)
ANY = pl.BlockSpec(memory_space=pl.ANY)
PARAMS = pltpu.CompilerParams(vmem_limit_bytes=56 * 1024 * 1024)


def lanes_of(x, c):
    return jnp.broadcast_to(x[:, c : c + 1], (8, BLK))


def rows_of(x, r):
    return jnp.broadcast_to(x[r : r + 1, :], (8, BLK))


def factor_block(rows):
    sub = lax.broadcasted_iota(jnp.int32, (8, BLK), 0)
    lane = lax.broadcasted_iota(jnp.int32, (8, BLK), 1)
    a = list(rows)
    n = len(a)
    up, inv = [], []
    cols = [lanes_of(a[0], m) for m in range(8)]
    for g in range(n):
        c0 = 8 * g
        here = (lane >= c0) & (lane < c0 + 8)
        left = [[lanes_of(a[b], c0 + m) for m in range(8)] for b in range(g + 1, n)]
        ahead = [lanes_of(a[g + 1], c0 + 8 + m) for m in range(8)] if g + 1 < n else None
        mult, recip, piv = [], [], None
        for k in range(8):
            d = rows_of(cols[k], k)
            r = 1.0 / d
            recip.append(r)
            piv = d if piv is None else jnp.where(sub == k, d, piv)
            for m in range(k + 1, 8):
                cols[m] = cols[m] - (cols[k] * rows_of(cols[k], m)) * r
            mult.append(jnp.where(sub > k, cols[k] * r, 0.0))
        s = jnp.where(here, jnp.where(lane == c0 + sub, 1.0, 0.0), a[g])
        s2 = a[g]
        for k in range(7):
            s = s - mult[k] * rows_of(s, k)
            s2 = s2 - mult[k] * rows_of(s2, k)
        root = lax.rsqrt(piv)
        r_ = s * root
        t = r_ * root
        diag = jnp.where(lane >= c0 + sub, s2 * root, 0.0)
        up.append(jnp.where(here, diag, jnp.where(lane >= c0 + 8, r_, 0.0)))
        inv.append(jnp.where(lane < c0 + 8, r_, 0.0))
        if g + 1 == n:
            break
        mk = [[rows_of(mult[k], m) if m > k else None for m in range(8)] for k in range(8)]
        tk = [rows_of(t, k) for k in range(8)]
        for b in range(g + 1, n):
            x = left[b - g - 1]
            for k in range(8):
                for m in range(k + 1, 8):
                    x[m] = x[m] - x[k] * mk[k][m]
            if b == g + 1:
                cols = ahead
                for k in range(8):
                    xs = x[k] * recip[k]
                    for m in range(8):
                        cols[m] = cols[m] - x[k] * rows_of(xs, m)
            new = jnp.where(here, 0.0, a[b])
            for k in range(8):
                new = new - x[k] * tk[k]
            a[b] = new
    return up, inv


def split(x):
    hi = x.astype(BF16)
    return hi, (x - hi.astype(F32)).astype(BF16)


def mm(a, b):
    return jnp.dot(a, b, preferred_element_type=F32)


def mm3(a, b):
    return mm(a[0], b[0]) + (mm(a[0], b[1]) + mm(a[1], b[0]))


def unfold(raw, work, take):
    for r in range(NBLK):
        n = min(5, NBLK - r)
        rows = slice(r * BLK, (r + 1) * BLK)
        work[rows, r * BLK : (r + n) * BLK] = take(r, slice(0, n * BLK))
        for c in range(r + 5, NBLK):
            o = (NBLK - (c - r)) * BLK
            work[rows, c * BLK : (c + 1) * BLK] = take(c, slice(o, o + BLK)).T


def cholesky_blocks(work, lb, mh, ml, inv_s):
    def body(k, _):
        off = pl.multiple_of(k * BLK, BLK)
        rows = [work[pl.ds(pl.multiple_of(off + 8 * i, 8), 8), pl.ds(off, BLK)] for i in range(16)]
        up, inv = factor_block(rows)
        for i in range(16):
            inv_s[8 * i : 8 * i + 8, :] = inv[i]
        work[pl.ds(off, BLK), pl.ds(off, BLK)] = jnp.concatenate(up, axis=0).T
        hi, lo = split(inv_s[...])
        mh[pl.ds(off, BLK), :] = hi
        ml[pl.ds(off, BLK), :] = lo
        for kk in range(NBLK - 1):

            @pl.when(k == kk)
            def _():
                o = BLK * kk
                e = o + BLK
                upper = mm3((hi, lo), split(work[o:e, e:]))
                parts = split(upper)
                for ib in range(kk + 1, NBLK):
                    i0 = BLK * ib
                    c = i0 - e
                    low = upper[:, c : c + BLK].T
                    lows = split(low)
                    lb[i0 : i0 + BLK, o:e] = lows[0]
                    work[i0 : i0 + BLK, o:e] = low
                    work[i0 : i0 + BLK, i0:] = work[i0 : i0 + BLK, i0:] - mm3(
                        lows, (parts[0][:, c:], parts[1][:, c:])
                    )

        return 0

    lax.fori_loop(0, NBLK, body, 0)


def write_rows(place, work, lrow):
    start = pl.multiple_of(64 * (2 * place[0] + place[1]), 64)
    r = lax.broadcasted_iota(jnp.int32, (64, NB), 0) + start
    c = lax.broadcasted_iota(jnp.int32, (64, NB), 1)
    lrow[...] = jnp.where(c <= r, work[pl.ds(start, 64), :], 0.0)


def first_kernel(place, *refs):
    shards = refs[:16]
    lrow, lb, mh, ml, raw, work, inv_s, sems = refs[16:]
    z, core = place[0], place[1]
    copies = []
    for i in range(16):
        n = lax.rem(z + i % 8, 8)
        half = core if i < 8 else 1 - core
        start = pl.multiple_of(n * BLK + half * 64, 64)
        copies.append(pltpu.make_async_copy(shards[i], raw.at[pl.ds(start, 64), :], sems.at[i]))
    for one in copies:
        one.start()
    for one in copies:
        one.wait()
    unfold(raw, work, lambda r, cols: raw[r * BLK : (r + 1) * BLK, cols])
    cholesky_blocks(work, lb, mh, ml, inv_s)
    write_rows(place, work, lrow)


def solve_step(k, w, lb, mh, ml, p):
    o = BLK * k
    e = o + BLK
    x = mm3((mh[o:e, :], ml[o:e, :]), split(w[o:e, :]))
    p[o:e, :] = x.astype(BF16)
    if e < NB:
        xs = split(x)
        low = lb[e:, o:e]
        w[e:, :] = w[e:, :] - (mm(low, xs[0]) + mm(low, xs[1]))


def second_kernel(place, raw, uv, lb0, mh0, ml0, lrow, lb, mh, ml, p10, work, w, inv_s):
    w[...] = uv[:, RANK:].astype(F32)
    for k in range(NBLK):
        solve_step(k, w, lb0, mh0, ml0, p10)
    solved = p10[...]
    inner = lax.dot_general(solved, solved, TN, preferred_element_type=F32).astype(BF16)
    u = uv[:, :RANK]
    corr = split(mm(u, inner))
    unfold(raw, work, lambda r, cols: raw[r * BLK : (r + 1) * BLK, cols])
    for r in range(NBLK):
        o = r * BLK
        right = u[o:, :]
        work[o : o + BLK, o:] = work[o : o + BLK, o:] - (
            lax.dot_general(corr[0][o : o + BLK], right, NT, preferred_element_type=F32)
            + lax.dot_general(corr[1][o : o + BLK], right, NT, preferred_element_type=F32)
        )
    cholesky_blocks(work, lb, mh, ml, inv_s)
    write_rows(place, work, lrow)


def last_kernel(
    place, rows, cols, uv, p10, diag, lrow0, lrow1, lb0, mh0, ml0, lb1, mh1, ml1, new, upd, w0, w1, p0, p1
):
    j = 2 * place[0] + place[1]
    i = place[2]
    w0[:, :RANK] = rows[:, RANK : 2 * RANK].astype(F32)
    w0[:, RANK:] = cols[:, :RANK].astype(F32)
    w1[:, :RANK] = rows[:, 3 * RANK :].astype(F32)
    w1[:, RANK : 2 * RANK] = uv[:, :RANK].astype(F32)
    w1[:, 2 * RANK :] = cols[:, RANK:].astype(F32)
    for k in range(NBLK):
        solve_step(k, w0, lb0, mh0, ml0, p0)
        solve_step(k, w1, lb1, mh1, ml1, p1)
    zero = jnp.zeros((), BF16)

    def tn(a, b):
        return lax.dot_general(a, b, TN, preferred_element_type=F32).astype(BF16)

    pi = jnp.where(i > 0, p0[:, :RANK], zero)
    pj = jnp.where(j > 0, p0[:, RANK:], zero)
    ui = rows[:, :RANK]
    start = pl.multiple_of(64 * j, 64)
    ui_part = rows[pl.ds(start, 64), :RANK]
    c0 = mm(ui, tn(pi, pj)).astype(BF16)
    c01 = mm(ui, tn(pi, p10[...])).astype(BF16)
    c0_part = mm(ui_part, tn(pi, pi)).astype(BF16)
    d = diag[...] - lax.dot_general(c0_part, ui, NT, preferred_element_type=F32)
    upd[:, :RANK] = jnp.where(j == 0, pi, jnp.where(i > j, c0, zero))
    q = jnp.where(i > 1, p1[...], zero)
    q_i = q[:, : 2 * RANK]
    q_j = jnp.concatenate([q[:, 2 * RANK :], q[:, RANK : 2 * RANK]], axis=1)
    up = jnp.concatenate([rows[:, 2 * RANK : 3 * RANK], -c01], axis=1)
    c1 = mm(up, tn(q_i, q_j)).astype(BF16)
    up_part = jnp.concatenate(
        [rows[pl.ds(start, 64), 2 * RANK : 3 * RANK], -mm(ui_part, tn(pi, p10[...])).astype(BF16)], axis=1
    )
    c1_part = mm(up_part, tn(q_i, q_i)).astype(BF16)
    d = d - lax.dot_general(c1_part, up, NT, preferred_element_type=F32)
    new[...] = jnp.where(i == 0, lrow0[...], jnp.where(i == 1, lrow1[...], d))
    upd[:, RANK:] = jnp.where(j == 1, q_i, jnp.where((i > j) & (j > 1), c1, zero))


def shape(rows, cols, dtype):
    return jax.ShapeDtypeStruct((rows, cols), dtype)


FACTOR = [shape(64, NB, F32), shape(NB, NB, BF16), shape(NB, BLK, BF16), shape(NB, BLK, BF16)]


def shift_z(x, s):
    return lax.ppermute(x, "col", [(2 * z + c, 2 * ((z + s) % 8) + c) for z in range(8) for c in range(2)])


def swap_core(x):
    return lax.ppermute(x, "col", [(c, c ^ 1) for c in range(16)])


def spread_pair(x, row_at):
    at_x, at_y = row_at // 4, row_at % 4
    cur = x
    for k in (1, 2, 3):
        got = lax.ppermute(x, "row", [(0, 4 * k), (1, 4 * k + 1)])
        cur = jnp.where(at_x == k, got, cur)
    got = [
        lax.ppermute(cur, "row", [(4 * a + y, 4 * a + (y + s) % 4) for a in range(4) for y in (0, 1)])
        for s in (1, 2, 3)
    ]

    def pick(home):
        out = cur
        for s in (1, 2, 3):
            out = jnp.where(at_y == (home + s) % 4, got[s - 1], out)
        return out

    return pick(0), pick(1)


def spread_one(x, row_at):
    at_x, at_y = row_at // 4, row_at % 4
    cur = x
    for k in (1, 2, 3):
        got = lax.ppermute(x, "row", [(1, 4 * k + 1)])
        cur = jnp.where(at_x == k, got, cur)
    out = cur
    for s in (1, 2, 3):
        got = lax.ppermute(cur, "row", [(4 * a + 1, 4 * a + (1 + s) % 4) for a in range(4)])
        out = jnp.where(at_y == (1 + s) % 4, got, out)
    return out


def shards(diag_tiles, left_factors, right_factors, ranks):
    row_at = lax.axis_index("row")
    col_at = lax.axis_index("col")
    z = col_at // 2
    place = jnp.stack([z, col_at % 2, row_at]).astype(jnp.int32)
    mine = diag_tiles[0, 0]
    band = lax.dynamic_slice(jnp.concatenate([mine, mine[:, :BAND]], axis=1), (0, BLK * z), (64, BAND))
    band0, band1 = spread_pair(band, row_at)

    fwd, bwd = [band0], [band0]
    for t in range(4):
        fwd.append(shift_z(fwd[-1], 1))
        if t < 3:
            bwd.append(shift_z(bwd[-1], -1))
    own = [band0, bwd[1], bwd[2], bwd[3], fwd[4], fwd[3], fwd[2], fwd[1]]
    pieces = own + [swap_core(x) for x in own]

    keep = jnp.arange(RANK)[None, :] < ranks[0, 0, 0, 0]
    zero = jnp.zeros((), BF16)
    both = jnp.concatenate(
        [jnp.where(keep, left_factors[0, 0, 0, 0], zero), jnp.where(keep, right_factors[0, 0, 0, 0], zero)], axis=1
    )
    parts = lax.all_to_all(both.reshape(16, 64, 2 * RANK), "col", 0, 0)
    chunk = jnp.concatenate([parts[0], parts[1]], axis=1)
    first = spread_one(parts[0], row_at)
    flip = lax.ppermute(
        jnp.concatenate([parts[0][:, RANK:], parts[1][:, RANK:]], axis=1),
        ("row", "col"),
        [(r * 16 + c, c * 16 + r) for r in range(16) for c in range(16)],
    )
    raw1 = lax.all_gather(band1, "col", tiled=True)
    uv = lax.all_gather(first, "col", tiled=True)
    rows = lax.all_gather(chunk, "col", tiled=True)
    cols = lax.all_gather(flip, "row", tiled=True)

    lrow0, lb0, mh0, ml0 = pl.pallas_call(
        first_kernel,
        out_shape=FACTOR,
        in_specs=[SMEM] + [ANY] * 16,
        out_specs=[VMEM] * 4,
        scratch_shapes=[
            pltpu.VMEM((NB, BAND), F32),
            pltpu.VMEM((NB, NB), F32),
            pltpu.VMEM((BLK, BLK), F32),
            pltpu.SemaphoreType.DMA((16,)),
        ],
        compiler_params=PARAMS,
        name="factor_first",
    )(place, *pieces)
    lrow1, lb1, mh1, ml1, p10 = pl.pallas_call(
        second_kernel,
        out_shape=FACTOR + [shape(NB, RANK, BF16)],
        in_specs=[SMEM] + [VMEM] * 5,
        out_specs=[VMEM] * 5,
        scratch_shapes=[pltpu.VMEM((NB, NB), F32), pltpu.VMEM((NB, RANK), F32), pltpu.VMEM((BLK, BLK), F32)],
        compiler_params=PARAMS,
        name="factor_second",
    )(place, raw1, uv, lb0, mh0, ml0)
    new, upd = pl.pallas_call(
        last_kernel,
        out_shape=[shape(64, NB, F32), shape(NB, 3 * RANK, BF16)],
        in_specs=[SMEM] + [VMEM] * 13,
        out_specs=[VMEM] * 2,
        scratch_shapes=[
            pltpu.VMEM((NB, 2 * RANK), F32),
            pltpu.VMEM((NB, 3 * RANK), F32),
            pltpu.VMEM((NB, 2 * RANK), BF16),
            pltpu.VMEM((NB, 3 * RANK), BF16),
        ],
        compiler_params=PARAMS,
        name="finish",
    )(place, rows, cols, uv, p10, mine, lrow0, lrow1, lb0, mh0, ml0, lb1, mh1, ml1)
    return new[None, None], upd[None, None, None, None]


def solution(mesh):
    in_specs = (
        P(None, "row", "col", None),
        P(None, "row", None, "col", None, None),
        P(None, "row", None, "col", None, None),
        P(None, "row", None, "col"),
    )
    out_specs = (P(None, "row", "col", None), P(None, "row", None, "col", None, None))
    return jax.shard_map(shards, mesh=mesh, in_specs=in_specs, out_specs=out_specs, check_vma=False)
```

```python
import functools

import jax
import jax.numpy as jnp
from jax import lax
from jax.experimental import pallas as pl
from jax.experimental.pallas import tpu as pltpu
from jax.sharding import PartitionSpec as P

F32 = jnp.float32
BF16 = jnp.bfloat16
NB = 1024
RANK = 256
BLK = 128
NBLK = NB // BLK
BAND = 5 * BLK
TN = (((0,), (0,)), ((), ()))
NT = (((1,), (1,)), ((), ()))
VMEM = pl.BlockSpec(memory_space=pltpu.VMEM)
SMEM = pl.BlockSpec(memory_space=pltpu.SMEM)


def grant(mib):
    return pltpu.CompilerParams(vmem_limit_bytes=mib * 1024 * 1024)


def lanes_of(x, c):
    return jnp.broadcast_to(x[:, c : c + 1], (8, BLK))


def rows_of(x, r):
    return jnp.broadcast_to(x[r : r + 1, :], (8, BLK))


def factor_block(rows):
    sub = lax.broadcasted_iota(jnp.int32, (8, BLK), 0)
    lane = lax.broadcasted_iota(jnp.int32, (8, BLK), 1)
    a = list(rows)
    n = len(a)
    up, inv = [], []
    cols = [lanes_of(a[0], m) for m in range(8)]
    for g in range(n):
        c0 = 8 * g
        here = (lane >= c0) & (lane < c0 + 8)
        left = [[lanes_of(a[b], c0 + m) for m in range(8)] for b in range(g + 1, n)]
        ahead = [lanes_of(a[g + 1], c0 + 8 + m) for m in range(8)] if g + 1 < n else None
        mult, recip, piv = [], [], None
        for k in range(8):
            d = rows_of(cols[k], k)
            r = 1.0 / d
            recip.append(r)
            piv = d if piv is None else jnp.where(sub == k, d, piv)
            for m in range(k + 1, 8):
                cols[m] = cols[m] - (cols[k] * rows_of(cols[k], m)) * r
            mult.append(jnp.where(sub > k, cols[k] * r, 0.0))
        s = jnp.where(here, jnp.where(lane == c0 + sub, 1.0, 0.0), a[g])
        s2 = a[g]
        for k in range(7):
            s = s - mult[k] * rows_of(s, k)
            s2 = s2 - mult[k] * rows_of(s2, k)
        root = lax.rsqrt(piv)
        r_ = s * root
        t = r_ * root
        diag = jnp.where(lane >= c0 + sub, s2 * root, 0.0)
        up.append(jnp.where(here, diag, jnp.where(lane >= c0 + 8, r_, 0.0)))
        inv.append(jnp.where(lane < c0 + 8, r_, 0.0))
        if g + 1 == n:
            break
        mk = [[rows_of(mult[k], m) if m > k else None for m in range(8)] for k in range(8)]
        tk = [rows_of(t, k) for k in range(8)]
        for b in range(g + 1, n):
            x = left[b - g - 1]
            for k in range(8):
                for m in range(k + 1, 8):
                    x[m] = x[m] - x[k] * mk[k][m]
            if b == g + 1:
                cols = ahead
                for k in range(8):
                    xs = x[k] * recip[k]
                    for m in range(8):
                        cols[m] = cols[m] - x[k] * rows_of(xs, m)
            new = jnp.where(here, 0.0, a[b])
            for k in range(8):
                new = new - x[k] * tk[k]
            a[b] = new
    return up, inv


def split(x):
    hi = x.astype(BF16)
    return hi, (x - hi.astype(F32)).astype(BF16)


def mm(a, b):
    return jnp.dot(a, b, preferred_element_type=F32)


def mm3(a, b):
    return mm(a[0], b[0]) + (mm(a[0], b[1]) + mm(a[1], b[0]))


def unfold(raw, work, take):
    for r in range(NBLK):
        n = min(5, NBLK - r)
        rows = slice(r * BLK, (r + 1) * BLK)
        work[rows, r * BLK : (r + n) * BLK] = take(r, slice(0, n * BLK))
        for c in range(r + 5, NBLK):
            o = (NBLK - (c - r)) * BLK
            work[rows, c * BLK : (c + 1) * BLK] = take(c, slice(o, o + BLK)).T


def cholesky_blocks(work, lb, mh, ml, inv_s):
    def body(k, _):
        off = pl.multiple_of(k * BLK, BLK)
        rows = [work[pl.ds(pl.multiple_of(off + 8 * i, 8), 8), pl.ds(off, BLK)] for i in range(16)]
        up, inv = factor_block(rows)
        for i in range(16):
            inv_s[8 * i : 8 * i + 8, :] = inv[i]
        work[pl.ds(off, BLK), pl.ds(off, BLK)] = jnp.concatenate(up, axis=0).T
        hi, lo = split(inv_s[...])
        mh[pl.ds(off, BLK), :] = hi
        ml[pl.ds(off, BLK), :] = lo
        for kk in range(NBLK - 1):

            @pl.when(k == kk)
            def _():
                o = BLK * kk
                e = o + BLK
                upper = mm3((hi, lo), split(work[o:e, e:]))
                parts = split(upper)
                for ib in range(kk + 1, NBLK):
                    i0 = BLK * ib
                    c = i0 - e
                    low = upper[:, c : c + BLK].T
                    lows = split(low)
                    lb[i0 : i0 + BLK, o:e] = lows[0]
                    work[i0 : i0 + BLK, o:e] = low
                    work[i0 : i0 + BLK, i0:] = work[i0 : i0 + BLK, i0:] - mm3(
                        lows, (parts[0][:, c:], parts[1][:, c:])
                    )

        return 0

    lax.fori_loop(0, NBLK, body, 0)


def write_rows(place, work, lrow):
    start = pl.multiple_of(64 * (2 * place[0] + place[1]), 64)
    r = lax.broadcasted_iota(jnp.int32, (64, NB), 0) + start
    c = lax.broadcasted_iota(jnp.int32, (64, NB), 1)
    lrow[...] = jnp.where(c <= r, work[pl.ds(start, 64), :], 0.0)


def first_kernel(place, *refs):
    own, other = refs[:8], refs[8:10]
    lrow, lb, mh, ml, raw, work, inv_s = refs[10:]
    z, core = place[0], place[1]
    for i in range(8):
        n = lax.rem(z + i, 8)
        raw[pl.ds(pl.multiple_of(n * BLK + core * 64, 64), 64), :] = own[i][...]
        theirs = other[1][...] if i == 4 else other[0][64 * (i - i // 5) : 64 * (i - i // 5 + 1), :]
        raw[pl.ds(pl.multiple_of(n * BLK + (1 - core) * 64, 64), 64), :] = theirs
    unfold(raw, work, lambda r, cols: raw[r * BLK : (r + 1) * BLK, cols])
    cholesky_blocks(work, lb, mh, ml, inv_s)
    write_rows(place, work, lrow)


def solve_step(k, w, lb, mh, ml, p):
    o = BLK * k
    e = o + BLK
    x = mm3((mh[o:e, :], ml[o:e, :]), split(w[o:e, :]))
    p[o:e, :] = x.astype(BF16)
    if e < NB:
        xs = split(x)
        low = lb[e:, o:e]
        w[e:, :] = w[e:, :] - (mm(low, xs[0]) + mm(low, xs[1]))


def second_kernel(place, raw, uv, lb0, mh0, ml0, lrow, lb, mh, ml, p10, work, w, inv_s):
    w[...] = uv[:, 5 * RANK :].astype(F32)
    for k in range(NBLK):
        solve_step(k, w, lb0, mh0, ml0, p10)
    solved = p10[...]
    inner = lax.dot_general(solved, solved, TN, preferred_element_type=F32).astype(BF16)
    u = uv[:, 4 * RANK : 5 * RANK]
    corr = split(mm(u, inner))
    unfold(raw, work, lambda r, cols: raw[r * BLK : (r + 1) * BLK, cols])
    for r in range(NBLK):
        o = r * BLK
        right = u[o:, :]
        work[o : o + BLK, o:] = work[o : o + BLK, o:] - (
            lax.dot_general(corr[0][o : o + BLK], right, NT, preferred_element_type=F32)
            + lax.dot_general(corr[1][o : o + BLK], right, NT, preferred_element_type=F32)
        )
    cholesky_blocks(work, lb, mh, ml, inv_s)
    write_rows(place, work, lrow)


def last_kernel(
    place, rows, cols, p10, diag, lrow0, lrow1, lb0, mh0, ml0, lb1, mh1, ml1, new, upd, w0, w1, p0, p1
):
    j = 2 * place[0] + place[1]
    i = place[2]
    w0[:, :RANK] = rows[:, RANK : 2 * RANK].astype(F32)
    w0[:, RANK:] = cols[:, :RANK].astype(F32)
    w1[:, :RANK] = rows[:, 3 * RANK : 4 * RANK].astype(F32)
    w1[:, RANK : 2 * RANK] = rows[:, 4 * RANK : 5 * RANK].astype(F32)
    w1[:, 2 * RANK :] = cols[:, RANK:].astype(F32)
    for k in range(NBLK):
        solve_step(k, w0, lb0, mh0, ml0, p0)
        solve_step(k, w1, lb1, mh1, ml1, p1)
    zero = jnp.zeros((), BF16)

    def tn(a, b):
        return lax.dot_general(a, b, TN, preferred_element_type=F32).astype(BF16)

    pi = jnp.where(i > 0, p0[:, :RANK], zero)
    pj = jnp.where(j > 0, p0[:, RANK:], zero)
    ui = rows[:, :RANK]
    start = pl.multiple_of(64 * j, 64)
    ui_part = rows[pl.ds(start, 64), :RANK]
    c0 = mm(ui, tn(pi, pj)).astype(BF16)
    c01 = mm(ui, tn(pi, p10[...])).astype(BF16)
    c0_part = mm(ui_part, tn(pi, pi)).astype(BF16)
    d = diag[...] - lax.dot_general(c0_part, ui, NT, preferred_element_type=F32)
    upd[:, :RANK] = jnp.where(j == 0, pi, jnp.where(i > j, c0, zero))
    q = jnp.where(i > 1, p1[...], zero)
    q_i = q[:, : 2 * RANK]
    q_j = jnp.concatenate([q[:, 2 * RANK :], q[:, RANK : 2 * RANK]], axis=1)
    up = jnp.concatenate([rows[:, 2 * RANK : 3 * RANK], -c01], axis=1)
    c1 = mm(up, tn(q_i, q_j)).astype(BF16)
    up_part = jnp.concatenate(
        [rows[pl.ds(start, 64), 2 * RANK : 3 * RANK], -mm(ui_part, tn(pi, p10[...])).astype(BF16)], axis=1
    )
    c1_part = mm(up_part, tn(q_i, q_i)).astype(BF16)
    d = d - lax.dot_general(c1_part, up, NT, preferred_element_type=F32)
    new[...] = jnp.where(i == 0, lrow0[...], jnp.where(i == 1, lrow1[...], d))
    upd[:, RANK:] = jnp.where(j == 1, q_i, jnp.where((i > j) & (j > 1), c1, zero))


def shape(rows, cols, dtype):
    return jax.ShapeDtypeStruct((rows, cols), dtype)


FACTOR = [shape(64, NB, F32), shape(NB, NB, BF16), shape(NB, BLK, BF16), shape(NB, BLK, BF16)]


def shift_z(x, s):
    return lax.ppermute(x, "col", [(2 * z + c, 2 * ((z + s) % 8) + c) for z in range(8) for c in range(2)])


def swap_core(x):
    return lax.ppermute(x, "col", [(c, c ^ 1) for c in range(16)])


def spread_pair(x, row_at):
    at_x, at_y = row_at // 4, row_at % 4
    cur = x
    for k in (1, 2, 3):
        got = lax.ppermute(x, "row", [(0, 4 * k), (1, 4 * k + 1)])
        cur = jnp.where(at_x == k, got, cur)
    got = [
        lax.ppermute(cur, "row", [(4 * a + y, 4 * a + (y + s) % 4) for a in range(4) for y in (0, 1)])
        for s in (1, 2, 3)
    ]

    def pick(home):
        out = cur
        for s in (1, 2, 3):
            out = jnp.where(at_y == (home + s) % 4, got[s - 1], out)
        return out

    return pick(0), pick(1)


def spread_one(x, row_at, token0, token1):
    at_x, at_y = row_at // 4, row_at % 4
    x = after(x, *token0)
    cur = x
    for k in (1, 2, 3):
        got = lax.ppermute(x, "row", [(1, 4 * k + 1)])
        cur = jnp.where(at_x == k, got, cur)
    cur = after(cur, *token1)
    out = cur
    for s in (1, 2, 3):
        got = lax.ppermute(cur, "row", [(4 * a + 1, 4 * a + (1 + s) % 4) for a in range(4)])
        out = jnp.where(at_y == (1 + s) % 4, got, out)
    return out


def after(x, *tokens):
    return lax.optimization_barrier((x, *tokens))[0]


def scatter_rows(both, z, core, token0, token1):
    cur = both
    for gap, token in ((4, ()), (2, token0)):
        half = cur.shape[0] // 2
        got = lax.ppermute(
            after(cur[half:], *token),
            "col",
            [(2 * a + c, 2 * (a + gap) + c) for a in range(0, 8, 2 * gap) for c in (0, 1)],
        )
        cur = jnp.where((z // gap) % 2 == 1, got, cur[:half])
    first = core == 0

    def chunk(q0, q1):
        return jnp.where(first, cur[64 * q0 : 64 * q0 + 64], cur[64 * q1 : 64 * q1 + 64])

    def deal(x, step, flip):
        pairs = [(2 * a + c, 2 * (a + step) + (c ^ flip)) for a in range(0, 8, 2) for c in (0, 1)]
        return lax.ppermute(after(x, *token1), "col", pairs)

    odd = z % 2 == 1
    same = jnp.where(odd, deal(chunk(2, 3), 1, 0), chunk(0, 1))
    cross = jnp.where(odd, deal(chunk(3, 2), 1, 1), deal(chunk(1, 0), 0, 1))
    return jnp.where(first, same, cross), jnp.where(first, cross, same)


def shards(diag_tiles, left_factors, right_factors, ranks):
    row_at = lax.axis_index("row")
    col_at = lax.axis_index("col")
    z, core = col_at // 2, col_at % 2
    place = jnp.stack([z, core, row_at]).astype(jnp.int32)
    mine = diag_tiles[0, 0]
    band = lax.dynamic_slice(jnp.concatenate([mine, mine[:, :BAND]], axis=1), (0, BLK * z), (64, BAND))
    band0, band1 = spread_pair(band, row_at)

    fwd, bwd = [band0], [band0]
    for _ in range(3):
        fwd.append(shift_z(fwd[-1], 1))
        bwd.append(shift_z(bwd[-1], -1))
    fwd.append(shift_z(fwd[-1], 1))
    cross = lax.ppermute(bwd[3], "col", [(2 * a + c, 2 * ((a - 1) % 8) + 1 - c) for a in range(8) for c in (0, 1)])
    own = [band0, bwd[1], bwd[2], bwd[3], fwd[4], fwd[3], fwd[2], fwd[1]]
    pieces = own + [swap_core(jnp.concatenate(own[:4] + own[5:], axis=0)), cross]

    keep = jnp.arange(RANK)[None, :] < ranks[0, 0, 0, 0]
    zero = jnp.zeros((), BF16)
    both = jnp.concatenate(
        [jnp.where(keep, left_factors[0, 0, 0, 0], zero), jnp.where(keep, right_factors[0, 0, 0, 0], zero)], axis=1
    )
    part0, part1 = scatter_rows(both, z, core, (band0,), (fwd[1], bwd[1]))
    first = spread_one(part0, row_at, (fwd[2], bwd[2]), (fwd[3], bwd[3]))
    flip = lax.ppermute(
        after(jnp.concatenate([part0[:, RANK:], part1[:, RANK:]], axis=1), fwd[3], bwd[3]),
        ("row", "col"),
        [(r * 16 + c, c * 16 + r) for r in range(16) for c in range(16)],
    )
    raw1 = lax.all_gather(band1, "col", tiled=True)
    rows = lax.all_gather(after(jnp.concatenate([part0, part1, first], axis=1), fwd[4], cross), "col", tiled=True)
    cols = lax.all_gather(after(flip, fwd[4], cross), "row", tiled=True)

    lrow0, lb0, mh0, ml0 = pl.pallas_call(
        first_kernel,
        out_shape=FACTOR,
        in_specs=[SMEM] + [VMEM] * 10,
        out_specs=[VMEM] * 4,
        scratch_shapes=[pltpu.VMEM((NB, BAND), F32), pltpu.VMEM((NB, NB), F32), pltpu.VMEM((BLK, BLK), F32)],
        compiler_params=grant(24),
        name="factor_first",
    )(place, *pieces)
    lrow1, lb1, mh1, ml1, p10 = pl.pallas_call(
        second_kernel,
        out_shape=FACTOR + [shape(NB, RANK, BF16)],
        in_specs=[SMEM] + [VMEM] * 5,
        out_specs=[VMEM] * 5,
        scratch_shapes=[pltpu.VMEM((NB, NB), F32), pltpu.VMEM((NB, RANK), F32), pltpu.VMEM((BLK, BLK), F32)],
        compiler_params=grant(32),
        name="factor_second",
    )(place, raw1, rows, lb0, mh0, ml0)
    new, upd = pl.pallas_call(
        last_kernel,
        out_shape=[shape(64, NB, F32), shape(NB, 3 * RANK, BF16)],
        in_specs=[SMEM] + [VMEM] * 12,
        out_specs=[VMEM] * 2,
        scratch_shapes=[
            pltpu.VMEM((NB, 2 * RANK), F32),
            pltpu.VMEM((NB, 3 * RANK), F32),
            pltpu.VMEM((NB, 2 * RANK), BF16),
            pltpu.VMEM((NB, 3 * RANK), BF16),
        ],
        compiler_params=grant(40),
        name="finish",
    )(place, rows, cols, p10, mine, lrow0, lrow1, lb0, mh0, ml0, lb1, mh1, ml1)
    return new[None, None], upd[None, None, None, None]


def solution(mesh):
    in_specs = (
        P(None, "row", "col", None),
        P(None, "row", None, "col", None, None),
        P(None, "row", None, "col", None, None),
        P(None, "row", None, "col"),
    )
    out_specs = (P(None, "row", "col", None), P(None, "row", None, "col", None, None))
    return jax.shard_map(shards, mesh=mesh, in_specs=in_specs, out_specs=out_specs, check_vma=False)
```

```python
import functools

import jax
import jax.numpy as jnp
from jax import lax
from jax.experimental import pallas as pl
from jax.experimental.pallas import tpu as pltpu
from jax.sharding import PartitionSpec as P

F32 = jnp.float32
BF16 = jnp.bfloat16
NB = 1024
RANK = 256
BLK = 128
NBLK = NB // BLK
BAND = 5 * BLK
TN = (((0,), (0,)), ((), ()))
NT = (((1,), (1,)), ((), ()))
VMEM = pl.BlockSpec(memory_space=pltpu.VMEM)
SMEM = pl.BlockSpec(memory_space=pltpu.SMEM)
ANY = pl.BlockSpec(memory_space=pl.ANY)


def grant(mib):
    return pltpu.CompilerParams(vmem_limit_bytes=mib * 1024 * 1024)


def lanes_of(x, c):
    return jnp.broadcast_to(x[:, c : c + 1], (8, BLK))


def rows_of(x, r):
    return jnp.broadcast_to(x[r : r + 1, :], (8, BLK))


def factor_block(rows):
    sub = lax.broadcasted_iota(jnp.int32, (8, BLK), 0)
    lane = lax.broadcasted_iota(jnp.int32, (8, BLK), 1)
    a = list(rows)
    n = len(a)
    up, inv = [], []
    cols = [lanes_of(a[0], m) for m in range(8)]
    for g in range(n):
        c0 = 8 * g
        here = (lane >= c0) & (lane < c0 + 8)
        left = [[lanes_of(a[b], c0 + m) for m in range(8)] for b in range(g + 1, n)]
        ahead = [lanes_of(a[g + 1], c0 + 8 + m) for m in range(8)] if g + 1 < n else None
        mult, recip, piv = [], [], None
        for k in range(8):
            d = rows_of(cols[k], k)
            r = 1.0 / d
            recip.append(r)
            piv = d if piv is None else jnp.where(sub == k, d, piv)
            for m in range(k + 1, 8):
                cols[m] = cols[m] - (cols[k] * rows_of(cols[k], m)) * r
            mult.append(jnp.where(sub > k, cols[k] * r, 0.0))
        s = jnp.where(here, jnp.where(lane == c0 + sub, 1.0, 0.0), a[g])
        s2 = a[g]
        for k in range(7):
            s = s - mult[k] * rows_of(s, k)
            s2 = s2 - mult[k] * rows_of(s2, k)
        root = lax.rsqrt(piv)
        r_ = s * root
        t = r_ * root
        diag = jnp.where(lane >= c0 + sub, s2 * root, 0.0)
        up.append(jnp.where(here, diag, jnp.where(lane >= c0 + 8, r_, 0.0)))
        inv.append(jnp.where(lane < c0 + 8, r_, 0.0))
        if g + 1 == n:
            break
        mk = [[rows_of(mult[k], m) if m > k else None for m in range(8)] for k in range(8)]
        tk = [rows_of(t, k) for k in range(8)]
        for b in range(g + 1, n):
            x = left[b - g - 1]
            for k in range(8):
                for m in range(k + 1, 8):
                    x[m] = x[m] - x[k] * mk[k][m]
            if b == g + 1:
                cols = ahead
                for k in range(8):
                    xs = x[k] * recip[k]
                    for m in range(8):
                        cols[m] = cols[m] - x[k] * rows_of(xs, m)
            new = jnp.where(here, 0.0, a[b])
            for k in range(8):
                new = new - x[k] * tk[k]
            a[b] = new
    return up, inv


def split(x):
    hi = x.astype(BF16)
    return hi, (x - hi.astype(F32)).astype(BF16)


def mm(a, b):
    return jnp.dot(a, b, preferred_element_type=F32)


def mm3(a, b):
    return mm(a[0], b[0]) + (mm(a[0], b[1]) + mm(a[1], b[0]))


def unfold(work, take):
    for r in range(NBLK):
        n = min(5, NBLK - r)
        rows = slice(r * BLK, (r + 1) * BLK)
        work[rows, r * BLK : (r + n) * BLK] = take(r, slice(0, n * BLK))
        for c in range(r + 5, NBLK):
            o = (NBLK - (c - r)) * BLK
            work[rows, c * BLK : (c + 1) * BLK] = take(c, slice(o, o + BLK)).T


def cholesky_blocks(work, lb, mh, ml, inv_s):
    def body(k, _):
        off = pl.multiple_of(k * BLK, BLK)
        rows = [work[pl.ds(pl.multiple_of(off + 8 * i, 8), 8), pl.ds(off, BLK)] for i in range(16)]
        up, inv = factor_block(rows)
        for i in range(16):
            inv_s[8 * i : 8 * i + 8, :] = inv[i]
        work[pl.ds(off, BLK), pl.ds(off, BLK)] = jnp.concatenate(up, axis=0).T
        hi, lo = split(inv_s[...])
        mh[pl.ds(off, BLK), :] = hi
        ml[pl.ds(off, BLK), :] = lo
        for kk in range(NBLK - 1):

            @pl.when(k == kk)
            def _():
                o = BLK * kk
                e = o + BLK
                upper = mm3((hi, lo), split(work[o:e, e:]))
                parts = split(upper)
                for ib in range(kk + 1, NBLK):
                    i0 = BLK * ib
                    c = i0 - e
                    low = upper[:, c : c + BLK].T
                    lows = split(low)
                    lb[i0 : i0 + BLK, o:e] = lows[0]
                    work[i0 : i0 + BLK, o:e] = low
                    work[i0 : i0 + BLK, i0:] = work[i0 : i0 + BLK, i0:] - mm3(
                        lows, (parts[0][:, c:], parts[1][:, c:])
                    )

        return 0

    lax.fori_loop(0, NBLK, body, 0)


def write_rows(place, work, lrow):
    start = pl.multiple_of(64 * (2 * place[0] + place[1]), 64)
    r = lax.broadcasted_iota(jnp.int32, (64, NB), 0) + start
    c = lax.broadcasted_iota(jnp.int32, (64, NB), 1)
    lrow[...] = jnp.where(c <= r, work[pl.ds(start, 64), :], 0.0)


def first_kernel(place, *refs):
    own, other = refs[:8], refs[8:10]
    lrow, lb, mh, ml, raw, work, inv_s = refs[10:]
    z, core = place[0], place[1]
    for i in range(8):
        n = lax.rem(z + i, 8)
        raw[pl.ds(pl.multiple_of(n * BLK + core * 64, 64), 64), :] = own[i][...]
        theirs = other[1][...] if i == 4 else other[0][64 * (i - i // 5) : 64 * (i - i // 5 + 1), :]
        raw[pl.ds(pl.multiple_of(n * BLK + (1 - core) * 64, 64), 64), :] = theirs
    unfold(work, lambda r, cols: raw[r * BLK : (r + 1) * BLK, cols])
    cholesky_blocks(work, lb, mh, ml, inv_s)
    write_rows(place, work, lrow)


def solve_step(k, w, lb, mh, ml, p):
    o = BLK * k
    e = o + BLK
    x = mm3((mh[o:e, :], ml[o:e, :]), split(w[o:e, :]))
    p[o:e, :] = x.astype(BF16)
    if e < NB:
        xs = split(x)
        low = lb[e:, o:e]
        w[e:, :] = w[e:, :] - (mm(low, xs[0]) + mm(low, xs[1]))


def fetch(pairs, sems):
    copies = [pltpu.make_async_copy(src, dst, sems.at[n]) for n, (src, dst) in enumerate(pairs)]
    for one in copies:
        one.start()
    return copies


def second_kernel(
    place, tile_h, lb0_h, mh0_h, ml0_h, lrow, lb, mh, ml, p10, tile, lb0, mh0, ml0, work, w, inv_s, sems
):
    copies = fetch([(mh0_h, mh0), (ml0_h, ml0), (tile_h, tile), (lb0_h, lb0)], sems)
    for one in copies:
        one.wait()
    w[...] = tile[:, 2 * BAND + RANK :].astype(F32)
    for k in range(NBLK):
        solve_step(k, w, lb0, mh0, ml0, p10)
    solved = p10[...]
    inner = lax.dot_general(solved, solved, TN, preferred_element_type=F32).astype(BF16)
    u = tile[:, 2 * BAND : 2 * BAND + RANK]
    corr = split(mm(u, inner))

    def take(r, cols):
        rows = slice(r * BLK, (r + 1) * BLK)
        return tile[rows, cols].astype(F32) + tile[rows, cols.start + BAND : cols.stop + BAND].astype(F32)

    unfold(work, take)
    for r in range(NBLK):
        o = r * BLK
        right = u[o:, :]
        work[o : o + BLK, o:] = work[o : o + BLK, o:] - (
            lax.dot_general(corr[0][o : o + BLK], right, NT, preferred_element_type=F32)
            + lax.dot_general(corr[1][o : o + BLK], right, NT, preferred_element_type=F32)
        )
    cholesky_blocks(work, lb, mh, ml, inv_s)
    write_rows(place, work, lrow)


def last_kernel(place, own_h, other_h, cols_h, tile_h, *refs):
    (p10_h, diag_h, lrow0_h, lrow1_h, lb0_h, mh0_h, ml0_h, lb1_h, mh1_h, ml1_h, new, upd) = refs[:12]
    (rows, cols, u10, p10, diag, lrow0, lrow1, lb0, mh0, ml0, lb1, mh1, ml1, w0, w1, p0, p1, sems) = refs[12:]
    core = place[1]
    j = 2 * place[0] + core
    i = place[2]
    copies = fetch(
        [
            (own_h, rows.at[core]),
            (other_h, rows.at[1 - core]),
            (cols_h, cols),
            (tile_h.at[:, 2 * BAND : 2 * BAND + RANK], u10),
            (mh0_h, mh0),
            (ml0_h, ml0),
            (mh1_h, mh1),
            (ml1_h, ml1),
            (lb0_h, lb0),
            (lb1_h, lb1),
            (p10_h, p10),
            (diag_h, diag),
            (lrow0_h, lrow0),
            (lrow1_h, lrow1),
        ],
        sems,
    )
    for one in copies[:4]:
        one.wait()
    w0[:, :RANK] = rows[0, :, RANK:].astype(F32)
    w0[:, RANK:] = cols[:, :RANK].astype(F32)
    w1[:, :RANK] = rows[1, :, RANK:].astype(F32)
    w1[:, RANK : 2 * RANK] = u10[...].astype(F32)
    w1[:, 2 * RANK :] = cols[:, RANK:].astype(F32)
    for one in copies[4:]:
        one.wait()
    for k in range(NBLK):
        solve_step(k, w0, lb0, mh0, ml0, p0)
        solve_step(k, w1, lb1, mh1, ml1, p1)
    zero = jnp.zeros((), BF16)

    def tn(a, b):
        return lax.dot_general(a, b, TN, preferred_element_type=F32).astype(BF16)

    pi = jnp.where(i > 0, p0[:, :RANK], zero)
    pj = jnp.where(j > 0, p0[:, RANK:], zero)
    ui = rows[0, :, :RANK]
    start = pl.multiple_of(64 * j, 64)
    ui_part = rows[0, pl.ds(start, 64), :RANK]
    inner01 = tn(pi, p10[...])
    c0 = mm(ui, tn(pi, pj)).astype(BF16)
    c01 = mm(ui, inner01).astype(BF16)
    c0_part = mm(ui_part, tn(pi, pi)).astype(BF16)
    d = diag[...] - lax.dot_general(c0_part, ui, NT, preferred_element_type=F32)
    upd[:, :RANK] = jnp.where(j == 0, pi, jnp.where(i > j, c0, zero))
    q = jnp.where(i > 1, p1[...], zero)
    q_i = q[:, : 2 * RANK]
    q_j = jnp.concatenate([q[:, 2 * RANK :], q[:, RANK : 2 * RANK]], axis=1)
    up = jnp.concatenate([rows[1, :, :RANK], -c01], axis=1)
    c1 = mm(up, tn(q_i, q_j)).astype(BF16)
    up_part = jnp.concatenate([rows[1, pl.ds(start, 64), :RANK], -mm(ui_part, inner01).astype(BF16)], axis=1)
    c1_part = mm(up_part, tn(q_i, q_i)).astype(BF16)
    d = d - lax.dot_general(c1_part, up, NT, preferred_element_type=F32)
    new[...] = jnp.where(i == 0, lrow0[...], jnp.where(i == 1, lrow1[...], d))
    upd[:, RANK:] = jnp.where(j == 1, q_i, jnp.where((i > j) & (j > 1), c1, zero))


def shape(rows, cols, dtype):
    return jax.ShapeDtypeStruct((rows, cols), dtype)


FACTOR = [shape(64, NB, F32), shape(NB, NB, BF16), shape(NB, BLK, BF16), shape(NB, BLK, BF16)]


def shift_z(x, s):
    return lax.ppermute(x, "col", [(2 * z + c, 2 * ((z + s) % 8) + c) for z in range(8) for c in range(2)])


def swap_core(x):
    return lax.ppermute(x, "col", [(c, c ^ 1) for c in range(16)])


def after(x, *tokens):
    return lax.optimization_barrier((x, *tokens))[0]


def at(row, col):
    return 16 * row + col


def pick(cases, default):
    for hit, x in cases:
        default = jnp.where(hit, x, default)
    return default


def spread_x(x, row_at, rows):
    got = [lax.ppermute(x, "row", [(y, 4 * k + y) for y in rows]) for k in (1, 2, 3)]
    return pick([(row_at // 4 == k, got[k - 1]) for k in (1, 2, 3)], x)


def spread_y(x, row_at, rows):
    got = [lax.ppermute(x, "row", [(4 * a + y, 4 * a + (y + s) % 4) for a in range(4) for y in rows]) for s in (1, 2, 3)]
    return [pick([(row_at % 4 == (y + s) % 4, got[s - 1]) for s in (1, 2, 3)], x) for y in rows]


def deal_first(both, col_at, token):
    got = [lax.ppermute(both[256 * q : 256 * q + 256], ("row", "col"), [(at(1, 0), at(1, 4 * q))]) for q in (1, 2, 3)]
    cur = after(pick([(col_at // 4 == q, got[q - 1]) for q in (1, 2, 3)], both[:256]), token)
    got = [
        lax.ppermute(cur[64 * k : 64 * k + 64], ("row", "col"), [(at(1, 4 * q), at(1, 4 * q + k)) for q in range(4)])
        for k in (1, 2, 3)
    ]
    return pick([(col_at % 4 == k, got[k - 1]) for k in (1, 2, 3)], cur[:64])


def shards(diag_tiles, left_factors, right_factors, ranks):
    row_at = lax.axis_index("row")
    col_at = lax.axis_index("col")
    z, core = col_at // 2, col_at % 2
    place = jnp.stack([z, core, row_at]).astype(jnp.int32)
    mine = diag_tiles[0, 0]
    keep = jnp.arange(RANK)[None, :] < ranks[0, 0, 0, 0]
    zero = jnp.zeros((), BF16)
    both = jnp.concatenate(
        [jnp.where(keep, left_factors[0, 0, 0, 0], zero), jnp.where(keep, right_factors[0, 0, 0, 0], zero)], axis=1
    )

    far = [lax.ppermute(both, "col", [(c, 2 * a + c) for c in (0, 1)]) for a in (3, 5)]

    band = lax.dynamic_slice(jnp.concatenate([mine, mine[:, :BAND]], axis=1), (0, BLK * z), (64, BAND))
    half_way = spread_x(band, row_at, (0, 1))
    band0, band1 = spread_y(half_way, row_at, (0, 1))
    band0 = after(band0, *far)
    fwd, bwd = [band0], [band0]
    for _ in range(3):
        fwd.append(shift_z(fwd[-1], 1))
        bwd.append(shift_z(bwd[-1], -1))
    fwd.append(shift_z(fwd[-1], 1))
    cross = lax.ppermute(bwd[3], "col", [(2 * a + c, 2 * ((a - 1) % 8) + 1 - c) for a in range(8) for c in (0, 1)])
    own = [band0, bwd[1], bwd[2], bwd[3], fwd[4], fwd[3], fwd[2], fwd[1]]
    theirs = swap_core(jnp.concatenate(own[:4] + own[5:], axis=0))

    first = deal_first(both, col_at, half_way)
    first = spread_x(after(first, band0), row_at, (1,))
    (first,) = spread_y(after(first, fwd[1], bwd[1]), row_at, (1,))
    hi, lo = split(band1)
    tile1 = lax.all_gather(after(jnp.concatenate([hi, lo, first], axis=1), fwd[2], bwd[2]), "col", tiled=True)

    lrow0, lb0, mh0, ml0 = pl.pallas_call(
        first_kernel,
        out_shape=FACTOR,
        in_specs=[SMEM] + [VMEM] * 10,
        out_specs=[VMEM] * 4,
        scratch_shapes=[pltpu.VMEM((NB, BAND), F32), pltpu.VMEM((NB, NB), F32), pltpu.VMEM((BLK, BLK), F32)],
        compiler_params=grant(24),
        name="factor_first",
    )(place, *own, theirs, cross)

    tile = after(pick([(z == 3, far[0]), (z == 5, far[1])], both), fwd[4], cross, theirs)
    up = lax.ppermute(tile, "col", [(2 * a + c, 2 * a + 2 + c) for a in (0, 3, 5) for c in (0, 1)])
    down = lax.ppermute(tile, "col", [(2 * a + c, 2 * a - 2 + c + 16 * (a == 0)) for a in (0, 3) for c in (0, 1)])
    up, down, _ = lax.optimization_barrier((up, down, mh0))
    tile = pick([((z == 1) | (z == 4) | (z == 6), up), ((z == 2) | (z == 7), down)], tile)
    other = swap_core(tile)
    got = []
    for c in (0, 1):
        part = lax.dynamic_slice(tile, (64 * (z + 8 * (core ^ c)), RANK), (64, RANK))
        pairs = [(at(r, 2 * a + b), at(a + 8 * (b ^ c), r)) for r in range(16) for a in range(8) for b in (0, 1)]
        got.append(lax.ppermute(part, ("row", "col"), pairs))
    low = row_at < 8
    cols = jnp.concatenate([jnp.where(low, got[0], got[1]), jnp.where(low, got[1], got[0])], axis=1)
    cols = lax.all_gather(cols, "row", tiled=True)

    lrow1, lb1, mh1, ml1, p10 = pl.pallas_call(
        second_kernel,
        out_shape=FACTOR + [shape(NB, RANK, BF16)],
        in_specs=[SMEM] + [ANY] * 4,
        out_specs=[VMEM] * 5,
        scratch_shapes=[
            pltpu.VMEM((NB, 2 * BAND + 2 * RANK), BF16),
            pltpu.VMEM((NB, NB), BF16),
            pltpu.VMEM((NB, BLK), BF16),
            pltpu.VMEM((NB, BLK), BF16),
            pltpu.VMEM((NB, NB), F32),
            pltpu.VMEM((NB, RANK), F32),
            pltpu.VMEM((BLK, BLK), F32),
            pltpu.SemaphoreType.DMA((4,)),
        ],
        compiler_params=grant(56),
        name="factor_second",
    )(place, tile1, lb0, mh0, ml0)
    new, upd = pl.pallas_call(
        last_kernel,
        out_shape=[shape(64, NB, F32), shape(NB, 3 * RANK, BF16)],
        in_specs=[SMEM] + [ANY] * 14,
        out_specs=[VMEM] * 2,
        scratch_shapes=[
            pltpu.VMEM((2, NB, 2 * RANK), BF16),
            pltpu.VMEM((NB, 2 * RANK), BF16),
            pltpu.VMEM((NB, RANK), BF16),
            pltpu.VMEM((NB, RANK), BF16),
            pltpu.VMEM((64, NB), F32),
            pltpu.VMEM((64, NB), F32),
            pltpu.VMEM((64, NB), F32),
            pltpu.VMEM((NB, NB), BF16),
            pltpu.VMEM((NB, BLK), BF16),
            pltpu.VMEM((NB, BLK), BF16),
            pltpu.VMEM((NB, NB), BF16),
            pltpu.VMEM((NB, BLK), BF16),
            pltpu.VMEM((NB, BLK), BF16),
            pltpu.VMEM((NB, 2 * RANK), F32),
            pltpu.VMEM((NB, 3 * RANK), F32),
            pltpu.VMEM((NB, 2 * RANK), BF16),
            pltpu.VMEM((NB, 3 * RANK), BF16),
            pltpu.SemaphoreType.DMA((14,)),
        ],
        compiler_params=grant(56),
        name="finish",
    )(place, tile, other, cols, tile1, p10, mine, lrow0, lrow1, lb0, mh0, ml0, lb1, mh1, ml1)
    return new[None, None], upd[None, None, None, None]


def solution(mesh):
    in_specs = (
        P(None, "row", "col", None),
        P(None, "row", None, "col", None, None),
        P(None, "row", None, "col", None, None),
        P(None, "row", None, "col"),
    )
    out_specs = (P(None, "row", "col", None), P(None, "row", None, "col", None, None))
    return jax.shard_map(shards, mesh=mesh, in_specs=in_specs, out_specs=out_specs, check_vma=False)
```

```python
import functools

import jax
import jax.numpy as jnp
from jax import lax
from jax.experimental import pallas as pl
from jax.experimental.pallas import tpu as pltpu
from jax.sharding import PartitionSpec as P

F32 = jnp.float32
BF16 = jnp.bfloat16
NB = 1024
RANK = 256
BLK = 128
NBLK = NB // BLK
BAND = 5 * BLK
TILE1 = 2 * BAND + 2 * RANK
TN = (((0,), (0,)), ((), ()))
NT = (((1,), (1,)), ((), ()))
VMEM = pl.BlockSpec(memory_space=pltpu.VMEM)
SMEM = pl.BlockSpec(memory_space=pltpu.SMEM)
ANY = pl.BlockSpec(memory_space=pl.ANY)


def grant(mib):
    return pltpu.CompilerParams(vmem_limit_bytes=mib * 1024 * 1024)


def lanes_of(x, c):
    return jnp.broadcast_to(x[:, c : c + 1], (8, BLK))


def rows_of(x, r):
    return jnp.broadcast_to(x[r : r + 1, :], (8, BLK))


def factor_block(rows):
    sub = lax.broadcasted_iota(jnp.int32, (8, BLK), 0)
    lane = lax.broadcasted_iota(jnp.int32, (8, BLK), 1)
    a = list(rows)
    n = len(a)
    up, inv = [], []
    cols = [lanes_of(a[0], m) for m in range(8)]
    for g in range(n):
        c0 = 8 * g
        here = (lane >= c0) & (lane < c0 + 8)
        left = [[lanes_of(a[b], c0 + m) for m in range(8)] for b in range(g + 1, n)]
        ahead = [lanes_of(a[g + 1], c0 + 8 + m) for m in range(8)] if g + 1 < n else None
        mult, recip, piv = [], [], None
        for k in range(8):
            d = rows_of(cols[k], k)
            r = 1.0 / d
            recip.append(r)
            piv = d if piv is None else jnp.where(sub == k, d, piv)
            for m in range(k + 1, 8):
                cols[m] = cols[m] - (cols[k] * rows_of(cols[k], m)) * r
            mult.append(jnp.where(sub > k, cols[k] * r, 0.0))
        s = jnp.where(here, jnp.where(lane == c0 + sub, 1.0, 0.0), a[g])
        s2 = a[g]
        for k in range(7):
            s = s - mult[k] * rows_of(s, k)
            s2 = s2 - mult[k] * rows_of(s2, k)
        root = lax.rsqrt(piv)
        r_ = s * root
        t = r_ * root
        diag = jnp.where(lane >= c0 + sub, s2 * root, 0.0)
        up.append(jnp.where(here, diag, jnp.where(lane >= c0 + 8, r_, 0.0)))
        inv.append(jnp.where(lane < c0 + 8, r_, 0.0))
        if g + 1 == n:
            break
        mk = [[rows_of(mult[k], m) if m > k else None for m in range(8)] for k in range(8)]
        tk = [rows_of(t, k) for k in range(8)]
        for b in range(g + 1, n):
            x = left[b - g - 1]
            for k in range(8):
                for m in range(k + 1, 8):
                    x[m] = x[m] - x[k] * mk[k][m]
            if b == g + 1:
                cols = ahead
                for k in range(8):
                    xs = x[k] * recip[k]
                    for m in range(8):
                        cols[m] = cols[m] - x[k] * rows_of(xs, m)
            new = jnp.where(here, 0.0, a[b])
            for k in range(8):
                new = new - x[k] * tk[k]
            a[b] = new
    return up, inv


def split(x):
    hi = x.astype(BF16)
    return hi, (x - hi.astype(F32)).astype(BF16)


def mm(a, b):
    return jnp.dot(a, b, preferred_element_type=F32)


def mm3(a, b):
    return mm(a[0], b[0]) + (mm(a[0], b[1]) + mm(a[1], b[0]))


def unfold(work, take):
    for r in range(NBLK):
        n = min(5, NBLK - r)
        rows = slice(r * BLK, (r + 1) * BLK)
        work[rows, r * BLK : (r + n) * BLK] = take(r, slice(0, n * BLK))
        for c in range(r + 5, NBLK):
            o = (NBLK - (c - r)) * BLK
            work[rows, c * BLK : (c + 1) * BLK] = take(c, slice(o, o + BLK)).T


def cholesky_blocks(work, lb, mh, ml, inv_s):
    def body(k, _):
        off = pl.multiple_of(k * BLK, BLK)
        rows = [work[pl.ds(pl.multiple_of(off + 8 * i, 8), 8), pl.ds(off, BLK)] for i in range(16)]
        up, inv = factor_block(rows)
        for i in range(16):
            inv_s[8 * i : 8 * i + 8, :] = inv[i]
        work[pl.ds(off, BLK), pl.ds(off, BLK)] = jnp.concatenate(up, axis=0).T
        hi, lo = split(inv_s[...])
        mh[pl.ds(off, BLK), :] = hi
        ml[pl.ds(off, BLK), :] = lo
        for kk in range(NBLK - 1):

            @pl.when(k == kk)
            def _():
                o = BLK * kk
                e = o + BLK
                upper = mm3((hi, lo), split(work[o:e, e:]))
                parts = split(upper)
                for ib in range(kk + 1, NBLK):
                    i0 = BLK * ib
                    c = i0 - e
                    low = upper[:, c : c + BLK].T
                    lows = split(low)
                    lb[i0 : i0 + BLK, o:e] = lows[0]
                    work[i0 : i0 + BLK, o:e] = low
                    work[i0 : i0 + BLK, i0:] = work[i0 : i0 + BLK, i0:] - mm3(
                        lows, (parts[0][:, c:], parts[1][:, c:])
                    )

        return 0

    lax.fori_loop(0, NBLK, body, 0)


def write_rows(place, work, lrow):
    start = pl.multiple_of(64 * (2 * place[0] + place[1]), 64)
    r = lax.broadcasted_iota(jnp.int32, (64, NB), 0) + start
    c = lax.broadcasted_iota(jnp.int32, (64, NB), 1)
    lrow[...] = jnp.where(c <= r, work[pl.ds(start, 64), :], 0.0)


def first_kernel(place, *refs):
    shards_in = refs[:16]
    lrow, lb, mh, ml, raw, work, inv_s = refs[16:]
    z, core = place[0], place[1]
    for i in range(16):
        n = lax.rem(z + i % 8, 8)
        half = core if i < 8 else 1 - core
        raw[pl.ds(pl.multiple_of(n * BLK + half * 64, 64), 64), :] = shards_in[i][...]
    unfold(work, lambda r, cols: raw[r * BLK : (r + 1) * BLK, cols])
    cholesky_blocks(work, lb, mh, ml, inv_s)
    write_rows(place, work, lrow)


def solve_step(k, w, lb, mh, ml, p):
    o = BLK * k
    e = o + BLK
    x = mm3((mh[o:e, :], ml[o:e, :]), split(w[o:e, :]))
    p[o:e, :] = x.astype(BF16)
    if e < NB:
        xs = split(x)
        low = lb[e:, o:e]
        w[e:, :] = w[e:, :] - (mm(low, xs[0]) + mm(low, xs[1]))


def fetch(pairs, sems):
    copies = [pltpu.make_async_copy(src, dst, sems.at[n]) for n, (src, dst) in enumerate(pairs)]
    for one in copies:
        one.start()
    return copies


def second_kernel(
    place, tile_h, lb0_h, mh0_h, ml0_h, lrow, lb, mh, ml, p10, tile, lb0, mh0, ml0, work, w, inv_s, sems
):
    copies = fetch([(mh0_h, mh0), (ml0_h, ml0), (tile_h.at[:, :TILE1], tile), (lb0_h, lb0)], sems)
    for one in copies:
        one.wait()
    w[...] = tile[:, 2 * BAND + RANK :].astype(F32)
    for k in range(NBLK):
        solve_step(k, w, lb0, mh0, ml0, p10)
    solved = p10[...]
    inner = lax.dot_general(solved, solved, TN, preferred_element_type=F32).astype(BF16)
    u = tile[:, 2 * BAND : 2 * BAND + RANK]
    corr = split(mm(u, inner))

    def take(r, cols):
        rows = slice(r * BLK, (r + 1) * BLK)
        return tile[rows, cols].astype(F32) + tile[rows, cols.start + BAND : cols.stop + BAND].astype(F32)

    unfold(work, take)
    for r in range(NBLK):
        o = r * BLK
        right = u[o:, :]
        work[o : o + BLK, o:] = work[o : o + BLK, o:] - (
            lax.dot_general(corr[0][o : o + BLK], right, NT, preferred_element_type=F32)
            + lax.dot_general(corr[1][o : o + BLK], right, NT, preferred_element_type=F32)
        )
    cholesky_blocks(work, lb, mh, ml, inv_s)
    write_rows(place, work, lrow)


def tn(a, b):
    return lax.dot_general(a, b, TN, preferred_element_type=F32).astype(BF16)


def row_kernel(place, tile_h, *refs):
    (p10_h, diag_h, lrow0_h, lrow1_h, lb0_h, mh0_h, ml0_h, lb1_h, mh1_h, ml1_h, new, pi, qi, up) = refs[:14]
    (rows, u10, p10, diag, lrow0, lrow1, lb0, mh0, ml0, lb1, mh1, ml1, w0, w1, sems) = refs[14:]
    j = 2 * place[0] + place[1]
    i = place[2]
    copies = fetch(
        [
            (tile_h.at[:, TILE1:], rows),
            (tile_h.at[:, 2 * BAND : 2 * BAND + RANK], u10),
            (mh0_h, mh0),
            (ml0_h, ml0),
            (mh1_h, mh1),
            (ml1_h, ml1),
            (lb0_h, lb0),
            (lb1_h, lb1),
            (p10_h, p10),
            (diag_h, diag),
            (lrow0_h, lrow0),
            (lrow1_h, lrow1),
        ],
        sems,
    )
    for one in copies[:2]:
        one.wait()
    w0[...] = rows[:, RANK : 2 * RANK].astype(F32)
    w1[:, :RANK] = rows[:, 3 * RANK :].astype(F32)
    w1[:, RANK:] = u10[...].astype(F32)
    for one in copies[2:]:
        one.wait()
    for k in range(NBLK):
        solve_step(k, w0, lb0, mh0, ml0, pi)
        solve_step(k, w1, lb1, mh1, ml1, qi)
    zero = jnp.zeros((), BF16)
    pi[...] = jnp.where(i > 0, pi[...], zero)
    qi[...] = jnp.where(i > 1, qi[...], zero)
    ui = rows[:, :RANK]
    start = pl.multiple_of(64 * j, 64)
    ui_part = rows[pl.ds(start, 64), :RANK]
    inner01 = tn(pi[...], p10[...])
    up[:, :RANK] = rows[:, 2 * RANK : 3 * RANK]
    up[:, RANK:] = -mm(ui, inner01).astype(BF16)
    c0_part = mm(ui_part, tn(pi[...], pi[...])).astype(BF16)
    d = diag[...] - lax.dot_general(c0_part, ui, NT, preferred_element_type=F32)
    c1_part = mm(up[pl.ds(start, 64), :], tn(qi[...], qi[...])).astype(BF16)
    d = d - lax.dot_general(c1_part, up[...], NT, preferred_element_type=F32)
    new[...] = jnp.where(i == 0, lrow0[...], jnp.where(i == 1, lrow1[...], d))


def col_kernel(place, cols_h, tile_h, pi_h, qi_h, up_h, lb0_h, mh0_h, ml0_h, lb1_h, mh1_h, ml1_h, upd, *refs):
    (cols, ui, pi, qi, up, lb0, mh0, ml0, lb1, mh1, ml1, w0, w1, pj, qj, sems) = refs
    j = 2 * place[0] + place[1]
    i = place[2]
    copies = fetch(
        [
            (cols_h, cols),
            (mh0_h, mh0),
            (ml0_h, ml0),
            (mh1_h, mh1),
            (ml1_h, ml1),
            (lb0_h, lb0),
            (lb1_h, lb1),
            (pi_h, pi),
            (tile_h.at[:, TILE1 : TILE1 + RANK], ui),
            (qi_h, qi),
            (up_h, up),
        ],
        sems,
    )
    copies[0].wait()
    w0[...] = cols[:, :RANK].astype(F32)
    w1[...] = cols[:, RANK:].astype(F32)
    for one in copies[1:]:
        one.wait()
    for k in range(NBLK):
        solve_step(k, w0, lb0, mh0, ml0, pj)
        solve_step(k, w1, lb1, mh1, ml1, qj)
    zero = jnp.zeros((), BF16)
    c0 = mm(ui[...], tn(pi[...], pj[...])).astype(BF16)
    upd[:, :RANK] = jnp.where(j == 0, pi[...], jnp.where((i > j) & (j > 0), c0, zero))
    inner = jnp.concatenate([tn(qi[...], qj[...]), tn(qi[...], qi[:, RANK:])], axis=1)
    c1 = mm(up[...], inner).astype(BF16)
    upd[:, RANK:] = jnp.where(j == 1, qi[...], jnp.where((i > j) & (j > 1), c1, zero))


def shape(rows, cols, dtype):
    return jax.ShapeDtypeStruct((rows, cols), dtype)


FACTOR = [shape(64, NB, F32), shape(NB, NB, BF16), shape(NB, BLK, BF16), shape(NB, BLK, BF16)]


def shift_z(x, s):
    return lax.ppermute(x, "col", [(2 * z + c, 2 * ((z + s) % 8) + c) for z in range(8) for c in range(2)])


def swap_core(x):
    return lax.ppermute(x, "col", [(c, c ^ 1) for c in range(16)])


def after(x, *tokens):
    return lax.optimization_barrier((x, *tokens))[0]


def at(row, col):
    return 16 * row + col


def pick(cases, default):
    for hit, x in cases:
        default = jnp.where(hit, x, default)
    return default


def spread_x(x, row_at, rows):
    got = [lax.ppermute(x, "row", [(y, 4 * k + y) for y in rows]) for k in (1, 2, 3)]
    return pick([(row_at // 4 == k, got[k - 1]) for k in (1, 2, 3)], x)


def spread_y(x, row_at, rows):
    got = [lax.ppermute(x, "row", [(4 * a + y, 4 * a + (y + s) % 4) for a in range(4) for y in rows]) for s in (1, 2, 3)]
    return [pick([(row_at % 4 == (y + s) % 4, got[s - 1]) for s in (1, 2, 3)], x) for y in rows]


def halve(x, z, gap):
    half = x.shape[0] // 2
    pairs = [(2 * a + c, 2 * (a + gap) + c) for a in range(0, 8, 2 * gap) for c in (0, 1)]
    got = lax.ppermute(x[half:], "col", pairs)
    return jnp.where((z // gap) % 2 == 1, got, x[:half])


def deal(cur, z, core, tokens):
    first = core == 0

    def chunk(q0, q1):
        return jnp.where(first, cur[64 * q0 : 64 * q0 + 64], cur[64 * q1 : 64 * q1 + 64])

    def send(x, step, flip):
        pairs = [(2 * a + c, 2 * (a + step) + (c ^ flip)) for a in range(0, 8, 2) for c in (0, 1)]
        return lax.ppermute(after(x, *tokens), "col", pairs)

    odd = z % 2 == 1
    same = jnp.where(odd, send(chunk(2, 3), 1, 0), chunk(0, 1))
    cross = jnp.where(odd, send(chunk(3, 2), 1, 1), send(chunk(1, 0), 0, 1))
    return jnp.where(first, same, cross), jnp.where(first, cross, same)


def shards(diag_tiles, left_factors, right_factors, ranks):
    row_at = lax.axis_index("row")
    col_at = lax.axis_index("col")
    z, core = col_at // 2, col_at % 2
    place = jnp.stack([z, core, row_at]).astype(jnp.int32)
    mine = diag_tiles[0, 0]
    keep = jnp.arange(RANK)[None, :] < ranks[0, 0, 0, 0]
    zero = jnp.zeros((), BF16)
    both = jnp.concatenate(
        [jnp.where(keep, left_factors[0, 0, 0, 0], zero), jnp.where(keep, right_factors[0, 0, 0, 0], zero)], axis=1
    )

    half = halve(both, z, 4)

    band = lax.dynamic_slice(jnp.concatenate([mine, mine[:, :BAND]], axis=1), (0, BLK * z), (64, BAND))
    band0, band1 = spread_y(spread_x(band, row_at, (0, 1)), row_at, (0, 1))
    band0, half = lax.optimization_barrier((band0, half))
    fwd, bwd = [band0], [band0]
    fwd_other, bwd_other = [swap_core(band0)], []
    for _ in range(3):
        fwd.append(shift_z(fwd[-1], 1))
        bwd.append(shift_z(bwd[-1], -1))
        ready = (fwd_other[-1], *bwd_other[-1:])
        fwd[-1], bwd[-1], *_ = lax.optimization_barrier((fwd[-1], bwd[-1], *ready))
        fwd_other.append(swap_core(fwd[-1]))
        bwd_other.append(swap_core(bwd[-1]))
    fwd.append(shift_z(fwd[-1], 1))
    cross = lax.ppermute(bwd[3], "col", [(2 * a + c, 2 * ((a - 1) % 8) + 1 - c) for a in range(8) for c in (0, 1)])
    own = [band0, bwd[1], bwd[2], bwd[3], fwd[4], fwd[3], fwd[2], fwd[1]]
    theirs = [fwd_other[0], *bwd_other, cross, *fwd_other[:0:-1]]

    part0, part1 = deal(halve(half, z, 2), z, core, (fwd[1], bwd[1]))
    first = spread_x(after(part0, fwd[2], bwd[2]), row_at, (1,))
    (first,) = spread_y(after(first, fwd[3], bwd[3]), row_at, (1,))
    hi, lo = split(band1)
    tile = lax.all_gather(
        after(jnp.concatenate([hi, lo, first, part0, part1], axis=1), fwd[4], cross), "col", tiled=True
    )

    lrow0, lb0, mh0, ml0 = pl.pallas_call(
        first_kernel,
        out_shape=FACTOR,
        in_specs=[SMEM] + [VMEM] * 16,
        out_specs=[VMEM] * 4,
        scratch_shapes=[pltpu.VMEM((NB, BAND), F32), pltpu.VMEM((NB, NB), F32), pltpu.VMEM((BLK, BLK), F32)],
        compiler_params=grant(24),
        name="factor_first",
    )(place, *own, *theirs)

    flip = lax.ppermute(
        after(jnp.concatenate([part0[:, RANK:], part1[:, RANK:]], axis=1), fwd[4], cross),
        ("row", "col"),
        [(at(r, c), at(c, r)) for r in range(16) for c in range(16)],
    )
    cols = lax.all_gather(after(flip, mh0), "row", tiled=True)

    lrow1, lb1, mh1, ml1, p10 = pl.pallas_call(
        second_kernel,
        out_shape=FACTOR + [shape(NB, RANK, BF16)],
        in_specs=[SMEM] + [ANY] * 4,
        out_specs=[VMEM] * 5,
        scratch_shapes=[
            pltpu.VMEM((NB, TILE1), BF16),
            pltpu.VMEM((NB, NB), BF16),
            pltpu.VMEM((NB, BLK), BF16),
            pltpu.VMEM((NB, BLK), BF16),
            pltpu.VMEM((NB, NB), F32),
            pltpu.VMEM((NB, RANK), F32),
            pltpu.VMEM((BLK, BLK), F32),
            pltpu.SemaphoreType.DMA((4,)),
        ],
        compiler_params=grant(56),
        name="factor_second",
    )(place, tile, lb0, mh0, ml0)
    new, pi, qi, up = pl.pallas_call(
        row_kernel,
        out_shape=[shape(64, NB, F32), shape(NB, RANK, BF16), shape(NB, 2 * RANK, BF16), shape(NB, 2 * RANK, BF16)],
        in_specs=[SMEM] + [ANY] * 11,
        out_specs=[VMEM] * 4,
        scratch_shapes=[
            pltpu.VMEM((NB, 4 * RANK), BF16),
            pltpu.VMEM((NB, RANK), BF16),
            pltpu.VMEM((NB, RANK), BF16),
            pltpu.VMEM((64, NB), F32),
            pltpu.VMEM((64, NB), F32),
            pltpu.VMEM((64, NB), F32),
            pltpu.VMEM((NB, NB), BF16),
            pltpu.VMEM((NB, BLK), BF16),
            pltpu.VMEM((NB, BLK), BF16),
            pltpu.VMEM((NB, NB), BF16),
            pltpu.VMEM((NB, BLK), BF16),
            pltpu.VMEM((NB, BLK), BF16),
            pltpu.VMEM((NB, RANK), F32),
            pltpu.VMEM((NB, 2 * RANK), F32),
            pltpu.SemaphoreType.DMA((12,)),
        ],
        compiler_params=grant(56),
        name="row_part",
    )(place, tile, p10, mine, lrow0, lrow1, lb0, mh0, ml0, lb1, mh1, ml1)
    upd = pl.pallas_call(
        col_kernel,
        out_shape=shape(NB, 3 * RANK, BF16),
        in_specs=[SMEM] + [ANY] * 11,
        out_specs=VMEM,
        scratch_shapes=[
            pltpu.VMEM((NB, 2 * RANK), BF16),
            pltpu.VMEM((NB, RANK), BF16),
            pltpu.VMEM((NB, RANK), BF16),
            pltpu.VMEM((NB, 2 * RANK), BF16),
            pltpu.VMEM((NB, 2 * RANK), BF16),
            pltpu.VMEM((NB, NB), BF16),
            pltpu.VMEM((NB, BLK), BF16),
            pltpu.VMEM((NB, BLK), BF16),
            pltpu.VMEM((NB, NB), BF16),
            pltpu.VMEM((NB, BLK), BF16),
            pltpu.VMEM((NB, BLK), BF16),
            pltpu.VMEM((NB, RANK), F32),
            pltpu.VMEM((NB, RANK), F32),
            pltpu.VMEM((NB, RANK), BF16),
            pltpu.VMEM((NB, RANK), BF16),
            pltpu.SemaphoreType.DMA((11,)),
        ],
        compiler_params=grant(56),
        name="column_part",
    )(place, cols, tile, pi, qi, up, lb0, mh0, ml0, lb1, mh1, ml1)
    return new[None, None], upd[None, None, None, None]


def solution(mesh):
    in_specs = (
        P(None, "row", "col", None),
        P(None, "row", None, "col", None, None),
        P(None, "row", None, "col", None, None),
        P(None, "row", None, "col"),
    )
    out_specs = (P(None, "row", "col", None), P(None, "row", None, "col", None, None))
    return jax.shard_map(shards, mesh=mesh, in_specs=in_specs, out_specs=out_specs, check_vma=False)
```

```python
import functools

import jax
import jax.numpy as jnp
from jax import lax
from jax.experimental import pallas as pl
from jax.experimental.pallas import tpu as pltpu
from jax.sharding import PartitionSpec as P

F32 = jnp.float32
BF16 = jnp.bfloat16
NB = 1024
RANK = 256
BLK = 128
NBLK = NB // BLK
BAND = 5 * BLK
SPAN = 4
TILE1 = 2 * BAND + 2 * RANK
TN = (((0,), (0,)), ((), ()))
NT = (((1,), (1,)), ((), ()))
VMEM = pl.BlockSpec(memory_space=pltpu.VMEM)
SMEM = pl.BlockSpec(memory_space=pltpu.SMEM)
ANY = pl.BlockSpec(memory_space=pl.ANY)


def grant(mib):
    return pltpu.CompilerParams(vmem_limit_bytes=mib * 1024 * 1024)


def lanes_of(x, c):
    return jnp.broadcast_to(x[:, c : c + 1], (8, BLK))


def rows_of(x, r):
    return jnp.broadcast_to(x[r : r + 1, :], (8, BLK))


def factor_block(rows):
    sub = lax.broadcasted_iota(jnp.int32, (8, BLK), 0)
    lane = lax.broadcasted_iota(jnp.int32, (8, BLK), 1)
    a = list(rows)
    n = len(a)
    up, inv, wide = [], [], []
    cols = [lanes_of(a[0], m) for m in range(8)]
    for g in range(n):
        c0 = 8 * g
        near = min(n, g // SPAN * SPAN + 2 * SPAN)
        here = (lane >= c0) & (lane < c0 + 8)
        left = [[lanes_of(a[b], c0 + m) for m in range(8)] for b in range(g + 1, near)]
        ahead = [lanes_of(a[g + 1], c0 + 8 + m) for m in range(8)] if g + 1 < n else None
        mult, recip, piv = [], [], None
        for k in range(8):
            d = rows_of(cols[k], k)
            r = 1.0 / d
            recip.append(r)
            piv = d if piv is None else jnp.where(sub == k, d, piv)
            for m in range(k + 1, 8):
                cols[m] = cols[m] - (cols[k] * rows_of(cols[k], m)) * r
            mult.append(jnp.where(sub > k, cols[k] * r, 0.0))
        s = jnp.where(here, jnp.where(lane == c0 + sub, 1.0, 0.0), a[g])
        s2 = a[g]
        for k in range(7):
            s = s - mult[k] * rows_of(s, k)
            s2 = s2 - mult[k] * rows_of(s2, k)
        root = lax.rsqrt(piv)
        r_ = s * root
        t = r_ * root
        diag = jnp.where(lane >= c0 + sub, s2 * root, 0.0)
        up.append(jnp.where(here, diag, jnp.where(lane >= c0 + 8, r_, 0.0)))
        inv.append(jnp.where(lane < c0 + 8, r_, 0.0))
        if g + 1 == n:
            break
        mk = [[rows_of(mult[k], m) if m > k else None for m in range(8)] for k in range(8)]
        tk = [rows_of(t, k) for k in range(8)]
        for b in range(g + 1, near):
            x = left[b - g - 1]
            for k in range(8):
                for m in range(k + 1, 8):
                    x[m] = x[m] - x[k] * mk[k][m]
            if b == g + 1:
                cols = ahead
                for k in range(8):
                    xs = x[k] * recip[k]
                    for m in range(8):
                        cols[m] = cols[m] - x[k] * rows_of(xs, m)
            new = jnp.where(here, 0.0, a[b])
            for k in range(8):
                new = new - x[k] * tk[k]
            a[b] = new
        wide.append(jnp.where((lane >= c0 + 8) & (lane < 8 * (g // SPAN * SPAN + SPAN)), 0.0, r_))
        if (g + 1) % SPAN == 0 and near < n:
            hi, lo = split(jnp.concatenate(wide, axis=0))
            wide = []
            both = tn32(hi, hi) + (tn32(hi, lo) + tn32(lo, hi))
            done = (lane >= c0 + 8 - 8 * SPAN) & (lane < c0 + 8)
            for b in range(near, n):
                a[b] = jnp.where(done, 0.0, a[b]) - both[8 * b : 8 * b + 8]
    return up, inv


def split(x):
    hi = x.astype(BF16)
    return hi, (x - hi.astype(F32)).astype(BF16)


def tn32(a, b):
    return lax.dot_general(a, b, TN, preferred_element_type=F32)


def tn(a, b):
    return tn32(a, b).astype(BF16)


def mm(a, b):
    return jnp.dot(a, b, preferred_element_type=F32)


def mm3(a, b):
    return mm(a[0], b[0]) + (mm(a[0], b[1]) + mm(a[1], b[0]))


def unfold(work, take):
    for r in range(NBLK):
        n = min(5, NBLK - r)
        rows = slice(r * BLK, (r + 1) * BLK)
        work[rows, r * BLK : (r + n) * BLK] = take(r, slice(0, n * BLK))
        for c in range(r + 5, NBLK):
            o = (NBLK - (c - r)) * BLK
            work[rows, c * BLK : (c + 1) * BLK] = take(c, slice(o, o + BLK)).T


def cholesky_blocks(work, lb, mh, ml, inv_s):
    def body(k, _):
        off = pl.multiple_of(k * BLK, BLK)
        rows = [work[pl.ds(pl.multiple_of(off + 8 * i, 8), 8), pl.ds(off, BLK)] for i in range(16)]
        up, inv = factor_block(rows)
        for i in range(16):
            inv_s[8 * i : 8 * i + 8, :] = inv[i]
        work[pl.ds(off, BLK), pl.ds(off, BLK)] = jnp.concatenate(up, axis=0).T
        hi, lo = split(inv_s[...])
        mh[pl.ds(off, BLK), :] = hi
        ml[pl.ds(off, BLK), :] = lo
        for kk in range(NBLK - 1):

            @pl.when(k == kk)
            def _():
                o = BLK * kk
                e = o + BLK
                upper = mm3((hi, lo), split(work[o:e, e:]))
                parts = split(upper)
                for ib in range(kk + 1, NBLK):
                    i0 = BLK * ib
                    c = i0 - e
                    low = upper[:, c : c + BLK].T
                    lows = split(low)
                    lb[i0 : i0 + BLK, o:e] = lows[0]
                    work[i0 : i0 + BLK, o:e] = low
                    work[i0 : i0 + BLK, i0:] = work[i0 : i0 + BLK, i0:] - mm3(
                        lows, (parts[0][:, c:], parts[1][:, c:])
                    )

        return 0

    lax.fori_loop(0, NBLK, body, 0)


def write_rows(place, work, lrow):
    start = pl.multiple_of(64 * (2 * place[0] + place[1]), 64)
    r = lax.broadcasted_iota(jnp.int32, (64, NB), 0) + start
    c = lax.broadcasted_iota(jnp.int32, (64, NB), 1)
    lrow[...] = jnp.where(c <= r, work[pl.ds(start, 64), :], 0.0)


def first_kernel(place, *refs):
    pair, ahead, behind = refs[:2], refs[2:6], refs[6:9]
    lrow, lb, mh, ml, raw, work, inv_s = refs[9:]
    z, core = place[0], place[1]
    turn = 2 * core - 1

    def put(chip, half, x):
        raw[pl.ds(pl.multiple_of(lax.rem(chip + 8, 8) * BLK + half * 64, 64), 64), :] = x

    put(z, core, pair[0][...])
    put(z, 1 - core, pair[1][...])
    for t in range(4):
        put(z + turn * (t + 1), core, ahead[t][:64])
        put(z + turn * (t + 1), 1 - core, ahead[t][64:])
    for t in range(3):
        put(z - turn * (t + 1), 1 - core, behind[t][:64])
        put(z - turn * (t + 1), core, behind[t][64:])
    unfold(work, lambda r, cols: raw[r * BLK : (r + 1) * BLK, cols])
    cholesky_blocks(work, lb, mh, ml, inv_s)
    write_rows(place, work, lrow)


def solve_step(k, w, lb, mh, ml, p):
    o = BLK * k
    e = o + BLK
    x = mm3((mh[o:e, :], ml[o:e, :]), split(w[o:e, :]))
    p[o:e, :] = x.astype(BF16)
    if e < NB:
        xs = split(x)
        low = lb[e:, o:e]
        w[e:, :] = w[e:, :] - (mm(low, xs[0]) + mm(low, xs[1]))


def fetch(pairs, sems):
    copies = [pltpu.make_async_copy(src, dst, sems.at[n]) for n, (src, dst) in enumerate(pairs)]
    for one in copies:
        one.start()
    return copies


def second_kernel(
    place, tile_h, lb0_h, mh0_h, ml0_h, lrow, lb, mh, ml, p10, tile, lb0, mh0, ml0, work, w, inv_s, sems
):
    copies = fetch([(tile_h.at[:, : TILE1 + 2 * RANK], tile), (mh0_h, mh0), (ml0_h, ml0), (lb0_h, lb0)], sems)
    for one in copies:
        one.wait()
    w[:, :RANK] = tile[:, 2 * BAND + RANK : TILE1].astype(F32)
    w[:, RANK:] = tile[:, TILE1 + RANK : TILE1 + 2 * RANK].astype(F32)
    for k in range(NBLK):
        solve_step(k, w, lb0, mh0, ml0, p10)
    solved = p10[:, :RANK]
    inner = lax.dot_general(solved, solved, TN, preferred_element_type=F32).astype(BF16)
    u = tile[:, 2 * BAND : 2 * BAND + RANK]
    corr = split(mm(u, inner))

    def take(r, cols):
        rows = slice(r * BLK, (r + 1) * BLK)
        return tile[rows, cols].astype(F32) + tile[rows, cols.start + BAND : cols.stop + BAND].astype(F32)

    unfold(work, take)
    for r in range(NBLK):
        o = r * BLK
        right = u[o:, :]
        work[o : o + BLK, o:] = work[o : o + BLK, o:] - (
            lax.dot_general(corr[0][o : o + BLK], right, NT, preferred_element_type=F32)
            + lax.dot_general(corr[1][o : o + BLK], right, NT, preferred_element_type=F32)
        )
    cholesky_blocks(work, lb, mh, ml, inv_s)
    write_rows(place, work, lrow)


def last_kernel(place, *refs):
    parts, (tile_h, p10i_h, diag_h, lrow0_h, lrow1_h) = refs[:4], refs[4:9]
    lb0_h, mh0_h, ml0_h, lb1_h, mh1_h, ml1_h, new, upd = refs[9:17]
    (cols, rows, u10, p10i, diag, lrow0, lrow1, lb0, mh0, ml0, lb1, mh1, ml1, w0, w1, pj, p1, sems) = refs[17:]
    j = 2 * place[0] + place[1]
    i = place[2]
    x, y = i // 4, lax.rem(i, 4)
    pairs = [(tile_h.at[:, TILE1:], rows), (tile_h.at[:, 2 * BAND : 2 * BAND + RANK], u10)]
    for b in range(4):
        for a in range(4):
            k = 4 * lax.rem(x + 4 - a, 4) + lax.rem(y + 4 - b, 4)
            pairs.append((parts[b].at[pl.ds(64 * a, 64)], cols.at[pl.ds(pl.multiple_of(64 * k, 64), 64)]))
    head = len(pairs)
    pairs += [(mh0_h, mh0), (ml0_h, ml0), (mh1_h, mh1), (ml1_h, ml1), (lb0_h, lb0), (lb1_h, lb1)]
    body = len(pairs)
    pairs += [(p10i_h, p10i), (diag_h, diag), (lrow0_h, lrow0), (lrow1_h, lrow1)]
    copies = fetch(pairs, sems)
    for one in copies[:head]:
        one.wait()
    w0[...] = cols[:, :RANK].astype(F32)
    w1[:, :RANK] = rows[:, 3 * RANK :].astype(F32)
    w1[:, RANK : 2 * RANK] = u10[...].astype(F32)
    w1[:, 2 * RANK :] = cols[:, RANK:].astype(F32)
    for one in copies[head:body]:
        one.wait()
    for k in range(NBLK):
        solve_step(k, w0, lb0, mh0, ml0, pj)
        solve_step(k, w1, lb1, mh1, ml1, p1)
    for one in copies[body:]:
        one.wait()
    zero = jnp.zeros((), BF16)
    pi = jnp.where(i > 0, p10i[:, RANK:], zero)
    ui = rows[:, :RANK]
    start = pl.multiple_of(64 * j, 64)
    ui_part = rows[pl.ds(start, 64), :RANK]
    inner01 = tn(pi, p10i[:, :RANK])
    c0 = mm(ui, tn(pi, pj[...])).astype(BF16)
    c01 = mm(ui, inner01).astype(BF16)
    c0_part = mm(ui_part, tn(pi, pi)).astype(BF16)
    d = diag[...] - lax.dot_general(c0_part, ui, NT, preferred_element_type=F32)
    upd[:, :RANK] = jnp.where(j == 0, pi, jnp.where((i > j) & (j > 0), c0, zero))
    q = jnp.where(i > 1, p1[...], zero)
    q_i = q[:, : 2 * RANK]
    square = tn(q_i, q_i)
    inner = jnp.concatenate([tn(q_i, q[:, 2 * RANK :]), square[:, RANK:]], axis=1)
    up = jnp.concatenate([rows[:, 2 * RANK : 3 * RANK], -c01], axis=1)
    c1 = mm(up, inner).astype(BF16)
    up_part = jnp.concatenate(
        [rows[pl.ds(start, 64), 2 * RANK : 3 * RANK], -mm(ui_part, inner01).astype(BF16)], axis=1
    )
    c1_part = mm(up_part, square).astype(BF16)
    d = d - lax.dot_general(c1_part, up, NT, preferred_element_type=F32)
    new[...] = jnp.where(i == 0, lrow0[...], jnp.where(i == 1, lrow1[...], d))
    upd[:, RANK:] = jnp.where(j == 1, q_i, jnp.where((i > j) & (j > 1), c1, zero))


def shape(rows, cols, dtype):
    return jax.ShapeDtypeStruct((rows, cols), dtype)


FACTOR = [shape(64, NB, F32), shape(NB, NB, BF16), shape(NB, BLK, BF16), shape(NB, BLK, BF16)]


def swap_core(x):
    return lax.ppermute(x, "col", [(c, c ^ 1) for c in range(16)])


def after(x, *tokens):
    return lax.optimization_barrier((x, *tokens))[0]


def at(row, col):
    return 16 * row + col


def pick(cases, default):
    for hit, x in cases:
        default = jnp.where(hit, x, default)
    return default


def spread_x(x, row_at, rows):
    got = [lax.ppermute(x, "row", [(y, 4 * k + y) for y in rows]) for k in (1, 2, 3)]
    return pick([(row_at // 4 == k, got[k - 1]) for k in (1, 2, 3)], x)


def spread_y(x, row_at, rows):
    got = [lax.ppermute(x, "row", [(4 * a + y, 4 * a + (y + s) % 4) for a in range(4) for y in rows]) for s in (1, 2, 3)]
    return [pick([(row_at % 4 == (y + s) % 4, got[s - 1]) for s in (1, 2, 3)], x) for y in rows]


def halve(x, z, gap):
    half = x.shape[0] // 2
    pairs = [(2 * a + c, 2 * (a + gap) + c) for a in range(0, 8, 2 * gap) for c in (0, 1)]
    got = lax.ppermute(x[half:], "col", pairs)
    return jnp.where((z // gap) % 2 == 1, got, x[:half])


def deal(cur, z, core, tokens):
    first = core == 0

    def chunk(q0, q1):
        return jnp.where(first, cur[64 * q0 : 64 * q0 + 64], cur[64 * q1 : 64 * q1 + 64])

    def send(x, step, flip):
        pairs = [(2 * a + c, 2 * (a + step) + (c ^ flip)) for a in range(0, 8, 2) for c in (0, 1)]
        return lax.ppermute(after(x, *tokens), "col", pairs)

    odd = z % 2 == 1
    same = jnp.where(odd, send(chunk(2, 3), 1, 0), chunk(0, 1))
    cross = jnp.where(odd, send(chunk(3, 2), 1, 1), send(chunk(1, 0), 0, 1))
    return jnp.where(first, same, cross), jnp.where(first, cross, same)


def shards(diag_tiles, left_factors, right_factors, ranks):
    row_at = lax.axis_index("row")
    col_at = lax.axis_index("col")
    z, core = col_at // 2, col_at % 2
    place = jnp.stack([z, core, row_at]).astype(jnp.int32)
    mine = diag_tiles[0, 0]
    keep = jnp.arange(RANK)[None, :] < ranks[0, 0, 0, 0]
    zero = jnp.zeros((), BF16)
    both = jnp.concatenate(
        [jnp.where(keep, left_factors[0, 0, 0, 0], zero), jnp.where(keep, right_factors[0, 0, 0, 0], zero)], axis=1
    )

    half = halve(both, z, 4)
    band = lax.dynamic_slice(jnp.concatenate([mine, mine[:, :BAND]], axis=1), (0, BLK * z), (64, BAND))
    half_way, half = lax.optimization_barrier((spread_x(band, row_at, (0, 1)), half))
    quarter = halve(half, z, 2)
    band0, band1 = spread_y(half_way, row_at, (0, 1))
    band0, band1, quarter = lax.optimization_barrier((band0, band1, quarter))

    def onward(x, flip=0):
        pairs = [(2 * a + c, 2 * ((a + (-1 if c ^ flip else 1)) % 8) + (c ^ flip)) for a in range(8) for c in (0, 1)]
        return lax.ppermute(x, "col", pairs)

    pair = [band0, swap_core(band0)]
    part0, part1 = deal(quarter, z, core, ())
    ahead = [jnp.concatenate([onward(band0), onward(band0, 1)], axis=0)]
    ahead[0], part0, part1, pair[1] = lax.optimization_barrier((ahead[0], part0, part1, pair[1]))
    behind = [swap_core(ahead[0])]
    ahead.append(onward(ahead[0]))
    first = spread_x(part0, row_at, (1,))
    flip = lax.ppermute(
        jnp.concatenate([part0[:, RANK:], part1[:, RANK:]], axis=1),
        ("row", "col"),
        [(at(r, c), at(c, r)) for r in range(16) for c in range(16)],
    )
    ahead[1], behind[0], first, flip = lax.optimization_barrier((ahead[1], behind[0], first, flip))
    behind.append(swap_core(ahead[1]))
    ahead.append(onward(ahead[1]))
    (first,) = spread_y(first, row_at, (1,))
    ahead[2], behind[1], first = lax.optimization_barrier((ahead[2], behind[1], first))
    behind.append(swap_core(ahead[2]))
    ahead.append(onward(ahead[2]))

    hi, lo = split(band1)
    tile = lax.all_gather(jnp.concatenate([hi, lo, first, part0, part1], axis=1), "col", tiled=True)
    flip = after(flip, ahead[2])
    over_x = [
        lax.ppermute(flip, "row", [(4 * a + b, 4 * ((a + s) % 4) + b) for a in range(4) for b in range(4)])
        for s in (1, 2, 3)
    ]

    lrow0, lb0, mh0, ml0 = pl.pallas_call(
        first_kernel,
        out_shape=FACTOR,
        in_specs=[SMEM] + [VMEM] * 9,
        out_specs=[VMEM] * 4,
        scratch_shapes=[pltpu.VMEM((NB, BAND), F32), pltpu.VMEM((NB, NB), F32), pltpu.VMEM((BLK, BLK), F32)],
        compiler_params=grant(24),
        name="factor_first",
    )(place, *pair, *ahead, *behind)

    parts = [jnp.concatenate(lax.optimization_barrier((flip, *over_x, mh0))[:4], axis=0)]
    for s in (1, 2, 3):
        parts.append(
            lax.ppermute(parts[0], "row", [(4 * a + b, 4 * a + (b + s) % 4) for a in range(4) for b in range(4)])
        )

    lrow1, lb1, mh1, ml1, p10i = pl.pallas_call(
        second_kernel,
        out_shape=FACTOR + [shape(NB, 2 * RANK, BF16)],
        in_specs=[SMEM] + [ANY] * 4,
        out_specs=[VMEM] * 5,
        scratch_shapes=[
            pltpu.VMEM((NB, TILE1 + 2 * RANK), BF16),
            pltpu.VMEM((NB, NB), BF16),
            pltpu.VMEM((NB, BLK), BF16),
            pltpu.VMEM((NB, BLK), BF16),
            pltpu.VMEM((NB, NB), F32),
            pltpu.VMEM((NB, 2 * RANK), F32),
            pltpu.VMEM((BLK, BLK), F32),
            pltpu.SemaphoreType.DMA((4,)),
        ],
        compiler_params=grant(56),
        name="factor_second",
    )(place, tile, lb0, mh0, ml0)
    new, upd = pl.pallas_call(
        last_kernel,
        out_shape=[shape(64, NB, F32), shape(NB, 3 * RANK, BF16)],
        in_specs=[SMEM] + [ANY] * 15,
        out_specs=[VMEM] * 2,
        scratch_shapes=[
            pltpu.VMEM((NB, 2 * RANK), BF16),
            pltpu.VMEM((NB, 4 * RANK), BF16),
            pltpu.VMEM((NB, RANK), BF16),
            pltpu.VMEM((NB, 2 * RANK), BF16),
            pltpu.VMEM((64, NB), F32),
            pltpu.VMEM((64, NB), F32),
            pltpu.VMEM((64, NB), F32),
            pltpu.VMEM((NB, NB), BF16),
            pltpu.VMEM((NB, BLK), BF16),
            pltpu.VMEM((NB, BLK), BF16),
            pltpu.VMEM((NB, NB), BF16),
            pltpu.VMEM((NB, BLK), BF16),
            pltpu.VMEM((NB, BLK), BF16),
            pltpu.VMEM((NB, RANK), F32),
            pltpu.VMEM((NB, 3 * RANK), F32),
            pltpu.VMEM((NB, RANK), BF16),
            pltpu.VMEM((NB, 3 * RANK), BF16),
            pltpu.SemaphoreType.DMA((28,)),
        ],
        compiler_params=grant(56),
        name="finish",
    )(place, *parts, tile, p10i, mine, lrow0, lrow1, lb0, mh0, ml0, lb1, mh1, ml1)
    return new[None, None], upd[None, None, None, None]


def solution(mesh):
    in_specs = (
        P(None, "row", "col", None),
        P(None, "row", None, "col", None, None),
        P(None, "row", None, "col", None, None),
        P(None, "row", None, "col"),
    )
    out_specs = (P(None, "row", "col", None), P(None, "row", None, "col", None, None))
    return jax.shard_map(shards, mesh=mesh, in_specs=in_specs, out_specs=out_specs, check_vma=False)
```

```python
import functools

import jax
import jax.numpy as jnp
from jax import lax
from jax.experimental import pallas as pl
from jax.experimental.pallas import tpu as pltpu
from jax.sharding import PartitionSpec as P

F32 = jnp.float32
BF16 = jnp.bfloat16
NB = 1024
RANK = 256
BLK = 128
NBLK = NB // BLK
BAND = 5 * BLK
SPAN = 4
TILE1 = 2 * BAND + 2 * RANK
TN = (((0,), (0,)), ((), ()))
NT = (((1,), (1,)), ((), ()))
VMEM = pl.BlockSpec(memory_space=pltpu.VMEM)
SMEM = pl.BlockSpec(memory_space=pltpu.SMEM)
ANY = pl.BlockSpec(memory_space=pl.ANY)


def grant(mib):
    return pltpu.CompilerParams(vmem_limit_bytes=mib * 1024 * 1024)


def lanes_of(x, c):
    return jnp.broadcast_to(x[:, c : c + 1], (8, BLK))


def rows_of(x, r):
    return jnp.broadcast_to(x[r : r + 1, :], (8, BLK))


def factor_block(rows):
    sub = lax.broadcasted_iota(jnp.int32, (8, BLK), 0)
    lane = lax.broadcasted_iota(jnp.int32, (8, BLK), 1)
    a = list(rows)
    n = len(a)
    up, inv, wide = [], [], []
    cols = [lanes_of(a[0], m) for m in range(8)]
    for g in range(n):
        c0 = 8 * g
        near = min(n, g // SPAN * SPAN + 2 * SPAN)
        here = (lane >= c0) & (lane < c0 + 8)
        left = [[lanes_of(a[b], c0 + m) for m in range(8)] for b in range(g + 1, near)]
        ahead = [lanes_of(a[g + 1], c0 + 8 + m) for m in range(8)] if g + 1 < n else None
        mult, recip, piv = [], [], None
        for k in range(8):
            d = rows_of(cols[k], k)
            r = 1.0 / d
            recip.append(r)
            piv = d if piv is None else jnp.where(sub == k, d, piv)
            for m in range(k + 1, 8):
                cols[m] = cols[m] - (cols[k] * rows_of(cols[k], m)) * r
            mult.append(jnp.where(sub > k, cols[k] * r, 0.0))
        s = jnp.where(here, jnp.where(lane == c0 + sub, 1.0, 0.0), a[g])
        s2 = a[g]
        for k in range(7):
            s = s - mult[k] * rows_of(s, k)
            s2 = s2 - mult[k] * rows_of(s2, k)
        root = lax.rsqrt(piv)
        r_ = s * root
        t = r_ * root
        diag = jnp.where(lane >= c0 + sub, s2 * root, 0.0)
        up.append(jnp.where(here, diag, jnp.where(lane >= c0 + 8, r_, 0.0)))
        inv.append(jnp.where(lane < c0 + 8, r_, 0.0))
        if g + 1 == n:
            break
        mk = [[rows_of(mult[k], m) if m > k else None for m in range(8)] for k in range(8)]
        tk = [rows_of(t, k) for k in range(8)]
        for b in range(g + 1, near):
            x = left[b - g - 1]
            for k in range(8):
                for m in range(k + 1, 8):
                    x[m] = x[m] - x[k] * mk[k][m]
            if b == g + 1:
                cols = ahead
                for k in range(8):
                    xs = x[k] * recip[k]
                    for m in range(8):
                        cols[m] = cols[m] - x[k] * rows_of(xs, m)
            new = jnp.where(here, 0.0, a[b])
            for k in range(8):
                new = new - x[k] * tk[k]
            a[b] = new
        wide.append(jnp.where((lane >= c0 + 8) & (lane < 8 * (g // SPAN * SPAN + SPAN)), 0.0, r_))
        if (g + 1) % SPAN == 0 and near < n:
            hi, lo = split(jnp.concatenate(wide, axis=0))
            wide = []
            both = tn32(hi, hi) + (tn32(hi, lo) + tn32(lo, hi))
            done = (lane >= c0 + 8 - 8 * SPAN) & (lane < c0 + 8)
            for b in range(near, n):
                a[b] = jnp.where(done, 0.0, a[b]) - both[8 * b : 8 * b + 8]
    return up, inv


def split(x):
    hi = x.astype(BF16)
    return hi, (x - hi.astype(F32)).astype(BF16)


def tn32(a, b):
    return lax.dot_general(a, b, TN, preferred_element_type=F32)


def tn(a, b):
    return tn32(a, b).astype(BF16)


def mm(a, b):
    return jnp.dot(a, b, preferred_element_type=F32)


def mm3(a, b):
    return mm(a[0], b[0]) + (mm(a[0], b[1]) + mm(a[1], b[0]))


def unfold(work, take):
    for r in range(NBLK):
        n = min(5, NBLK - r)
        rows = slice(r * BLK, (r + 1) * BLK)
        work[rows, r * BLK : (r + n) * BLK] = take(r, slice(0, n * BLK))
        for c in range(r + 5, NBLK):
            o = (NBLK - (c - r)) * BLK
            work[rows, c * BLK : (c + 1) * BLK] = take(c, slice(o, o + BLK)).T


def cholesky_blocks(work, lb, mh, ml, inv_s):
    def body(k, _):
        off = pl.multiple_of(k * BLK, BLK)
        rows = [work[pl.ds(pl.multiple_of(off + 8 * i, 8), 8), pl.ds(off, BLK)] for i in range(16)]
        up, inv = factor_block(rows)
        for i in range(16):
            inv_s[8 * i : 8 * i + 8, :] = inv[i]
        work[pl.ds(off, BLK), pl.ds(off, BLK)] = jnp.concatenate(up, axis=0).T
        hi, lo = split(inv_s[...])
        mh[pl.ds(off, BLK), :] = hi
        ml[pl.ds(off, BLK), :] = lo
        for kk in range(NBLK - 1):

            @pl.when(k == kk)
            def _():
                o = BLK * kk
                e = o + BLK
                upper = mm3((hi, lo), split(work[o:e, e:]))
                parts = split(upper)
                for ib in range(kk + 1, NBLK):
                    i0 = BLK * ib
                    c = i0 - e
                    low = upper[:, c : c + BLK].T
                    lows = split(low)
                    lb[i0 : i0 + BLK, o:e] = lows[0]
                    work[i0 : i0 + BLK, o:e] = low
                    work[i0 : i0 + BLK, i0:] = work[i0 : i0 + BLK, i0:] - mm3(
                        lows, (parts[0][:, c:], parts[1][:, c:])
                    )

        return 0

    lax.fori_loop(0, NBLK, body, 0)


def write_rows(place, work, lrow):
    start = pl.multiple_of(64 * (2 * place[0] + place[1]), 64)
    r = lax.broadcasted_iota(jnp.int32, (64, NB), 0) + start
    c = lax.broadcasted_iota(jnp.int32, (64, NB), 1)
    lrow[...] = jnp.where(c <= r, work[pl.ds(start, 64), :], 0.0)


def fetch(pairs, sems):
    copies = [pltpu.make_async_copy(src, dst, sems.at[n]) for n, (src, dst) in enumerate(pairs)]
    for one in copies:
        one.start()
    return copies


def first_kernel(place, raw_h, lrow, lb, mh, ml, raw, work, inv_s, sems):
    for one in fetch([(raw_h, raw)], sems):
        one.wait()
    unfold(work, lambda r, cols: raw[r * BLK : (r + 1) * BLK, cols])
    cholesky_blocks(work, lb, mh, ml, inv_s)
    write_rows(place, work, lrow)


def solve_step(k, w, lb, mh, ml, p):
    o = BLK * k
    e = o + BLK
    x = mm3((mh[o:e, :], ml[o:e, :]), split(w[o:e, :]))
    p[o:e, :] = x.astype(BF16)
    if e < NB:
        xs = split(x)
        low = lb[e:, o:e]
        w[e:, :] = w[e:, :] - (mm(low, xs[0]) + mm(low, xs[1]))


def second_kernel(
    place, tile_h, lb0_h, mh0_h, ml0_h, lrow, lb, mh, ml, p10, tile, lb0, mh0, ml0, work, w, inv_s, sems
):
    copies = fetch([(tile_h.at[:, : TILE1 + 2 * RANK], tile), (mh0_h, mh0), (ml0_h, ml0), (lb0_h, lb0)], sems)
    for one in copies:
        one.wait()
    w[:, :RANK] = tile[:, 2 * BAND + RANK : TILE1].astype(F32)
    w[:, RANK:] = tile[:, TILE1 + RANK : TILE1 + 2 * RANK].astype(F32)
    for k in range(NBLK):
        solve_step(k, w, lb0, mh0, ml0, p10)
    solved = p10[:, :RANK]
    inner = lax.dot_general(solved, solved, TN, preferred_element_type=F32).astype(BF16)
    u = tile[:, 2 * BAND : 2 * BAND + RANK]
    corr = split(mm(u, inner))

    def take(r, cols):
        rows = slice(r * BLK, (r + 1) * BLK)
        return tile[rows, cols].astype(F32) + tile[rows, cols.start + BAND : cols.stop + BAND].astype(F32)

    unfold(work, take)
    for r in range(NBLK):
        o = r * BLK
        right = u[o:, :]
        work[o : o + BLK, o:] = work[o : o + BLK, o:] - (
            lax.dot_general(corr[0][o : o + BLK], right, NT, preferred_element_type=F32)
            + lax.dot_general(corr[1][o : o + BLK], right, NT, preferred_element_type=F32)
        )
    cholesky_blocks(work, lb, mh, ml, inv_s)
    write_rows(place, work, lrow)


def last_kernel(place, *refs):
    parts, (tile_h, p10i_h, diag_h, lrow0_h, lrow1_h) = refs[:4], refs[4:9]
    lb0_h, mh0_h, ml0_h, lb1_h, mh1_h, ml1_h, new, upd = refs[9:17]
    (cols, rows, u10, p10i, diag, lrow0, lrow1, lb0, mh0, ml0, lb1, mh1, ml1, w0, w1, pj, p1, sems) = refs[17:]
    j = 2 * place[0] + place[1]
    i = place[2]
    x, y = i // 4, lax.rem(i, 4)
    pairs = [(tile_h.at[:, TILE1:], rows), (tile_h.at[:, 2 * BAND : 2 * BAND + RANK], u10)]
    for b in range(4):
        for a in range(4):
            k = 4 * lax.rem(x + 4 - a, 4) + lax.rem(y + 4 - b, 4)
            pairs.append((parts[b].at[pl.ds(64 * a, 64)], cols.at[pl.ds(pl.multiple_of(64 * k, 64), 64)]))
    head = len(pairs)
    pairs += [(mh0_h, mh0), (ml0_h, ml0), (mh1_h, mh1), (ml1_h, ml1), (lb0_h, lb0), (lb1_h, lb1)]
    body = len(pairs)
    pairs += [(p10i_h, p10i), (diag_h, diag), (lrow0_h, lrow0), (lrow1_h, lrow1)]
    copies = fetch(pairs, sems)
    for one in copies[:head]:
        one.wait()
    w0[...] = cols[:, :RANK].astype(F32)
    w1[:, :RANK] = rows[:, 3 * RANK :].astype(F32)
    w1[:, RANK : 2 * RANK] = u10[...].astype(F32)
    w1[:, 2 * RANK :] = cols[:, RANK:].astype(F32)
    for one in copies[head:body]:
        one.wait()
    for k in range(NBLK):
        solve_step(k, w0, lb0, mh0, ml0, pj)
        solve_step(k, w1, lb1, mh1, ml1, p1)
    for one in copies[body:]:
        one.wait()
    zero = jnp.zeros((), BF16)
    pi = jnp.where(i > 0, p10i[:, RANK:], zero)
    ui = rows[:, :RANK]
    start = pl.multiple_of(64 * j, 64)
    ui_part = rows[pl.ds(start, 64), :RANK]
    inner01 = tn(pi, p10i[:, :RANK])
    c0 = mm(ui, tn(pi, pj[...])).astype(BF16)
    c01 = mm(ui, inner01).astype(BF16)
    c0_part = mm(ui_part, tn(pi, pi)).astype(BF16)
    d = diag[...] - lax.dot_general(c0_part, ui, NT, preferred_element_type=F32)
    upd[:, :RANK] = jnp.where(j == 0, pi, jnp.where((i > j) & (j > 0), c0, zero))
    q = jnp.where(i > 1, p1[...], zero)
    q_i = q[:, : 2 * RANK]
    square = tn(q_i, q_i)
    inner = jnp.concatenate([tn(q_i, q[:, 2 * RANK :]), square[:, RANK:]], axis=1)
    up = jnp.concatenate([rows[:, 2 * RANK : 3 * RANK], -c01], axis=1)
    c1 = mm(up, inner).astype(BF16)
    up_part = jnp.concatenate(
        [rows[pl.ds(start, 64), 2 * RANK : 3 * RANK], -mm(ui_part, inner01).astype(BF16)], axis=1
    )
    c1_part = mm(up_part, square).astype(BF16)
    d = d - lax.dot_general(c1_part, up, NT, preferred_element_type=F32)
    new[...] = jnp.where(i == 0, lrow0[...], jnp.where(i == 1, lrow1[...], d))
    upd[:, RANK:] = jnp.where(j == 1, q_i, jnp.where((i > j) & (j > 1), c1, zero))


def shape(rows, cols, dtype):
    return jax.ShapeDtypeStruct((rows, cols), dtype)


FACTOR = [shape(64, NB, F32), shape(NB, NB, BF16), shape(NB, BLK, BF16), shape(NB, BLK, BF16)]


def swap_core(x):
    return lax.ppermute(x, "col", [(c, c ^ 1) for c in range(16)])


def after(x, *tokens):
    return lax.optimization_barrier((x, *tokens))[0]


def at(row, col):
    return 16 * row + col


def pick(cases, default):
    for hit, x in cases:
        default = jnp.where(hit, x, default)
    return default


def spread_x(x, row_at, rows):
    got = [lax.ppermute(x, "row", [(y, 4 * k + y) for y in rows]) for k in (1, 2, 3)]
    return pick([(row_at // 4 == k, got[k - 1]) for k in (1, 2, 3)], x)


def spread_y(x, row_at, rows):
    got = [lax.ppermute(x, "row", [(4 * a + y, 4 * a + (y + s) % 4) for a in range(4) for y in rows]) for s in (1, 2, 3)]
    return [pick([(row_at % 4 == (y + s) % 4, got[s - 1]) for s in (1, 2, 3)], x) for y in rows]


def halve(x, z, gap):
    half = x.shape[0] // 2
    pairs = [(2 * a + c, 2 * (a + gap) + c) for a in range(0, 8, 2 * gap) for c in (0, 1)]
    got = lax.ppermute(x[half:], "col", pairs)
    return jnp.where((z // gap) % 2 == 1, got, x[:half])


def deal(cur, z, core, tokens):
    first = core == 0

    def chunk(q0, q1):
        return jnp.where(first, cur[64 * q0 : 64 * q0 + 64], cur[64 * q1 : 64 * q1 + 64])

    def send(x, step, flip):
        pairs = [(2 * a + c, 2 * (a + step) + (c ^ flip)) for a in range(0, 8, 2) for c in (0, 1)]
        return lax.ppermute(after(x, *tokens), "col", pairs)

    odd = z % 2 == 1
    same = jnp.where(odd, send(chunk(2, 3), 1, 0), chunk(0, 1))
    cross = jnp.where(odd, send(chunk(3, 2), 1, 1), send(chunk(1, 0), 0, 1))
    return jnp.where(first, same, cross), jnp.where(first, cross, same)


def shards(diag_tiles, left_factors, right_factors, ranks):
    row_at = lax.axis_index("row")
    col_at = lax.axis_index("col")
    z, core = col_at // 2, col_at % 2
    place = jnp.stack([z, core, row_at]).astype(jnp.int32)
    mine = diag_tiles[0, 0]
    keep = jnp.arange(RANK)[None, :] < ranks[0, 0, 0, 0]
    zero = jnp.zeros((), BF16)
    both = jnp.concatenate(
        [jnp.where(keep, left_factors[0, 0, 0, 0], zero), jnp.where(keep, right_factors[0, 0, 0, 0], zero)], axis=1
    )

    band = lax.dynamic_slice(jnp.concatenate([mine, mine[:, :BAND]], axis=1), (0, BLK * z), (64, BAND))
    half_way = spread_x(band, row_at, (0, 1))
    half = halve(after(both, half_way), z, 4)
    band0, band1 = spread_y(half_way, row_at, (0, 1))
    raw0 = lax.all_gather(band0, "col", tiled=True)

    quarter = halve(after(half, band0), z, 2)
    part0, part1 = deal(quarter, z, core, ())
    first = spread_x(part0, row_at, (1,))
    flip = lax.ppermute(
        jnp.concatenate([part0[:, RANK:], part1[:, RANK:]], axis=1),
        ("row", "col"),
        [(at(r, c), at(c, r)) for r in range(16) for c in range(16)],
    )
    first, flip = lax.optimization_barrier((first, flip))
    (first,) = spread_y(first, row_at, (1,))
    hi, lo = split(band1)
    tile = lax.all_gather(jnp.concatenate([hi, lo, first, part0, part1], axis=1), "col", tiled=True)
    over_x = [
        lax.ppermute(flip, "row", [(4 * a + b, 4 * ((a + s) % 4) + b) for a in range(4) for b in range(4)])
        for s in (1, 2, 3)
    ]

    lrow0, lb0, mh0, ml0 = pl.pallas_call(
        first_kernel,
        out_shape=FACTOR,
        in_specs=[SMEM, ANY],
        out_specs=[VMEM] * 4,
        scratch_shapes=[
            pltpu.VMEM((NB, BAND), F32),
            pltpu.VMEM((NB, NB), F32),
            pltpu.VMEM((BLK, BLK), F32),
            pltpu.SemaphoreType.DMA((1,)),
        ],
        compiler_params=grant(56),
        name="factor_first",
    )(place, raw0)

    parts = [jnp.concatenate(lax.optimization_barrier((flip, *over_x, mh0))[:4], axis=0)]
    for s in (1, 2, 3):
        parts.append(
            lax.ppermute(parts[0], "row", [(4 * a + b, 4 * a + (b + s) % 4) for a in range(4) for b in range(4)])
        )

    lrow1, lb1, mh1, ml1, p10i = pl.pallas_call(
        second_kernel,
        out_shape=FACTOR + [shape(NB, 2 * RANK, BF16)],
        in_specs=[SMEM] + [ANY] * 4,
        out_specs=[VMEM] * 5,
        scratch_shapes=[
            pltpu.VMEM((NB, TILE1 + 2 * RANK), BF16),
            pltpu.VMEM((NB, NB), BF16),
            pltpu.VMEM((NB, BLK), BF16),
            pltpu.VMEM((NB, BLK), BF16),
            pltpu.VMEM((NB, NB), F32),
            pltpu.VMEM((NB, 2 * RANK), F32),
            pltpu.VMEM((BLK, BLK), F32),
            pltpu.SemaphoreType.DMA((4,)),
        ],
        compiler_params=grant(56),
        name="factor_second",
    )(place, tile, lb0, mh0, ml0)
    new, upd = pl.pallas_call(
        last_kernel,
        out_shape=[shape(64, NB, F32), shape(NB, 3 * RANK, BF16)],
        in_specs=[SMEM] + [ANY] * 15,
        out_specs=[VMEM] * 2,
        scratch_shapes=[
            pltpu.VMEM((NB, 2 * RANK), BF16),
            pltpu.VMEM((NB, 4 * RANK), BF16),
            pltpu.VMEM((NB, RANK), BF16),
            pltpu.VMEM((NB, 2 * RANK), BF16),
            pltpu.VMEM((64, NB), F32),
            pltpu.VMEM((64, NB), F32),
            pltpu.VMEM((64, NB), F32),
            pltpu.VMEM((NB, NB), BF16),
            pltpu.VMEM((NB, BLK), BF16),
            pltpu.VMEM((NB, BLK), BF16),
            pltpu.VMEM((NB, NB), BF16),
            pltpu.VMEM((NB, BLK), BF16),
            pltpu.VMEM((NB, BLK), BF16),
            pltpu.VMEM((NB, RANK), F32),
            pltpu.VMEM((NB, 3 * RANK), F32),
            pltpu.VMEM((NB, RANK), BF16),
            pltpu.VMEM((NB, 3 * RANK), BF16),
            pltpu.SemaphoreType.DMA((28,)),
        ],
        compiler_params=grant(56),
        name="finish",
    )(place, *parts, tile, p10i, mine, lrow0, lrow1, lb0, mh0, ml0, lb1, mh1, ml1)
    return new[None, None], upd[None, None, None, None]


def solution(mesh):
    in_specs = (
        P(None, "row", "col", None),
        P(None, "row", None, "col", None, None),
        P(None, "row", None, "col", None, None),
        P(None, "row", None, "col"),
    )
    out_specs = (P(None, "row", "col", None), P(None, "row", None, "col", None, None))
    return jax.shard_map(shards, mesh=mesh, in_specs=in_specs, out_specs=out_specs, check_vma=False)
```

```python
import functools

import jax
import jax.numpy as jnp
from jax import lax
from jax.experimental import pallas as pl
from jax.experimental.pallas import tpu as pltpu
from jax.sharding import PartitionSpec as P

F32 = jnp.float32
BF16 = jnp.bfloat16
NB = 1024
RANK = 256
BLK = 128
NBLK = NB // BLK
BAND = 5 * BLK
SPAN = 4
TILE1 = 2 * BAND + 2 * RANK
TN = (((0,), (0,)), ((), ()))
NT = (((1,), (1,)), ((), ()))
VMEM = pl.BlockSpec(memory_space=pltpu.VMEM)
SMEM = pl.BlockSpec(memory_space=pltpu.SMEM)
ANY = pl.BlockSpec(memory_space=pl.ANY)


def grant(mib):
    return pltpu.CompilerParams(vmem_limit_bytes=mib * 1024 * 1024)


def lanes_of(x, c):
    return jnp.broadcast_to(x[:, c : c + 1], (8, BLK))


def rows_of(x, r):
    return jnp.broadcast_to(x[r : r + 1, :], (8, BLK))


def factor_block(rows):
    sub = lax.broadcasted_iota(jnp.int32, (8, BLK), 0)
    lane = lax.broadcasted_iota(jnp.int32, (8, BLK), 1)
    a = list(rows)
    n = len(a)
    up, inv, wide = [], [], []
    cols = [lanes_of(a[0], m) for m in range(8)]
    for g in range(n):
        c0 = 8 * g
        near = min(n, g // SPAN * SPAN + 2 * SPAN)
        here = (lane >= c0) & (lane < c0 + 8)
        left = [[lanes_of(a[b], c0 + m) for m in range(8)] for b in range(g + 1, near)]
        ahead = [lanes_of(a[g + 1], c0 + 8 + m) for m in range(8)] if g + 1 < n else None
        mult, recip, piv = [], [], None
        for k in range(8):
            d = rows_of(cols[k], k)
            r = 1.0 / d
            recip.append(r)
            piv = d if piv is None else jnp.where(sub == k, d, piv)
            for m in range(k + 1, 8):
                cols[m] = cols[m] - (cols[k] * rows_of(cols[k], m)) * r
            mult.append(jnp.where(sub > k, cols[k] * r, 0.0))
        s = jnp.where(here, jnp.where(lane == c0 + sub, 1.0, 0.0), a[g])
        s2 = a[g]
        for k in range(7):
            s = s - mult[k] * rows_of(s, k)
            s2 = s2 - mult[k] * rows_of(s2, k)
        root = lax.rsqrt(piv)
        r_ = s * root
        t = r_ * root
        diag = jnp.where(lane >= c0 + sub, s2 * root, 0.0)
        up.append(jnp.where(here, diag, jnp.where(lane >= c0 + 8, r_, 0.0)))
        inv.append(jnp.where(lane < c0 + 8, r_, 0.0))
        if g + 1 == n:
            break
        mk = [[rows_of(mult[k], m) if m > k else None for m in range(8)] for k in range(8)]
        tk = [rows_of(t, k) for k in range(8)]
        for b in range(g + 1, near):
            x = left[b - g - 1]
            for k in range(8):
                for m in range(k + 1, 8):
                    x[m] = x[m] - x[k] * mk[k][m]
            if b == g + 1:
                cols = ahead
                for k in range(8):
                    xs = x[k] * recip[k]
                    for m in range(8):
                        cols[m] = cols[m] - x[k] * rows_of(xs, m)
            new = jnp.where(here, 0.0, a[b])
            for k in range(8):
                new = new - x[k] * tk[k]
            a[b] = new
        wide.append(jnp.where((lane >= c0 + 8) & (lane < 8 * (g // SPAN * SPAN + SPAN)), 0.0, r_))
        if (g + 1) % SPAN == 0 and near < n:
            hi, lo = split(jnp.concatenate(wide, axis=0))
            wide = []
            both = tn32(hi, hi) + (tn32(hi, lo) + tn32(lo, hi))
            done = (lane >= c0 + 8 - 8 * SPAN) & (lane < c0 + 8)
            for b in range(near, n):
                a[b] = jnp.where(done, 0.0, a[b]) - both[8 * b : 8 * b + 8]
    return up, inv


def split(x):
    hi = x.astype(BF16)
    return hi, (x - hi.astype(F32)).astype(BF16)


def tn32(a, b):
    return lax.dot_general(a, b, TN, preferred_element_type=F32)


def tn(a, b):
    return tn32(a, b).astype(BF16)


def mm(a, b):
    return jnp.dot(a, b, preferred_element_type=F32)


def mm3(a, b):
    return mm(a[0], b[0]) + (mm(a[0], b[1]) + mm(a[1], b[0]))


def unfold(work, take):
    for r in range(NBLK):
        n = min(5, NBLK - r)
        rows = slice(r * BLK, (r + 1) * BLK)
        work[rows, r * BLK : (r + n) * BLK] = take(r, slice(0, n * BLK))
        for c in range(r + 5, NBLK):
            o = (NBLK - (c - r)) * BLK
            work[rows, c * BLK : (c + 1) * BLK] = take(c, slice(o, o + BLK)).T


def cholesky_blocks(work, lb, mh, ml, inv_s):
    def body(k, _):
        off = pl.multiple_of(k * BLK, BLK)
        rows = [work[pl.ds(pl.multiple_of(off + 8 * i, 8), 8), pl.ds(off, BLK)] for i in range(16)]
        up, inv = factor_block(rows)
        for i in range(16):
            inv_s[8 * i : 8 * i + 8, :] = inv[i]
        work[pl.ds(off, BLK), pl.ds(off, BLK)] = jnp.concatenate(up, axis=0).T
        hi, lo = split(inv_s[...])
        mh[pl.ds(off, BLK), :] = hi
        ml[pl.ds(off, BLK), :] = lo
        for kk in range(NBLK - 1):

            @pl.when(k == kk)
            def _():
                o = BLK * kk
                e = o + BLK
                upper = mm3((hi, lo), split(work[o:e, e:]))
                parts = split(upper)
                for ib in range(kk + 1, NBLK):
                    i0 = BLK * ib
                    c = i0 - e
                    low = upper[:, c : c + BLK].T
                    lows = split(low)
                    lb[i0 : i0 + BLK, o:e] = lows[0]
                    work[i0 : i0 + BLK, o:e] = low
                    work[i0 : i0 + BLK, i0:] = work[i0 : i0 + BLK, i0:] - mm3(
                        lows, (parts[0][:, c:], parts[1][:, c:])
                    )

        return 0

    lax.fori_loop(0, NBLK, body, 0)


def write_rows(place, work, lrow):
    start = pl.multiple_of(64 * (2 * place[0] + place[1]), 64)
    r = lax.broadcasted_iota(jnp.int32, (64, NB), 0) + start
    c = lax.broadcasted_iota(jnp.int32, (64, NB), 1)
    lrow[...] = jnp.where(c <= r, work[pl.ds(start, 64), :], 0.0)


def first_kernel(place, *refs):
    shards_in = refs[:16]
    lrow, lb, mh, ml, raw, work, inv_s = refs[16:]
    z, core = place[0], place[1]
    for i in range(16):
        n = lax.rem(z + i % 8, 8)
        half = core if i < 8 else 1 - core
        raw[pl.ds(pl.multiple_of(n * BLK + half * 64, 64), 64), :] = shards_in[i][...]
    unfold(work, lambda r, cols: raw[r * BLK : (r + 1) * BLK, cols])
    cholesky_blocks(work, lb, mh, ml, inv_s)
    write_rows(place, work, lrow)


def solve_step(k, w, lb, mh, ml, p):
    o = BLK * k
    e = o + BLK
    x = mm3((mh[o:e, :], ml[o:e, :]), split(w[o:e, :]))
    p[o:e, :] = x.astype(BF16)
    if e < NB:
        xs = split(x)
        low = lb[e:, o:e]
        w[e:, :] = w[e:, :] - (mm(low, xs[0]) + mm(low, xs[1]))


def fetch(pairs, sems):
    copies = [pltpu.make_async_copy(src, dst, sems.at[n]) for n, (src, dst) in enumerate(pairs)]
    for one in copies:
        one.start()
    return copies


def second_kernel(
    place, tile_h, lb0_h, mh0_h, ml0_h, lrow, lb, mh, ml, p10, tile, lb0, mh0, ml0, work, w, inv_s, sems
):
    copies = fetch([(tile_h.at[:, : TILE1 + 2 * RANK], tile), (mh0_h, mh0), (ml0_h, ml0), (lb0_h, lb0)], sems)
    for one in copies:
        one.wait()
    w[:, :RANK] = tile[:, 2 * BAND + RANK : TILE1].astype(F32)
    w[:, RANK:] = tile[:, TILE1 + RANK : TILE1 + 2 * RANK].astype(F32)
    for k in range(NBLK):
        solve_step(k, w, lb0, mh0, ml0, p10)
    solved = p10[:, :RANK]
    inner = lax.dot_general(solved, solved, TN, preferred_element_type=F32).astype(BF16)
    u = tile[:, 2 * BAND : 2 * BAND + RANK]
    corr = split(mm(u, inner))

    def take(r, cols):
        rows = slice(r * BLK, (r + 1) * BLK)
        return tile[rows, cols].astype(F32) + tile[rows, cols.start + BAND : cols.stop + BAND].astype(F32)

    unfold(work, take)
    for r in range(NBLK):
        o = r * BLK
        right = u[o:, :]
        work[o : o + BLK, o:] = work[o : o + BLK, o:] - (
            lax.dot_general(corr[0][o : o + BLK], right, NT, preferred_element_type=F32)
            + lax.dot_general(corr[1][o : o + BLK], right, NT, preferred_element_type=F32)
        )
    cholesky_blocks(work, lb, mh, ml, inv_s)
    write_rows(place, work, lrow)


def last_kernel(place, *refs):
    parts, (tile_h, p10i_h, diag_h, lrow0_h, lrow1_h) = refs[:4], refs[4:9]
    lb0_h, mh0_h, ml0_h, lb1_h, mh1_h, ml1_h, new, upd = refs[9:17]
    (cols, rows, u10, p10i, diag, lrow0, lrow1, lb0, mh0, ml0, lb1, mh1, ml1, w0, w1, pj, p1, sems) = refs[17:]
    j = 2 * place[0] + place[1]
    i = place[2]
    x, y = i // 4, lax.rem(i, 4)
    pairs = [(tile_h.at[:, TILE1:], rows), (tile_h.at[:, 2 * BAND : 2 * BAND + RANK], u10)]
    for b in range(4):
        for a in range(4):
            k = 4 * lax.rem(x + 4 - a, 4) + lax.rem(y + 4 - b, 4)
            pairs.append((parts[b].at[pl.ds(64 * a, 64)], cols.at[pl.ds(pl.multiple_of(64 * k, 64), 64)]))
    head = len(pairs)
    pairs += [(mh0_h, mh0), (ml0_h, ml0), (mh1_h, mh1), (ml1_h, ml1), (lb0_h, lb0), (lb1_h, lb1)]
    body = len(pairs)
    pairs += [(p10i_h, p10i), (diag_h, diag), (lrow0_h, lrow0), (lrow1_h, lrow1)]
    copies = fetch(pairs, sems)
    for one in copies[:head]:
        one.wait()
    w0[...] = cols[:, :RANK].astype(F32)
    w1[:, :RANK] = rows[:, 3 * RANK :].astype(F32)
    w1[:, RANK : 2 * RANK] = u10[...].astype(F32)
    w1[:, 2 * RANK :] = cols[:, RANK:].astype(F32)
    for one in copies[head:body]:
        one.wait()
    for k in range(NBLK):
        solve_step(k, w0, lb0, mh0, ml0, pj)
        solve_step(k, w1, lb1, mh1, ml1, p1)
    for one in copies[body:]:
        one.wait()
    zero = jnp.zeros((), BF16)
    pi = jnp.where(i > 0, p10i[:, RANK:], zero)
    ui = rows[:, :RANK]
    start = pl.multiple_of(64 * j, 64)
    ui_part = rows[pl.ds(start, 64), :RANK]
    inner01 = tn(pi, p10i[:, :RANK])
    c0 = mm(ui, tn(pi, pj[...])).astype(BF16)
    c01 = mm(ui, inner01).astype(BF16)
    c0_part = mm(ui_part, tn(pi, pi)).astype(BF16)
    d = diag[...] - lax.dot_general(c0_part, ui, NT, preferred_element_type=F32)
    upd[:, :RANK] = jnp.where(j == 0, pi, jnp.where((i > j) & (j > 0), c0, zero))
    q = jnp.where(i > 1, p1[...], zero)
    q_i = q[:, : 2 * RANK]
    square = tn(q_i, q_i)
    inner = jnp.concatenate([tn(q_i, q[:, 2 * RANK :]), square[:, RANK:]], axis=1)
    up = jnp.concatenate([rows[:, 2 * RANK : 3 * RANK], -c01], axis=1)
    c1 = mm(up, inner).astype(BF16)
    up_part = jnp.concatenate(
        [rows[pl.ds(start, 64), 2 * RANK : 3 * RANK], -mm(ui_part, inner01).astype(BF16)], axis=1
    )
    c1_part = mm(up_part, square).astype(BF16)
    d = d - lax.dot_general(c1_part, up, NT, preferred_element_type=F32)
    new[...] = jnp.where(i == 0, lrow0[...], jnp.where(i == 1, lrow1[...], d))
    upd[:, RANK:] = jnp.where(j == 1, q_i, jnp.where((i > j) & (j > 1), c1, zero))


def shape(rows, cols, dtype):
    return jax.ShapeDtypeStruct((rows, cols), dtype)


FACTOR = [shape(64, NB, F32), shape(NB, NB, BF16), shape(NB, BLK, BF16), shape(NB, BLK, BF16)]


def shift_z(x, s):
    return lax.ppermute(x, "col", [(2 * z + c, 2 * ((z + s) % 8) + c) for z in range(8) for c in range(2)])


def swap_core(x):
    return lax.ppermute(x, "col", [(c, c ^ 1) for c in range(16)])


def after(x, *tokens):
    return lax.optimization_barrier((x, *tokens))[0]


def at(row, col):
    return 16 * row + col


def pick(cases, default):
    for hit, x in cases:
        default = jnp.where(hit, x, default)
    return default


def spread_x(x, row_at, rows):
    got = [lax.ppermute(x, "row", [(y, 4 * k + y) for y in rows]) for k in (1, 2, 3)]
    return pick([(row_at // 4 == k, got[k - 1]) for k in (1, 2, 3)], x)


def spread_y(x, row_at, rows):
    got = [lax.ppermute(x, "row", [(4 * a + y, 4 * a + (y + s) % 4) for a in range(4) for y in rows]) for s in (1, 2, 3)]
    return [pick([(row_at % 4 == (y + s) % 4, got[s - 1]) for s in (1, 2, 3)], x) for y in rows]


def halve(x, z, gap):
    half = x.shape[0] // 2
    pairs = [(2 * a + c, 2 * (a + gap) + c) for a in range(0, 8, 2 * gap) for c in (0, 1)]
    got = lax.ppermute(x[half:], "col", pairs)
    return jnp.where((z // gap) % 2 == 1, got, x[:half])


def deal(cur, z, core, tokens):
    first = core == 0

    def chunk(q0, q1):
        return jnp.where(first, cur[64 * q0 : 64 * q0 + 64], cur[64 * q1 : 64 * q1 + 64])

    def send(x, step, flip):
        pairs = [(2 * a + c, 2 * (a + step) + (c ^ flip)) for a in range(0, 8, 2) for c in (0, 1)]
        return lax.ppermute(after(x, *tokens), "col", pairs)

    odd = z % 2 == 1
    same = jnp.where(odd, send(chunk(2, 3), 1, 0), chunk(0, 1))
    cross = jnp.where(odd, send(chunk(3, 2), 1, 1), send(chunk(1, 0), 0, 1))
    return jnp.where(first, same, cross), jnp.where(first, cross, same)


def shards(diag_tiles, left_factors, right_factors, ranks):
    row_at = lax.axis_index("row")
    col_at = lax.axis_index("col")
    z, core = col_at // 2, col_at % 2
    place = jnp.stack([z, core, row_at]).astype(jnp.int32)
    mine = diag_tiles[0, 0]
    keep = jnp.arange(RANK)[None, :] < ranks[0, 0, 0, 0]
    zero = jnp.zeros((), BF16)
    both = jnp.concatenate(
        [jnp.where(keep, left_factors[0, 0, 0, 0], zero), jnp.where(keep, right_factors[0, 0, 0, 0], zero)], axis=1
    )

    half = halve(both, z, 4)

    band = lax.dynamic_slice(jnp.concatenate([mine, mine[:, :BAND]], axis=1), (0, BLK * z), (64, BAND))
    band0, band1 = spread_y(spread_x(band, row_at, (0, 1)), row_at, (0, 1))
    band0, half = lax.optimization_barrier((band0, half))
    fwd, bwd = [band0], [band0]
    fwd_other, bwd_other = [swap_core(band0)], []
    for _ in range(3):
        fwd.append(shift_z(fwd[-1], 1))
        bwd.append(shift_z(bwd[-1], -1))
        ready = (fwd_other[-1], *bwd_other[-1:])
        fwd[-1], bwd[-1], *_ = lax.optimization_barrier((fwd[-1], bwd[-1], *ready))
        fwd_other.append(swap_core(fwd[-1]))
        bwd_other.append(swap_core(bwd[-1]))
    fwd.append(shift_z(fwd[-1], 1))
    cross = lax.ppermute(bwd[3], "col", [(2 * a + c, 2 * ((a - 1) % 8) + 1 - c) for a in range(8) for c in (0, 1)])
    own = [band0, bwd[1], bwd[2], bwd[3], fwd[4], fwd[3], fwd[2], fwd[1]]
    theirs = [fwd_other[0], *bwd_other, cross, *fwd_other[:0:-1]]

    part0, part1 = deal(halve(half, z, 2), z, core, (fwd[1], bwd[1]))
    first = spread_x(after(part0, fwd[2], bwd[2]), row_at, (1,))
    flip = lax.ppermute(
        after(jnp.concatenate([part0[:, RANK:], part1[:, RANK:]], axis=1), fwd[2], bwd[2]),
        ("row", "col"),
        [(at(r, c), at(c, r)) for r in range(16) for c in range(16)],
    )
    first, flip = lax.optimization_barrier((first, flip))
    (first,) = spread_y(after(first, fwd[3], bwd[3]), row_at, (1,))
    hi, lo = split(band1)
    tile = lax.all_gather(
        after(jnp.concatenate([hi, lo, first, part0, part1], axis=1), fwd[4], cross), "col", tiled=True
    )
    over_x = [
        lax.ppermute(flip, "row", [(4 * a + b, 4 * ((a + s) % 4) + b) for a in range(4) for b in range(4)])
        for s in (1, 2, 3)
    ]

    lrow0, lb0, mh0, ml0 = pl.pallas_call(
        first_kernel,
        out_shape=FACTOR,
        in_specs=[SMEM] + [VMEM] * 16,
        out_specs=[VMEM] * 4,
        scratch_shapes=[pltpu.VMEM((NB, BAND), F32), pltpu.VMEM((NB, NB), F32), pltpu.VMEM((BLK, BLK), F32)],
        compiler_params=grant(24),
        name="factor_first",
    )(place, *own, *theirs)

    parts = [jnp.concatenate(lax.optimization_barrier((flip, *over_x, mh0))[:4], axis=0)]
    for s in (1, 2, 3):
        parts.append(
            lax.ppermute(parts[0], "row", [(4 * a + b, 4 * a + (b + s) % 4) for a in range(4) for b in range(4)])
        )

    lrow1, lb1, mh1, ml1, p10i = pl.pallas_call(
        second_kernel,
        out_shape=FACTOR + [shape(NB, 2 * RANK, BF16)],
        in_specs=[SMEM] + [ANY] * 4,
        out_specs=[VMEM] * 5,
        scratch_shapes=[
            pltpu.VMEM((NB, TILE1 + 2 * RANK), BF16),
            pltpu.VMEM((NB, NB), BF16),
            pltpu.VMEM((NB, BLK), BF16),
            pltpu.VMEM((NB, BLK), BF16),
            pltpu.VMEM((NB, NB), F32),
            pltpu.VMEM((NB, 2 * RANK), F32),
            pltpu.VMEM((BLK, BLK), F32),
            pltpu.SemaphoreType.DMA((4,)),
        ],
        compiler_params=grant(56),
        name="factor_second",
    )(place, tile, lb0, mh0, ml0)
    new, upd = pl.pallas_call(
        last_kernel,
        out_shape=[shape(64, NB, F32), shape(NB, 3 * RANK, BF16)],
        in_specs=[SMEM] + [ANY] * 15,
        out_specs=[VMEM] * 2,
        scratch_shapes=[
            pltpu.VMEM((NB, 2 * RANK), BF16),
            pltpu.VMEM((NB, 4 * RANK), BF16),
            pltpu.VMEM((NB, RANK), BF16),
            pltpu.VMEM((NB, 2 * RANK), BF16),
            pltpu.VMEM((64, NB), F32),
            pltpu.VMEM((64, NB), F32),
            pltpu.VMEM((64, NB), F32),
            pltpu.VMEM((NB, NB), BF16),
            pltpu.VMEM((NB, BLK), BF16),
            pltpu.VMEM((NB, BLK), BF16),
            pltpu.VMEM((NB, NB), BF16),
            pltpu.VMEM((NB, BLK), BF16),
            pltpu.VMEM((NB, BLK), BF16),
            pltpu.VMEM((NB, RANK), F32),
            pltpu.VMEM((NB, 3 * RANK), F32),
            pltpu.VMEM((NB, RANK), BF16),
            pltpu.VMEM((NB, 3 * RANK), BF16),
            pltpu.SemaphoreType.DMA((28,)),
        ],
        compiler_params=grant(56),
        name="finish",
    )(place, *parts, tile, p10i, mine, lrow0, lrow1, lb0, mh0, ml0, lb1, mh1, ml1)
    return new[None, None], upd[None, None, None, None]


def solution(mesh):
    in_specs = (
        P(None, "row", "col", None),
        P(None, "row", None, "col", None, None),
        P(None, "row", None, "col", None, None),
        P(None, "row", None, "col"),
    )
    out_specs = (P(None, "row", "col", None), P(None, "row", None, "col", None, None))
    return jax.shard_map(shards, mesh=mesh, in_specs=in_specs, out_specs=out_specs, check_vma=False)
```

```python
import functools

import jax
import jax.numpy as jnp
from jax import lax
from jax.experimental import pallas as pl
from jax.experimental.pallas import tpu as pltpu
from jax.sharding import PartitionSpec as P

F32 = jnp.float32
BF16 = jnp.bfloat16
NB = 1024
RANK = 256
BLK = 128
NBLK = NB // BLK
BAND = 5 * BLK
SPAN = 4
TILE1 = 2 * BAND + 2 * RANK
TN = (((0,), (0,)), ((), ()))
NT = (((1,), (1,)), ((), ()))
VMEM = pl.BlockSpec(memory_space=pltpu.VMEM)
SMEM = pl.BlockSpec(memory_space=pltpu.SMEM)
ANY = pl.BlockSpec(memory_space=pl.ANY)


def grant(mib):
    return pltpu.CompilerParams(vmem_limit_bytes=mib * 1024 * 1024)


def lanes_of(x, c):
    return jnp.broadcast_to(x[:, c : c + 1], (8, BLK))


def rows_of(x, r):
    return jnp.broadcast_to(x[r : r + 1, :], (8, BLK))


def factor_block(rows):
    sub = lax.broadcasted_iota(jnp.int32, (8, BLK), 0)
    lane = lax.broadcasted_iota(jnp.int32, (8, BLK), 1)
    a = list(rows)
    n = len(a)
    up, inv, wide = [], [], []
    cols = [lanes_of(a[0], m) for m in range(8)]
    for g in range(n):
        c0 = 8 * g
        near = min(n, g // SPAN * SPAN + 2 * SPAN)
        here = (lane >= c0) & (lane < c0 + 8)
        left = [[lanes_of(a[b], c0 + m) for m in range(8)] for b in range(g + 1, near)]
        ahead = [lanes_of(a[g + 1], c0 + 8 + m) for m in range(8)] if g + 1 < n else None
        mult, recip, piv = [], [], None
        for k in range(8):
            d = rows_of(cols[k], k)
            r = 1.0 / d
            recip.append(r)
            piv = d if piv is None else jnp.where(sub == k, d, piv)
            for m in range(k + 1, 8):
                cols[m] = cols[m] - (cols[k] * rows_of(cols[k], m)) * r
            mult.append(jnp.where(sub > k, cols[k] * r, 0.0))
        s = jnp.where(here, jnp.where(lane == c0 + sub, 1.0, 0.0), a[g])
        s2 = a[g]
        for k in range(7):
            s = s - mult[k] * rows_of(s, k)
            s2 = s2 - mult[k] * rows_of(s2, k)
        root = lax.rsqrt(piv)
        r_ = s * root
        t = r_ * root
        diag = jnp.where(lane >= c0 + sub, s2 * root, 0.0)
        up.append(jnp.where(here, diag, jnp.where(lane >= c0 + 8, r_, 0.0)))
        inv.append(jnp.where(lane < c0 + 8, r_, 0.0))
        if g + 1 == n:
            break
        mk = [[rows_of(mult[k], m) if m > k else None for m in range(8)] for k in range(8)]
        tk = [rows_of(t, k) for k in range(8)]
        for b in range(g + 1, near):
            x = left[b - g - 1]
            for k in range(8):
                for m in range(k + 1, 8):
                    x[m] = x[m] - x[k] * mk[k][m]
            if b == g + 1:
                cols = ahead
                for k in range(8):
                    xs = x[k] * recip[k]
                    for m in range(8):
                        cols[m] = cols[m] - x[k] * rows_of(xs, m)
            new = jnp.where(here, 0.0, a[b])
            for k in range(8):
                new = new - x[k] * tk[k]
            a[b] = new
        wide.append(jnp.where((lane >= c0 + 8) & (lane < 8 * (g // SPAN * SPAN + SPAN)), 0.0, r_))
        if (g + 1) % SPAN == 0 and near < n:
            hi, lo = split(jnp.concatenate(wide, axis=0))
            wide = []
            both = tn32(hi, hi) + (tn32(hi, lo) + tn32(lo, hi))
            done = (lane >= c0 + 8 - 8 * SPAN) & (lane < c0 + 8)
            for b in range(near, n):
                a[b] = jnp.where(done, 0.0, a[b]) - both[8 * b : 8 * b + 8]
    return up, inv


def split(x):
    hi = x.astype(BF16)
    return hi, (x - hi.astype(F32)).astype(BF16)


def tn32(a, b):
    return lax.dot_general(a, b, TN, preferred_element_type=F32)


def tn(a, b):
    return tn32(a, b).astype(BF16)


def mm(a, b):
    return jnp.dot(a, b, preferred_element_type=F32)


def mm3(a, b):
    return mm(a[0], b[0]) + (mm(a[0], b[1]) + mm(a[1], b[0]))


def unfold(work, take):
    for r in range(NBLK):
        n = min(5, NBLK - r)
        rows = slice(r * BLK, (r + 1) * BLK)
        work[rows, r * BLK : (r + n) * BLK] = take(r, slice(0, n * BLK))
        for c in range(r + 5, NBLK):
            o = (NBLK - (c - r)) * BLK
            work[rows, c * BLK : (c + 1) * BLK] = take(c, slice(o, o + BLK)).T


def cholesky_blocks(work, lb, mh, ml, inv_s):
    def body(k, _):
        off = pl.multiple_of(k * BLK, BLK)
        rows = [work[pl.ds(pl.multiple_of(off + 8 * i, 8), 8), pl.ds(off, BLK)] for i in range(16)]
        up, inv = factor_block(rows)
        for i in range(16):
            inv_s[8 * i : 8 * i + 8, :] = inv[i]
        work[pl.ds(off, BLK), pl.ds(off, BLK)] = jnp.concatenate(up, axis=0).T
        hi, lo = split(inv_s[...])
        mh[pl.ds(off, BLK), :] = hi
        ml[pl.ds(off, BLK), :] = lo
        for kk in range(NBLK - 1):

            @pl.when(k == kk)
            def _():
                o = BLK * kk
                e = o + BLK
                upper = mm3((hi, lo), split(work[o:e, e:]))
                parts = split(upper)
                for ib in range(kk + 1, NBLK):
                    i0 = BLK * ib
                    c = i0 - e
                    low = upper[:, c : c + BLK].T
                    lows = split(low)
                    lb[i0 : i0 + BLK, o:e] = lows[0]
                    work[i0 : i0 + BLK, o:e] = low
                    work[i0 : i0 + BLK, i0:] = work[i0 : i0 + BLK, i0:] - mm3(
                        lows, (parts[0][:, c:], parts[1][:, c:])
                    )

        return 0

    lax.fori_loop(0, NBLK, body, 0)


def write_rows(place, work, lrow):
    start = pl.multiple_of(64 * (2 * place[0] + place[1]), 64)
    r = lax.broadcasted_iota(jnp.int32, (64, NB), 0) + start
    c = lax.broadcasted_iota(jnp.int32, (64, NB), 1)
    lrow[...] = jnp.where(c <= r, work[pl.ds(start, 64), :], 0.0)


def fetch(pairs, sems):
    copies = [pltpu.make_async_copy(src, dst, sems.at[n]) for n, (src, dst) in enumerate(pairs)]
    for one in copies:
        one.start()
    return copies


def first_kernel(place, raw_h, lrow, lb, mh, ml, raw, work, inv_s, sems):
    for one in fetch([(raw_h, raw)], sems):
        one.wait()
    unfold(work, lambda r, cols: raw[r * BLK : (r + 1) * BLK, cols])
    cholesky_blocks(work, lb, mh, ml, inv_s)
    write_rows(place, work, lrow)


def solve_step(k, w, lb, mh, ml, p):
    o = BLK * k
    e = o + BLK
    x = mm3((mh[o:e, :], ml[o:e, :]), split(w[o:e, :]))
    p[o:e, :] = x.astype(BF16)
    if e < NB:
        xs = split(x)
        low = lb[e:, o:e]
        w[e:, :] = w[e:, :] - (mm(low, xs[0]) + mm(low, xs[1]))


def second_kernel(
    place, tile_h, lb0_h, mh0_h, ml0_h, lrow, lb, mh, ml, p10, tile, lb0, mh0, ml0, work, w, inv_s, sems
):
    diag, factors = pl.ds(0, 2 * BAND), pl.ds(2 * BAND, 4 * RANK)
    copies = fetch(
        [
            (tile_h.at[:, factors], tile.at[:, factors]),
            (mh0_h, mh0),
            (ml0_h, ml0),
            (lb0_h, lb0),
            (tile_h.at[:, diag], tile.at[:, diag]),
        ],
        sems,
    )
    for one in copies[:4]:
        one.wait()
    w[:, :RANK] = tile[:, 2 * BAND + RANK : TILE1].astype(F32)
    w[:, RANK:] = tile[:, TILE1 + RANK : TILE1 + 2 * RANK].astype(F32)
    for k in range(NBLK):
        solve_step(k, w, lb0, mh0, ml0, p10)
    solved = p10[:, :RANK]
    inner = lax.dot_general(solved, solved, TN, preferred_element_type=F32).astype(BF16)
    u = tile[:, 2 * BAND : 2 * BAND + RANK]
    corr = split(mm(u, inner))

    def take(r, cols):
        rows = slice(r * BLK, (r + 1) * BLK)
        return tile[rows, cols].astype(F32) + tile[rows, cols.start + BAND : cols.stop + BAND].astype(F32)

    copies[4].wait()
    unfold(work, take)
    for r in range(NBLK):
        o = r * BLK
        right = u[o:, :]
        work[o : o + BLK, o:] = work[o : o + BLK, o:] - (
            lax.dot_general(corr[0][o : o + BLK], right, NT, preferred_element_type=F32)
            + lax.dot_general(corr[1][o : o + BLK], right, NT, preferred_element_type=F32)
        )
    cholesky_blocks(work, lb, mh, ml, inv_s)
    write_rows(place, work, lrow)


def last_kernel(place, *refs):
    parts, (tile_h, p10i_h, diag_h, lrow0_h, lrow1_h) = refs[:4], refs[4:9]
    lb0_h, mh0_h, ml0_h, lb1_h, mh1_h, ml1_h, new, upd = refs[9:17]
    (cols, rows, u10, p10i, diag, lrow0, lrow1, lb0, mh0, ml0, lb1, mh1, ml1, w0, w1, pj, p1, sems) = refs[17:]
    j = 2 * place[0] + place[1]
    i = place[2]
    x, y = i // 4, lax.rem(i, 4)
    pairs = [(tile_h.at[:, TILE1:], rows), (tile_h.at[:, 2 * BAND : 2 * BAND + RANK], u10)]
    for b in range(4):
        for a in range(4):
            k = 4 * lax.rem(x + 4 - a, 4) + lax.rem(y + 4 - b, 4)
            pairs.append((parts[b].at[pl.ds(64 * a, 64)], cols.at[pl.ds(pl.multiple_of(64 * k, 64), 64)]))
    head = len(pairs)
    pairs += [(mh0_h, mh0), (ml0_h, ml0), (mh1_h, mh1), (ml1_h, ml1), (lb0_h, lb0), (lb1_h, lb1)]
    body = len(pairs)
    pairs += [(p10i_h, p10i), (diag_h, diag), (lrow0_h, lrow0), (lrow1_h, lrow1)]
    copies = fetch(pairs, sems)
    for one in copies[:head]:
        one.wait()
    w0[...] = cols[:, :RANK].astype(F32)
    w1[:, :RANK] = rows[:, 3 * RANK :].astype(F32)
    w1[:, RANK : 2 * RANK] = u10[...].astype(F32)
    w1[:, 2 * RANK :] = cols[:, RANK:].astype(F32)
    for one in copies[head:body]:
        one.wait()
    for k in range(NBLK):
        solve_step(k, w0, lb0, mh0, ml0, pj)
        solve_step(k, w1, lb1, mh1, ml1, p1)
    for one in copies[body:]:
        one.wait()
    zero = jnp.zeros((), BF16)
    pi = jnp.where(i > 0, p10i[:, RANK:], zero)
    ui = rows[:, :RANK]
    start = pl.multiple_of(64 * j, 64)
    ui_part = rows[pl.ds(start, 64), :RANK]
    inner01 = tn(pi, p10i[:, :RANK])
    c0 = mm(ui, tn(pi, pj[...])).astype(BF16)
    c01 = mm(ui, inner01).astype(BF16)
    c0_part = mm(ui_part, tn(pi, pi)).astype(BF16)
    d = diag[...] - lax.dot_general(c0_part, ui, NT, preferred_element_type=F32)
    upd[:, :RANK] = jnp.where(j == 0, pi, jnp.where((i > j) & (j > 0), c0, zero))
    q = jnp.where(i > 1, p1[...], zero)
    q_i = q[:, : 2 * RANK]
    square = tn(q_i, q_i)
    inner = jnp.concatenate([tn(q_i, q[:, 2 * RANK :]), square[:, RANK:]], axis=1)
    up = jnp.concatenate([rows[:, 2 * RANK : 3 * RANK], -c01], axis=1)
    c1 = mm(up, inner).astype(BF16)
    up_part = jnp.concatenate(
        [rows[pl.ds(start, 64), 2 * RANK : 3 * RANK], -mm(ui_part, inner01).astype(BF16)], axis=1
    )
    c1_part = mm(up_part, square).astype(BF16)
    d = d - lax.dot_general(c1_part, up, NT, preferred_element_type=F32)
    new[...] = jnp.where(i == 0, lrow0[...], jnp.where(i == 1, lrow1[...], d))
    upd[:, RANK:] = jnp.where(j == 1, q_i, jnp.where((i > j) & (j > 1), c1, zero))


def shape(rows, cols, dtype):
    return jax.ShapeDtypeStruct((rows, cols), dtype)


FACTOR = [shape(64, NB, F32), shape(NB, NB, BF16), shape(NB, BLK, BF16), shape(NB, BLK, BF16)]


def swap_core(x):
    return lax.ppermute(x, "col", [(c, c ^ 1) for c in range(16)])


def after(x, *tokens):
    return lax.optimization_barrier((x, *tokens))[0]


def at(row, col):
    return 16 * row + col


def pick(cases, default):
    for hit, x in cases:
        default = jnp.where(hit, x, default)
    return default


def spread_x(x, row_at, rows):
    got = [lax.ppermute(x, "row", [(y, 4 * k + y) for y in rows]) for k in (1, 2, 3)]
    return pick([(row_at // 4 == k, got[k - 1]) for k in (1, 2, 3)], x)


def spread_y(x, row_at, rows):
    got = [lax.ppermute(x, "row", [(4 * a + y, 4 * a + (y + s) % 4) for a in range(4) for y in rows]) for s in (1, 2, 3)]
    return [pick([(row_at % 4 == (y + s) % 4, got[s - 1]) for s in (1, 2, 3)], x) for y in rows]


def halve(x, z, gap):
    half = x.shape[0] // 2
    pairs = [(2 * a + c, 2 * (a + gap) + c) for a in range(0, 8, 2 * gap) for c in (0, 1)]
    got = lax.ppermute(x[half:], "col", pairs)
    return jnp.where((z // gap) % 2 == 1, got, x[:half])


def deal(cur, z, core, tokens):
    first = core == 0

    def chunk(q0, q1):
        return jnp.where(first, cur[64 * q0 : 64 * q0 + 64], cur[64 * q1 : 64 * q1 + 64])

    def send(x, step, flip):
        pairs = [(2 * a + c, 2 * (a + step) + (c ^ flip)) for a in range(0, 8, 2) for c in (0, 1)]
        return lax.ppermute(after(x, *tokens), "col", pairs)

    odd = z % 2 == 1
    same = jnp.where(odd, send(chunk(2, 3), 1, 0), chunk(0, 1))
    cross = jnp.where(odd, send(chunk(3, 2), 1, 1), send(chunk(1, 0), 0, 1))
    return jnp.where(first, same, cross), jnp.where(first, cross, same)


def shards(diag_tiles, left_factors, right_factors, ranks):
    row_at = lax.axis_index("row")
    col_at = lax.axis_index("col")
    z, core = col_at // 2, col_at % 2
    place = jnp.stack([z, core, row_at]).astype(jnp.int32)
    mine = diag_tiles[0, 0]
    keep = jnp.arange(RANK)[None, :] < ranks[0, 0, 0, 0]
    zero = jnp.zeros((), BF16)
    both = jnp.concatenate(
        [jnp.where(keep, left_factors[0, 0, 0, 0], zero), jnp.where(keep, right_factors[0, 0, 0, 0], zero)], axis=1
    )

    band = lax.dynamic_slice(jnp.concatenate([mine, mine[:, :BAND]], axis=1), (0, BLK * z), (64, BAND))
    half = halve(both, z, 4)
    band0, band1 = spread_y(spread_x(band, row_at, (0, 1)), row_at, (0, 1))
    band0, half = lax.optimization_barrier((band0, half))
    raw0 = lax.all_gather(band0, "col", tiled=True)

    part0, part1 = deal(halve(half, z, 2), z, core, ())
    (first,) = spread_y(spread_x(part0, row_at, (1,)), row_at, (1,))
    hi, lo = split(band1)
    tile = lax.all_gather(jnp.concatenate([hi, lo, first, part0, part1], axis=1), "col", tiled=True)
    flip = lax.ppermute(
        after(jnp.concatenate([part0[:, RANK:], part1[:, RANK:]], axis=1), first),
        ("row", "col"),
        [(at(r, c), at(c, r)) for r in range(16) for c in range(16)],
    )

    lrow0, lb0, mh0, ml0 = pl.pallas_call(
        first_kernel,
        out_shape=FACTOR,
        in_specs=[SMEM, ANY],
        out_specs=[VMEM] * 4,
        scratch_shapes=[
            pltpu.VMEM((NB, BAND), F32),
            pltpu.VMEM((NB, NB), F32),
            pltpu.VMEM((BLK, BLK), F32),
            pltpu.SemaphoreType.DMA((1,)),
        ],
        compiler_params=grant(56),
        name="factor_first",
    )(place, raw0)

    flip = after(flip, mh0)
    over_x = [
        lax.ppermute(flip, "row", [(4 * a + b, 4 * ((a + s) % 4) + b) for a in range(4) for b in range(4)])
        for s in (1, 2, 3)
    ]
    parts = [jnp.concatenate([flip, *over_x], axis=0)]
    for s in (1, 2, 3):
        parts.append(
            lax.ppermute(parts[0], "row", [(4 * a + b, 4 * a + (b + s) % 4) for a in range(4) for b in range(4)])
        )

    lrow1, lb1, mh1, ml1, p10i = pl.pallas_call(
        second_kernel,
        out_shape=FACTOR + [shape(NB, 2 * RANK, BF16)],
        in_specs=[SMEM] + [ANY] * 4,
        out_specs=[VMEM] * 5,
        scratch_shapes=[
            pltpu.VMEM((NB, TILE1 + 2 * RANK), BF16),
            pltpu.VMEM((NB, NB), BF16),
            pltpu.VMEM((NB, BLK), BF16),
            pltpu.VMEM((NB, BLK), BF16),
            pltpu.VMEM((NB, NB), F32),
            pltpu.VMEM((NB, 2 * RANK), F32),
            pltpu.VMEM((BLK, BLK), F32),
            pltpu.SemaphoreType.DMA((5,)),
        ],
        compiler_params=grant(56),
        name="factor_second",
    )(place, tile, lb0, mh0, ml0)
    new, upd = pl.pallas_call(
        last_kernel,
        out_shape=[shape(64, NB, F32), shape(NB, 3 * RANK, BF16)],
        in_specs=[SMEM] + [ANY] * 15,
        out_specs=[VMEM] * 2,
        scratch_shapes=[
            pltpu.VMEM((NB, 2 * RANK), BF16),
            pltpu.VMEM((NB, 4 * RANK), BF16),
            pltpu.VMEM((NB, RANK), BF16),
            pltpu.VMEM((NB, 2 * RANK), BF16),
            pltpu.VMEM((64, NB), F32),
            pltpu.VMEM((64, NB), F32),
            pltpu.VMEM((64, NB), F32),
            pltpu.VMEM((NB, NB), BF16),
            pltpu.VMEM((NB, BLK), BF16),
            pltpu.VMEM((NB, BLK), BF16),
            pltpu.VMEM((NB, NB), BF16),
            pltpu.VMEM((NB, BLK), BF16),
            pltpu.VMEM((NB, BLK), BF16),
            pltpu.VMEM((NB, RANK), F32),
            pltpu.VMEM((NB, 3 * RANK), F32),
            pltpu.VMEM((NB, RANK), BF16),
            pltpu.VMEM((NB, 3 * RANK), BF16),
            pltpu.SemaphoreType.DMA((28,)),
        ],
        compiler_params=grant(56),
        name="finish",
    )(place, *parts, tile, p10i, mine, lrow0, lrow1, lb0, mh0, ml0, lb1, mh1, ml1)
    return new[None, None], upd[None, None, None, None]


def solution(mesh):
    in_specs = (
        P(None, "row", "col", None),
        P(None, "row", None, "col", None, None),
        P(None, "row", None, "col", None, None),
        P(None, "row", None, "col"),
    )
    out_specs = (P(None, "row", "col", None), P(None, "row", None, "col", None, None))
    return jax.shard_map(shards, mesh=mesh, in_specs=in_specs, out_specs=out_specs, check_vma=False)
```

```python
import functools

import jax
import jax.numpy as jnp
from jax import lax
from jax.experimental import pallas as pl
from jax.experimental.pallas import tpu as pltpu
from jax.sharding import PartitionSpec as P

F32 = jnp.float32
BF16 = jnp.bfloat16
NB = 1024
RANK = 256
BLK = 128
NBLK = NB // BLK
BAND = 5 * BLK
SPAN = 4
BELOW = range(1, 16)
TILE1 = 2 * BAND + 2 * RANK
TN = (((0,), (0,)), ((), ()))
NT = (((1,), (1,)), ((), ()))
VMEM = pl.BlockSpec(memory_space=pltpu.VMEM)
SMEM = pl.BlockSpec(memory_space=pltpu.SMEM)
ANY = pl.BlockSpec(memory_space=pl.ANY)


def grant(mib):
    return pltpu.CompilerParams(vmem_limit_bytes=mib * 1024 * 1024)


def lanes_of(x, c):
    return jnp.broadcast_to(x[:, c : c + 1], (8, BLK))


def rows_of(x, r):
    return jnp.broadcast_to(x[r : r + 1, :], (8, BLK))


def factor_block(rows):
    sub = lax.broadcasted_iota(jnp.int32, (8, BLK), 0)
    lane = lax.broadcasted_iota(jnp.int32, (8, BLK), 1)
    a = list(rows)
    n = len(a)
    up, inv, wide = [], [], []
    cols = [lanes_of(a[0], m) for m in range(8)]
    for g in range(n):
        c0 = 8 * g
        near = min(n, g // SPAN * SPAN + 2 * SPAN)
        here = (lane >= c0) & (lane < c0 + 8)
        left = [[lanes_of(a[b], c0 + m) for m in range(8)] for b in range(g + 1, near)]
        ahead = [lanes_of(a[g + 1], c0 + 8 + m) for m in range(8)] if g + 1 < n else None
        mult, recip, piv = [], [], None
        for k in range(8):
            d = rows_of(cols[k], k)
            r = 1.0 / d
            recip.append(r)
            piv = d if piv is None else jnp.where(sub == k, d, piv)
            for m in range(k + 1, 8):
                cols[m] = cols[m] - (cols[k] * rows_of(cols[k], m)) * r
            mult.append(jnp.where(sub > k, cols[k] * r, 0.0))
        s = jnp.where(here, jnp.where(lane == c0 + sub, 1.0, 0.0), a[g])
        s2 = a[g]
        for k in range(7):
            s = s - mult[k] * rows_of(s, k)
            s2 = s2 - mult[k] * rows_of(s2, k)
        root = lax.rsqrt(piv)
        r_ = s * root
        t = r_ * root
        diag = jnp.where(lane >= c0 + sub, s2 * root, 0.0)
        up.append(jnp.where(here, diag, jnp.where(lane >= c0 + 8, r_, 0.0)))
        inv.append(jnp.where(lane < c0 + 8, r_, 0.0))
        if g + 1 == n:
            break
        mk = [[rows_of(mult[k], m) if m > k else None for m in range(8)] for k in range(8)]
        tk = [rows_of(t, k) for k in range(8)]
        for b in range(g + 1, near):
            x = left[b - g - 1]
            for k in range(8):
                for m in range(k + 1, 8):
                    x[m] = x[m] - x[k] * mk[k][m]
            if b == g + 1:
                cols = ahead
                for k in range(8):
                    xs = x[k] * recip[k]
                    for m in range(8):
                        cols[m] = cols[m] - x[k] * rows_of(xs, m)
            new = jnp.where(here, 0.0, a[b])
            for k in range(8):
                new = new - x[k] * tk[k]
            a[b] = new
        wide.append(jnp.where((lane >= c0 + 8) & (lane < 8 * (g // SPAN * SPAN + SPAN)), 0.0, r_))
        if (g + 1) % SPAN == 0 and near < n:
            hi, lo = split(jnp.concatenate(wide, axis=0))
            wide = []
            both = tn32(hi, hi) + (tn32(hi, lo) + tn32(lo, hi))
            done = (lane >= c0 + 8 - 8 * SPAN) & (lane < c0 + 8)
            for b in range(near, n):
                a[b] = jnp.where(done, 0.0, a[b]) - both[8 * b : 8 * b + 8]
    return up, inv


def split(x):
    hi = x.astype(BF16)
    return hi, (x - hi.astype(F32)).astype(BF16)


def tn32(a, b):
    return lax.dot_general(a, b, TN, preferred_element_type=F32)


def tn(a, b):
    return tn32(a, b).astype(BF16)


def mm(a, b):
    return jnp.dot(a, b, preferred_element_type=F32)


def mm3(a, b):
    return mm(a[0], b[0]) + (mm(a[0], b[1]) + mm(a[1], b[0]))


def unfold(work, take):
    for r in range(NBLK):
        n = min(5, NBLK - r)
        rows = slice(r * BLK, (r + 1) * BLK)
        work[rows, r * BLK : (r + n) * BLK] = take(r, slice(0, n * BLK))
        for c in range(r + 5, NBLK):
            o = (NBLK - (c - r)) * BLK
            work[rows, c * BLK : (c + 1) * BLK] = take(c, slice(o, o + BLK)).T


def cholesky_blocks(work, lb, mh, ml, inv_s):
    def body(k, _):
        off = pl.multiple_of(k * BLK, BLK)
        rows = [work[pl.ds(pl.multiple_of(off + 8 * i, 8), 8), pl.ds(off, BLK)] for i in range(16)]
        up, inv = factor_block(rows)
        for i in range(16):
            inv_s[8 * i : 8 * i + 8, :] = inv[i]
        work[pl.ds(off, BLK), pl.ds(off, BLK)] = jnp.concatenate(up, axis=0).T
        hi, lo = split(inv_s[...])
        mh[pl.ds(off, BLK), :] = hi
        ml[pl.ds(off, BLK), :] = lo
        for kk in range(NBLK - 1):

            @pl.when(k == kk)
            def _():
                o = BLK * kk
                e = o + BLK
                upper = mm3((hi, lo), split(work[o:e, e:]))
                parts = split(upper)
                for ib in range(kk + 1, NBLK):
                    i0 = BLK * ib
                    c = i0 - e
                    low = upper[:, c : c + BLK].T
                    lows = split(low)
                    lb[i0 : i0 + BLK, o:e] = lows[0]
                    work[i0 : i0 + BLK, o:e] = low
                    work[i0 : i0 + BLK, i0:] = work[i0 : i0 + BLK, i0:] - mm3(
                        lows, (parts[0][:, c:], parts[1][:, c:])
                    )

        return 0

    lax.fori_loop(0, NBLK, body, 0)


def write_rows(place, work, lrow):
    start = pl.multiple_of(64 * (2 * place[0] + place[1]), 64)
    r = lax.broadcasted_iota(jnp.int32, (64, NB), 0) + start
    c = lax.broadcasted_iota(jnp.int32, (64, NB), 1)
    lrow[...] = jnp.where(c <= r, work[pl.ds(start, 64), :], 0.0)


def fetch(pairs, sems):
    copies = [pltpu.make_async_copy(src, dst, sems.at[n]) for n, (src, dst) in enumerate(pairs)]
    for one in copies:
        one.start()
    return copies


def first_kernel(place, raw_h, lrow, lb, mh, ml, raw, work, inv_s, sems):
    for one in fetch([(raw_h, raw)], sems):
        one.wait()
    unfold(work, lambda r, cols: raw[r * BLK : (r + 1) * BLK, cols])
    cholesky_blocks(work, lb, mh, ml, inv_s)
    write_rows(place, work, lrow)


def solve_step(k, w, lb, mh, ml, p):
    o = BLK * k
    e = o + BLK
    x = mm3((mh[o:e, :], ml[o:e, :]), split(w[o:e, :]))
    p[o:e, :] = x.astype(BF16)
    if e < NB:
        xs = split(x)
        low = lb[e:, o:e]
        w[e:, :] = w[e:, :] - (mm(low, xs[0]) + mm(low, xs[1]))


def second_kernel(
    place, tile_h, lb0_h, mh0_h, ml0_h, lrow, lb, mh, ml, p10, tile, lb0, mh0, ml0, work, w, inv_s, sems
):
    diag, factors = pl.ds(0, 2 * BAND), pl.ds(2 * BAND, 4 * RANK)
    copies = fetch(
        [
            (tile_h.at[:, factors], tile.at[:, factors]),
            (mh0_h, mh0),
            (ml0_h, ml0),
            (lb0_h, lb0),
            (tile_h.at[:, diag], tile.at[:, diag]),
        ],
        sems,
    )
    for one in copies[:4]:
        one.wait()
    w[:, :RANK] = tile[:, 2 * BAND + RANK : TILE1].astype(F32)
    w[:, RANK:] = tile[:, TILE1 + RANK : TILE1 + 2 * RANK].astype(F32)
    for k in range(NBLK):
        solve_step(k, w, lb0, mh0, ml0, p10)
    solved = p10[:, :RANK]
    inner = lax.dot_general(solved, solved, TN, preferred_element_type=F32).astype(BF16)
    u = tile[:, 2 * BAND : 2 * BAND + RANK]
    corr = split(mm(u, inner))

    def take(r, cols):
        rows = slice(r * BLK, (r + 1) * BLK)
        return tile[rows, cols].astype(F32) + tile[rows, cols.start + BAND : cols.stop + BAND].astype(F32)

    copies[4].wait()
    unfold(work, take)
    for r in range(NBLK):
        o = r * BLK
        right = u[o:, :]
        work[o : o + BLK, o:] = work[o : o + BLK, o:] - (
            lax.dot_general(corr[0][o : o + BLK], right, NT, preferred_element_type=F32)
            + lax.dot_general(corr[1][o : o + BLK], right, NT, preferred_element_type=F32)
        )
    cholesky_blocks(work, lb, mh, ml, inv_s)
    write_rows(place, work, lrow)


def last_kernel(place, *refs):
    parts, (tile_h, p10i_h, diag_h, lrow0_h, lrow1_h) = refs[:4], refs[4:9]
    lb0_h, mh0_h, ml0_h, lb1_h, mh1_h, ml1_h, new, upd = refs[9:17]
    (cols, rows, u10, p10i, diag, lrow0, lrow1, lb0, mh0, ml0, lb1, mh1, ml1, w0, w1, pj, p1, sems) = refs[17:]
    j = 2 * place[0] + place[1]
    i = place[2]
    x, y = i // 4, lax.rem(i, 4)
    pairs = [(tile_h.at[:, TILE1:], rows), (tile_h.at[:, 2 * BAND : 2 * BAND + RANK], u10)]
    for b in range(4):
        for a in range(4):
            k = 4 * lax.rem(x + 4 - a, 4) + lax.rem(y + 4 - b, 4)
            pairs.append((parts[b].at[pl.ds(64 * a, 64)], cols.at[pl.ds(pl.multiple_of(64 * k, 64), 64)]))
    head = len(pairs)
    pairs += [(mh0_h, mh0), (ml0_h, ml0), (mh1_h, mh1), (ml1_h, ml1), (lb0_h, lb0), (lb1_h, lb1)]
    body = len(pairs)
    pairs += [(p10i_h, p10i), (diag_h, diag), (lrow0_h, lrow0), (lrow1_h, lrow1)]
    copies = fetch(pairs, sems)
    for one in copies[:head]:
        one.wait()
    w0[...] = cols[:, :RANK].astype(F32)
    w1[:, :RANK] = rows[:, 3 * RANK :].astype(F32)
    w1[:, RANK : 2 * RANK] = u10[...].astype(F32)
    w1[:, 2 * RANK :] = cols[:, RANK:].astype(F32)
    for one in copies[head:body]:
        one.wait()
    for k in range(NBLK):
        solve_step(k, w0, lb0, mh0, ml0, pj)
        solve_step(k, w1, lb1, mh1, ml1, p1)
    for one in copies[body:]:
        one.wait()
    zero = jnp.zeros((), BF16)
    pi = jnp.where(i > 0, p10i[:, RANK:], zero)
    ui = rows[:, :RANK]
    start = pl.multiple_of(64 * j, 64)
    ui_part = rows[pl.ds(start, 64), :RANK]
    inner01 = tn(pi, p10i[:, :RANK])
    c0 = mm(ui, tn(pi, pj[...])).astype(BF16)
    c01 = mm(ui, inner01).astype(BF16)
    c0_part = mm(ui_part, tn(pi, pi)).astype(BF16)
    d = diag[...] - lax.dot_general(c0_part, ui, NT, preferred_element_type=F32)
    upd[:, :RANK] = jnp.where(j == 0, pi, jnp.where((i > j) & (j > 0), c0, zero))
    q = jnp.where(i > 1, p1[...], zero)
    q_i = q[:, : 2 * RANK]
    square = tn(q_i, q_i)
    inner = jnp.concatenate([tn(q_i, q[:, 2 * RANK :]), square[:, RANK:]], axis=1)
    up = jnp.concatenate([rows[:, 2 * RANK : 3 * RANK], -c01], axis=1)
    c1 = mm(up, inner).astype(BF16)
    up_part = jnp.concatenate(
        [rows[pl.ds(start, 64), 2 * RANK : 3 * RANK], -mm(ui_part, inner01).astype(BF16)], axis=1
    )
    c1_part = mm(up_part, square).astype(BF16)
    d = d - lax.dot_general(c1_part, up, NT, preferred_element_type=F32)
    new[...] = jnp.where(i == 0, lrow0[...], jnp.where(i == 1, lrow1[...], d))
    upd[:, RANK:] = jnp.where(j == 1, q_i, jnp.where((i > j) & (j > 1), c1, zero))


def shape(rows, cols, dtype):
    return jax.ShapeDtypeStruct((rows, cols), dtype)


FACTOR = [shape(64, NB, F32), shape(NB, NB, BF16), shape(NB, BLK, BF16), shape(NB, BLK, BF16)]


def swap_core(x):
    return lax.ppermute(x, "col", [(c, c ^ 1) for c in range(16)])


def after(x, *tokens):
    return lax.optimization_barrier((x, *tokens))[0]


def at(row, col):
    return 16 * row + col


def pick(cases, default):
    for hit, x in cases:
        default = jnp.where(hit, x, default)
    return default


def spread_x(x, row_at, rows):
    got = [lax.ppermute(x, "row", [(y, 4 * k + y) for y in rows]) for k in (1, 2, 3)]
    return pick([(row_at // 4 == k, got[k - 1]) for k in (1, 2, 3)], x)


def spread_y(x, row_at, rows):
    got = [lax.ppermute(x, "row", [(4 * a + y, 4 * a + (y + s) % 4) for a in range(4) for y in rows]) for s in (1, 2, 3)]
    return [pick([(row_at % 4 == (y + s) % 4, got[s - 1]) for s in (1, 2, 3)], x) for y in rows]


def halve(x, z, gap):
    half = x.shape[0] // 2
    pairs = [(at(r, 2 * a + c), at(r, 2 * (a + gap) + c)) for r in BELOW for a in range(0, 8, 2 * gap) for c in (0, 1)]
    got = lax.ppermute(x[half:], ("row", "col"), pairs)
    return jnp.where((z // gap) % 2 == 1, got, x[:half])


def deal(cur, z, core, tokens):
    first = core == 0

    def chunk(q0, q1):
        return jnp.where(first, cur[64 * q0 : 64 * q0 + 64], cur[64 * q1 : 64 * q1 + 64])

    def send(x, step, flip):
        pairs = [
            (at(r, 2 * a + c), at(r, 2 * (a + step) + (c ^ flip))) for r in BELOW for a in range(0, 8, 2) for c in (0, 1)
        ]
        return lax.ppermute(after(x, *tokens) if tokens else x, ("row", "col"), pairs)

    odd = z % 2 == 1
    same = jnp.where(odd, send(chunk(2, 3), 1, 0), chunk(0, 1))
    cross = jnp.where(odd, send(chunk(3, 2), 1, 1), send(chunk(1, 0), 0, 1))
    return jnp.where(first, same, cross), jnp.where(first, cross, same)


def shards(diag_tiles, left_factors, right_factors, ranks):
    row_at = lax.axis_index("row")
    col_at = lax.axis_index("col")
    z, core = col_at // 2, col_at % 2
    place = jnp.stack([z, core, row_at]).astype(jnp.int32)
    mine = diag_tiles[0, 0]
    keep = jnp.arange(RANK)[None, :] < ranks[0, 0, 0, 0]
    zero = jnp.zeros((), BF16)
    both = jnp.concatenate(
        [jnp.where(keep, left_factors[0, 0, 0, 0], zero), jnp.where(keep, right_factors[0, 0, 0, 0], zero)], axis=1
    )

    band = lax.dynamic_slice(jnp.concatenate([mine, mine[:, :BAND]], axis=1), (0, BLK * z), (64, BAND))
    half = halve(both, z, 4)
    (band0,) = spread_y(spread_x(band, row_at, (0,)), row_at, (0,))
    band0, half = lax.optimization_barrier((band0, half))
    raw0 = lax.all_gather(band0, "col", tiled=True)

    quarter = halve(half, z, 2)
    part0, part1 = deal(quarter, z, core, ())
    way1, part0, part1 = lax.optimization_barrier((spread_x(after(band, quarter), row_at, (1,)), part0, part1))
    (band1,) = spread_y(way1, row_at, (1,))
    first, band1 = lax.optimization_barrier((spread_x(part0, row_at, (1,)), band1))
    (first,) = spread_y(first, row_at, (1,))
    hi, lo = split(band1)
    tile = lax.all_gather(jnp.concatenate([hi, lo, first, part0, part1], axis=1), "col", tiled=True)
    flip = lax.ppermute(
        after(jnp.concatenate([part0[:, RANK:], part1[:, RANK:]], axis=1), first),
        ("row", "col"),
        [(at(r, c), at(c, r)) for r in range(16) for c in range(16)],
    )

    lrow0, lb0, mh0, ml0 = pl.pallas_call(
        first_kernel,
        out_shape=FACTOR,
        in_specs=[SMEM, ANY],
        out_specs=[VMEM] * 4,
        scratch_shapes=[
            pltpu.VMEM((NB, BAND), F32),
            pltpu.VMEM((NB, NB), F32),
            pltpu.VMEM((BLK, BLK), F32),
            pltpu.SemaphoreType.DMA((1,)),
        ],
        compiler_params=grant(56),
        name="factor_first",
    )(place, raw0)

    flip = after(flip, mh0)
    over_x = [
        lax.ppermute(flip, "row", [(4 * a + b, 4 * ((a + s) % 4) + b) for a in range(4) for b in range(4)])
        for s in (1, 2, 3)
    ]
    parts = [jnp.concatenate([flip, *over_x], axis=0)]
    for s in (1, 2, 3):
        parts.append(
            lax.ppermute(parts[0], "row", [(4 * a + b, 4 * a + (b + s) % 4) for a in range(4) for b in range(4)])
        )

    lrow1, lb1, mh1, ml1, p10i = pl.pallas_call(
        second_kernel,
        out_shape=FACTOR + [shape(NB, 2 * RANK, BF16)],
        in_specs=[SMEM] + [ANY] * 4,
        out_specs=[VMEM] * 5,
        scratch_shapes=[
            pltpu.VMEM((NB, TILE1 + 2 * RANK), BF16),
            pltpu.VMEM((NB, NB), BF16),
            pltpu.VMEM((NB, BLK), BF16),
            pltpu.VMEM((NB, BLK), BF16),
            pltpu.VMEM((NB, NB), F32),
            pltpu.VMEM((NB, 2 * RANK), F32),
            pltpu.VMEM((BLK, BLK), F32),
            pltpu.SemaphoreType.DMA((5,)),
        ],
        compiler_params=grant(56),
        name="factor_second",
    )(place, tile, lb0, mh0, ml0)
    new, upd = pl.pallas_call(
        last_kernel,
        out_shape=[shape(64, NB, F32), shape(NB, 3 * RANK, BF16)],
        in_specs=[SMEM] + [ANY] * 15,
        out_specs=[VMEM] * 2,
        scratch_shapes=[
            pltpu.VMEM((NB, 2 * RANK), BF16),
            pltpu.VMEM((NB, 4 * RANK), BF16),
            pltpu.VMEM((NB, RANK), BF16),
            pltpu.VMEM((NB, 2 * RANK), BF16),
            pltpu.VMEM((64, NB), F32),
            pltpu.VMEM((64, NB), F32),
            pltpu.VMEM((64, NB), F32),
            pltpu.VMEM((NB, NB), BF16),
            pltpu.VMEM((NB, BLK), BF16),
            pltpu.VMEM((NB, BLK), BF16),
            pltpu.VMEM((NB, NB), BF16),
            pltpu.VMEM((NB, BLK), BF16),
            pltpu.VMEM((NB, BLK), BF16),
            pltpu.VMEM((NB, RANK), F32),
            pltpu.VMEM((NB, 3 * RANK), F32),
            pltpu.VMEM((NB, RANK), BF16),
            pltpu.VMEM((NB, 3 * RANK), BF16),
            pltpu.SemaphoreType.DMA((28,)),
        ],
        compiler_params=grant(56),
        name="finish",
    )(place, *parts, tile, p10i, mine, lrow0, lrow1, lb0, mh0, ml0, lb1, mh1, ml1)
    return new[None, None], upd[None, None, None, None]


def solution(mesh):
    in_specs = (
        P(None, "row", "col", None),
        P(None, "row", None, "col", None, None),
        P(None, "row", None, "col", None, None),
        P(None, "row", None, "col"),
    )
    out_specs = (P(None, "row", "col", None), P(None, "row", None, "col", None, None))
    return jax.shard_map(shards, mesh=mesh, in_specs=in_specs, out_specs=out_specs, check_vma=False)
```

```python
import functools

import jax
import jax.numpy as jnp
from jax import lax
from jax.experimental import pallas as pl
from jax.experimental.pallas import tpu as pltpu
from jax.sharding import PartitionSpec as P

F32 = jnp.float32
BF16 = jnp.bfloat16
NB = 1024
RANK = 256
BLK = 128
NBLK = NB // BLK
BAND = 5 * BLK
SPAN = 4
BELOW = range(1, 16)
TILE1 = 2 * BAND + 2 * RANK
TN = (((0,), (0,)), ((), ()))
NT = (((1,), (1,)), ((), ()))
VMEM = pl.BlockSpec(memory_space=pltpu.VMEM)
SMEM = pl.BlockSpec(memory_space=pltpu.SMEM)
ANY = pl.BlockSpec(memory_space=pl.ANY)


def grant(mib):
    return pltpu.CompilerParams(vmem_limit_bytes=mib * 1024 * 1024)


def lanes_of(x, c):
    return jnp.broadcast_to(x[:, c : c + 1], (8, BLK))


def rows_of(x, r):
    return jnp.broadcast_to(x[r : r + 1, :], (8, BLK))


def factor_block(rows):
    sub = lax.broadcasted_iota(jnp.int32, (8, BLK), 0)
    lane = lax.broadcasted_iota(jnp.int32, (8, BLK), 1)
    a = list(rows)
    n = len(a)
    up, inv, wide = [], [], []
    cols = [lanes_of(a[0], m) for m in range(8)]
    for g in range(n):
        c0 = 8 * g
        near = min(n, g // SPAN * SPAN + 2 * SPAN)
        here = (lane >= c0) & (lane < c0 + 8)
        left = [[lanes_of(a[b], c0 + m) for m in range(8)] for b in range(g + 1, near)]
        ahead = [lanes_of(a[g + 1], c0 + 8 + m) for m in range(8)] if g + 1 < n else None
        mult, recip, piv = [], [], None
        for k in range(8):
            d = rows_of(cols[k], k)
            r = 1.0 / d
            recip.append(r)
            piv = d if piv is None else jnp.where(sub == k, d, piv)
            for m in range(k + 1, 8):
                cols[m] = cols[m] - (cols[k] * rows_of(cols[k], m)) * r
            mult.append(jnp.where(sub > k, cols[k] * r, 0.0))
        s = jnp.where(here, jnp.where(lane == c0 + sub, 1.0, 0.0), a[g])
        s2 = a[g]
        for k in range(7):
            s = s - mult[k] * rows_of(s, k)
            s2 = s2 - mult[k] * rows_of(s2, k)
        root = lax.rsqrt(piv)
        r_ = s * root
        t = r_ * root
        diag = jnp.where(lane >= c0 + sub, s2 * root, 0.0)
        up.append(jnp.where(here, diag, jnp.where(lane >= c0 + 8, r_, 0.0)))
        inv.append(jnp.where(lane < c0 + 8, r_, 0.0))
        if g + 1 == n:
            break
        mk = [[rows_of(mult[k], m) if m > k else None for m in range(8)] for k in range(8)]
        tk = [rows_of(t, k) for k in range(8)]
        for b in range(g + 1, near):
            x = left[b - g - 1]
            for k in range(8):
                for m in range(k + 1, 8):
                    x[m] = x[m] - x[k] * mk[k][m]
            if b == g + 1:
                cols = ahead
                for k in range(8):
                    xs = x[k] * recip[k]
                    for m in range(8):
                        cols[m] = cols[m] - x[k] * rows_of(xs, m)
            new = jnp.where(here, 0.0, a[b])
            for k in range(8):
                new = new - x[k] * tk[k]
            a[b] = new
        wide.append(jnp.where((lane >= c0 + 8) & (lane < 8 * (g // SPAN * SPAN + SPAN)), 0.0, r_))
        if (g + 1) % SPAN == 0 and near < n:
            hi, lo = split(jnp.concatenate(wide, axis=0))
            wide = []
            both = tn32(hi, hi) + (tn32(hi, lo) + tn32(lo, hi))
            done = (lane >= c0 + 8 - 8 * SPAN) & (lane < c0 + 8)
            for b in range(near, n):
                a[b] = jnp.where(done, 0.0, a[b]) - both[8 * b : 8 * b + 8]
    return up, inv


def split(x):
    hi = x.astype(BF16)
    return hi, (x - hi.astype(F32)).astype(BF16)


def tn32(a, b):
    return lax.dot_general(a, b, TN, preferred_element_type=F32)


def tn(a, b):
    return tn32(a, b).astype(BF16)


def mm(a, b):
    return jnp.dot(a, b, preferred_element_type=F32)


def mm3(a, b):
    return mm(a[0], b[0]) + (mm(a[0], b[1]) + mm(a[1], b[0]))


def unfold(work, take):
    for r in range(NBLK):
        n = min(5, NBLK - r)
        rows = slice(r * BLK, (r + 1) * BLK)
        work[rows, r * BLK : (r + n) * BLK] = take(r, slice(0, n * BLK))
        for c in range(r + 5, NBLK):
            o = (NBLK - (c - r)) * BLK
            work[rows, c * BLK : (c + 1) * BLK] = take(c, slice(o, o + BLK)).T


def cholesky_blocks(work, lb, mh, ml, inv_s):
    def body(k, _):
        off = pl.multiple_of(k * BLK, BLK)
        rows = [work[pl.ds(pl.multiple_of(off + 8 * i, 8), 8), pl.ds(off, BLK)] for i in range(16)]
        up, inv = factor_block(rows)
        for i in range(16):
            inv_s[8 * i : 8 * i + 8, :] = inv[i]
        work[pl.ds(off, BLK), pl.ds(off, BLK)] = jnp.concatenate(up, axis=0).T
        hi, lo = split(inv_s[...])
        mh[pl.ds(off, BLK), :] = hi
        ml[pl.ds(off, BLK), :] = lo
        for kk in range(NBLK - 1):

            @pl.when(k == kk)
            def _():
                o = BLK * kk
                e = o + BLK
                upper = mm3((hi, lo), split(work[o:e, e:]))
                parts = split(upper)
                for ib in range(kk + 1, NBLK):
                    i0 = BLK * ib
                    c = i0 - e
                    low = upper[:, c : c + BLK].T
                    lows = split(low)
                    lb[i0 : i0 + BLK, o:e] = lows[0]
                    work[i0 : i0 + BLK, o:e] = low
                    work[i0 : i0 + BLK, i0:] = work[i0 : i0 + BLK, i0:] - mm3(
                        lows, (parts[0][:, c:], parts[1][:, c:])
                    )

        return 0

    lax.fori_loop(0, NBLK, body, 0)


def write_rows(place, work, lrow):
    start = pl.multiple_of(64 * (2 * place[0] + place[1]), 64)
    r = lax.broadcasted_iota(jnp.int32, (64, NB), 0) + start
    c = lax.broadcasted_iota(jnp.int32, (64, NB), 1)
    lrow[...] = jnp.where(c <= r, work[pl.ds(start, 64), :], 0.0)


def fetch(pairs, sems):
    copies = [pltpu.make_async_copy(src, dst, sems.at[n]) for n, (src, dst) in enumerate(pairs)]
    for one in copies:
        one.start()
    return copies


def first_kernel(place, raw_h, lrow, lb, mh, ml, raw, work, inv_s, sems):
    for one in fetch([(raw_h, raw)], sems):
        one.wait()
    unfold(work, lambda r, cols: raw[r * BLK : (r + 1) * BLK, cols])
    cholesky_blocks(work, lb, mh, ml, inv_s)
    write_rows(place, work, lrow)


def solve_step(k, w, lb, mh, ml, p):
    o = BLK * k
    e = o + BLK
    x = mm3((mh[o:e, :], ml[o:e, :]), split(w[o:e, :]))
    p[o:e, :] = x.astype(BF16)
    if e < NB:
        w[e:, :] = w[e:, :] - mm(lb[e:, o:e], p[o:e, :])


def second_kernel(
    place, tile_h, lb0_h, mh0_h, ml0_h, lrow, lb, mh, ml, p10, tile, lb0, mh0, ml0, work, w, inv_s, sems
):
    diag, factors = pl.ds(0, 2 * BAND), pl.ds(2 * BAND, 4 * RANK)
    copies = fetch(
        [
            (tile_h.at[:, factors], tile.at[:, factors]),
            (mh0_h, mh0),
            (ml0_h, ml0),
            (lb0_h, lb0),
            (tile_h.at[:, diag], tile.at[:, diag]),
        ],
        sems,
    )
    for one in copies[:4]:
        one.wait()
    w[:, :RANK] = tile[:, 2 * BAND + RANK : TILE1].astype(F32)
    w[:, RANK:] = tile[:, TILE1 + RANK : TILE1 + 2 * RANK].astype(F32)
    for k in range(NBLK):
        solve_step(k, w, lb0, mh0, ml0, p10)
    solved = p10[:, :RANK]
    inner = lax.dot_general(solved, solved, TN, preferred_element_type=F32).astype(BF16)
    u = tile[:, 2 * BAND : 2 * BAND + RANK]
    corr = split(mm(u, inner))

    def take(r, cols):
        rows = slice(r * BLK, (r + 1) * BLK)
        return tile[rows, cols].astype(F32) + tile[rows, cols.start + BAND : cols.stop + BAND].astype(F32)

    copies[4].wait()
    unfold(work, take)
    for r in range(NBLK):
        o = r * BLK
        right = u[o:, :]
        work[o : o + BLK, o:] = work[o : o + BLK, o:] - (
            lax.dot_general(corr[0][o : o + BLK], right, NT, preferred_element_type=F32)
            + lax.dot_general(corr[1][o : o + BLK], right, NT, preferred_element_type=F32)
        )
    cholesky_blocks(work, lb, mh, ml, inv_s)
    write_rows(place, work, lrow)


def last_kernel(place, *refs):
    parts, (tile_h, p10i_h, diag_h, lrow0_h, lrow1_h) = refs[:4], refs[4:9]
    lb0_h, mh0_h, ml0_h, lb1_h, mh1_h, ml1_h, new, upd = refs[9:17]
    (cols, rows, u10, p10i, diag, lrow0, lrow1, lb0, mh0, ml0, lb1, mh1, ml1, w0, w1, pj, p1, sems) = refs[17:]
    j = 2 * place[0] + place[1]
    i = place[2]
    x, y = i // 4, lax.rem(i, 4)
    def tile_part(n):
        return tile_h.at[:, pl.ds(TILE1 + n * RANK, RANK)], rows.at[:, pl.ds(n * RANK, RANK)]

    pairs = [tile_part(3), (tile_h.at[:, 2 * BAND : 2 * BAND + RANK], u10)]
    for b in range(4):
        for a in range(4):
            k = 4 * lax.rem(x + 4 - a, 4) + lax.rem(y + 4 - b, 4)
            pairs.append((parts[b].at[pl.ds(64 * a, 64)], cols.at[pl.ds(pl.multiple_of(64 * k, 64), 64)]))
    head = len(pairs)
    pairs += [(mh0_h, mh0), (ml0_h, ml0), (mh1_h, mh1), (ml1_h, ml1), (lb0_h, lb0), (lb1_h, lb1)]
    body = len(pairs)
    pairs += [tile_part(0), tile_part(2), (p10i_h, p10i), (diag_h, diag), (lrow0_h, lrow0), (lrow1_h, lrow1)]
    copies = fetch(pairs, sems)
    for one in copies[:head]:
        one.wait()
    w0[...] = cols[:, :RANK].astype(F32)
    w1[:, :RANK] = rows[:, 3 * RANK :].astype(F32)
    w1[:, RANK : 2 * RANK] = u10[...].astype(F32)
    w1[:, 2 * RANK :] = cols[:, RANK:].astype(F32)
    for one in copies[head:body]:
        one.wait()
    for k in range(NBLK):
        solve_step(k, w0, lb0, mh0, ml0, pj)
        solve_step(k, w1, lb1, mh1, ml1, p1)
    for one in copies[body:]:
        one.wait()
    zero = jnp.zeros((), BF16)
    pi = jnp.where(i > 0, p10i[:, RANK:], zero)
    ui = rows[:, :RANK]
    start = pl.multiple_of(64 * j, 64)
    ui_part = rows[pl.ds(start, 64), :RANK]
    inner01 = tn(pi, p10i[:, :RANK])
    c0 = mm(ui, tn(pi, pj[...])).astype(BF16)
    c01 = mm(ui, inner01).astype(BF16)
    c0_part = mm(ui_part, tn(pi, pi)).astype(BF16)
    d = diag[...] - lax.dot_general(c0_part, ui, NT, preferred_element_type=F32)
    upd[:, :RANK] = jnp.where(j == 0, pi, jnp.where((i > j) & (j > 0), c0, zero))
    q = jnp.where(i > 1, p1[...], zero)
    q_i = q[:, : 2 * RANK]
    square = tn(q_i, q_i)
    inner = jnp.concatenate([tn(q_i, q[:, 2 * RANK :]), square[:, RANK:]], axis=1)
    up = jnp.concatenate([rows[:, 2 * RANK : 3 * RANK], -c01], axis=1)
    c1 = mm(up, inner).astype(BF16)
    up_part = jnp.concatenate(
        [rows[pl.ds(start, 64), 2 * RANK : 3 * RANK], -mm(ui_part, inner01).astype(BF16)], axis=1
    )
    c1_part = mm(up_part, square).astype(BF16)
    d = d - lax.dot_general(c1_part, up, NT, preferred_element_type=F32)
    new[...] = jnp.where(i == 0, lrow0[...], jnp.where(i == 1, lrow1[...], d))
    upd[:, RANK:] = jnp.where(j == 1, q_i, jnp.where((i > j) & (j > 1), c1, zero))


def shape(rows, cols, dtype):
    return jax.ShapeDtypeStruct((rows, cols), dtype)


FACTOR = [shape(64, NB, F32), shape(NB, NB, BF16), shape(NB, BLK, BF16), shape(NB, BLK, BF16)]


def swap_core(x):
    return lax.ppermute(x, "col", [(c, c ^ 1) for c in range(16)])


def after(x, *tokens):
    return lax.optimization_barrier((x, *tokens))[0]


def at(row, col):
    return 16 * row + col


def pick(cases, default):
    for hit, x in cases:
        default = jnp.where(hit, x, default)
    return default


def spread_x(x, row_at, rows):
    got = [lax.ppermute(x, "row", [(y, 4 * k + y) for y in rows]) for k in (1, 2, 3)]
    return pick([(row_at // 4 == k, got[k - 1]) for k in (1, 2, 3)], x)


def spread_y(x, row_at, rows):
    got = [lax.ppermute(x, "row", [(4 * a + y, 4 * a + (y + s) % 4) for a in range(4) for y in rows]) for s in (1, 2, 3)]
    return [pick([(row_at % 4 == (y + s) % 4, got[s - 1]) for s in (1, 2, 3)], x) for y in rows]


def halve(x, z, gap):
    half = x.shape[0] // 2
    pairs = [(at(r, 2 * a + c), at(r, 2 * (a + gap) + c)) for r in BELOW for a in range(0, 8, 2 * gap) for c in (0, 1)]
    got = lax.ppermute(x[half:], ("row", "col"), pairs)
    return jnp.where((z // gap) % 2 == 1, got, x[:half])


def deal(cur, z, core, tokens):
    first = core == 0

    def chunk(q0, q1):
        return jnp.where(first, cur[64 * q0 : 64 * q0 + 64], cur[64 * q1 : 64 * q1 + 64])

    def send(x, step, flip):
        pairs = [(2 * a + c, 2 * (a + step) + (c ^ flip)) for a in range(0, 8, 2) for c in (0, 1)]
        return lax.ppermute(after(x, *tokens), "col", pairs)

    odd = z % 2 == 1
    same = jnp.where(odd, send(chunk(2, 3), 1, 0), chunk(0, 1))
    cross = jnp.where(odd, send(chunk(3, 2), 1, 1), send(chunk(1, 0), 0, 1))
    return jnp.where(first, same, cross), jnp.where(first, cross, same)


def shards(diag_tiles, left_factors, right_factors, ranks):
    row_at = lax.axis_index("row")
    col_at = lax.axis_index("col")
    z, core = col_at // 2, col_at % 2
    place = jnp.stack([z, core, row_at]).astype(jnp.int32)
    mine = diag_tiles[0, 0]
    keep = jnp.arange(RANK)[None, :] < ranks[0, 0, 0, 0]
    zero = jnp.zeros((), BF16)
    both = jnp.concatenate(
        [jnp.where(keep, left_factors[0, 0, 0, 0], zero), jnp.where(keep, right_factors[0, 0, 0, 0], zero)], axis=1
    )

    band = lax.dynamic_slice(jnp.concatenate([mine, mine[:, :BAND]], axis=1), (0, BLK * z), (64, BAND))
    half = halve(both, z, 4)
    band0, band1 = spread_y(spread_x(band, row_at, (0, 1)), row_at, (0, 1))
    band0, half = lax.optimization_barrier((band0, half))
    raw0 = lax.all_gather(band0, "col", tiled=True)

    part0, part1 = deal(halve(half, z, 2), z, core, ())
    (first,) = spread_y(spread_x(part0, row_at, (1,)), row_at, (1,))
    hi, lo = split(band1)
    tile = lax.all_gather(jnp.concatenate([hi, lo, first, part0, part1], axis=1), "col", tiled=True)
    flip = lax.ppermute(
        after(jnp.concatenate([part0[:, RANK:], part1[:, RANK:]], axis=1), first),
        ("row", "col"),
        [(at(r, c), at(c, r)) for r in range(16) for c in range(16)],
    )

    lrow0, lb0, mh0, ml0 = pl.pallas_call(
        first_kernel,
        out_shape=FACTOR,
        in_specs=[SMEM, ANY],
        out_specs=[VMEM] * 4,
        scratch_shapes=[
            pltpu.VMEM((NB, BAND), F32),
            pltpu.VMEM((NB, NB), F32),
            pltpu.VMEM((BLK, BLK), F32),
            pltpu.SemaphoreType.DMA((1,)),
        ],
        compiler_params=grant(56),
        name="factor_first",
    )(place, raw0)

    flip = after(flip, mh0)
    over_x = [
        lax.ppermute(flip, "row", [(4 * a + b, 4 * ((a + s) % 4) + b) for a in range(4) for b in range(4)])
        for s in (1, 2, 3)
    ]
    parts = [jnp.concatenate([flip, *over_x], axis=0)]
    for s in (1, 2, 3):
        parts.append(
            lax.ppermute(parts[0], "row", [(4 * a + b, 4 * a + (b + s) % 4) for a in range(4) for b in range(4)])
        )

    lrow1, lb1, mh1, ml1, p10i = pl.pallas_call(
        second_kernel,
        out_shape=FACTOR + [shape(NB, 2 * RANK, BF16)],
        in_specs=[SMEM] + [ANY] * 4,
        out_specs=[VMEM] * 5,
        scratch_shapes=[
            pltpu.VMEM((NB, TILE1 + 2 * RANK), BF16),
            pltpu.VMEM((NB, NB), BF16),
            pltpu.VMEM((NB, BLK), BF16),
            pltpu.VMEM((NB, BLK), BF16),
            pltpu.VMEM((NB, NB), F32),
            pltpu.VMEM((NB, 2 * RANK), F32),
            pltpu.VMEM((BLK, BLK), F32),
            pltpu.SemaphoreType.DMA((5,)),
        ],
        compiler_params=grant(56),
        name="factor_second",
    )(place, tile, lb0, mh0, ml0)
    new, upd = pl.pallas_call(
        last_kernel,
        out_shape=[shape(64, NB, F32), shape(NB, 3 * RANK, BF16)],
        in_specs=[SMEM] + [ANY] * 15,
        out_specs=[VMEM] * 2,
        scratch_shapes=[
            pltpu.VMEM((NB, 2 * RANK), BF16),
            pltpu.VMEM((NB, 4 * RANK), BF16),
            pltpu.VMEM((NB, RANK), BF16),
            pltpu.VMEM((NB, 2 * RANK), BF16),
            pltpu.VMEM((64, NB), F32),
            pltpu.VMEM((64, NB), F32),
            pltpu.VMEM((64, NB), F32),
            pltpu.VMEM((NB, NB), BF16),
            pltpu.VMEM((NB, BLK), BF16),
            pltpu.VMEM((NB, BLK), BF16),
            pltpu.VMEM((NB, NB), BF16),
            pltpu.VMEM((NB, BLK), BF16),
            pltpu.VMEM((NB, BLK), BF16),
            pltpu.VMEM((NB, RANK), F32),
            pltpu.VMEM((NB, 3 * RANK), F32),
            pltpu.VMEM((NB, RANK), BF16),
            pltpu.VMEM((NB, 3 * RANK), BF16),
            pltpu.SemaphoreType.DMA((30,)),
        ],
        compiler_params=grant(56),
        name="finish",
    )(place, *parts, tile, p10i, mine, lrow0, lrow1, lb0, mh0, ml0, lb1, mh1, ml1)
    return new[None, None], upd[None, None, None, None]


def solution(mesh):
    in_specs = (
        P(None, "row", "col", None),
        P(None, "row", None, "col", None, None),
        P(None, "row", None, "col", None, None),
        P(None, "row", None, "col"),
    )
    out_specs = (P(None, "row", "col", None), P(None, "row", None, "col", None, None))
    return jax.shard_map(shards, mesh=mesh, in_specs=in_specs, out_specs=out_specs, check_vma=False)
```

```python
import functools

import jax
import jax.numpy as jnp
from jax import lax
from jax.experimental import pallas as pl
from jax.experimental.pallas import tpu as pltpu
from jax.sharding import PartitionSpec as P

F32 = jnp.float32
BF16 = jnp.bfloat16
NB = 1024
RANK = 256
BLK = 128
NBLK = NB // BLK
BAND = 5 * BLK
SPAN = 4
BELOW = range(1, 16)
TILE1 = 2 * BAND + 2 * RANK
TN = (((0,), (0,)), ((), ()))
NT = (((1,), (1,)), ((), ()))
VMEM = pl.BlockSpec(memory_space=pltpu.VMEM)
SMEM = pl.BlockSpec(memory_space=pltpu.SMEM)
ANY = pl.BlockSpec(memory_space=pl.ANY)


def grant(mib):
    return pltpu.CompilerParams(vmem_limit_bytes=mib * 1024 * 1024)


def lanes_of(x, c):
    return jnp.broadcast_to(x[:, c : c + 1], (8, BLK))


def rows_of(x, r):
    return jnp.broadcast_to(x[r : r + 1, :], (8, BLK))


def factor_block(rows):
    sub = lax.broadcasted_iota(jnp.int32, (8, BLK), 0)
    lane = lax.broadcasted_iota(jnp.int32, (8, BLK), 1)
    a = list(rows)
    n = len(a)
    up, inv, wide = [], [], []
    cols = [lanes_of(a[0], m) for m in range(8)]
    for g in range(n):
        c0 = 8 * g
        near = min(n, g // SPAN * SPAN + 2 * SPAN)
        here = (lane >= c0) & (lane < c0 + 8)
        left = [[lanes_of(a[b], c0 + m) for m in range(8)] for b in range(g + 1, near)]
        ahead = [lanes_of(a[g + 1], c0 + 8 + m) for m in range(8)] if g + 1 < n else None
        mult, recip, piv = [], [], None
        for k in range(8):
            d = rows_of(cols[k], k)
            r = 1.0 / d
            recip.append(r)
            piv = d if piv is None else jnp.where(sub == k, d, piv)
            for m in range(k + 1, 8):
                cols[m] = cols[m] - (cols[k] * rows_of(cols[k], m)) * r
            mult.append(jnp.where(sub > k, cols[k] * r, 0.0))
        s = jnp.where(here, jnp.where(lane == c0 + sub, 1.0, 0.0), a[g])
        s2 = a[g]
        for k in range(7):
            s = s - mult[k] * rows_of(s, k)
            s2 = s2 - mult[k] * rows_of(s2, k)
        root = lax.rsqrt(piv)
        r_ = s * root
        t = r_ * root
        diag = jnp.where(lane >= c0 + sub, s2 * root, 0.0)
        up.append(jnp.where(here, diag, jnp.where(lane >= c0 + 8, r_, 0.0)))
        inv.append(jnp.where(lane < c0 + 8, r_, 0.0))
        if g + 1 == n:
            break
        mk = [[rows_of(mult[k], m) if m > k else None for m in range(8)] for k in range(8)]
        tk = [rows_of(t, k) for k in range(8)]
        for b in range(g + 1, near):
            x = left[b - g - 1]
            for k in range(8):
                for m in range(k + 1, 8):
                    x[m] = x[m] - x[k] * mk[k][m]
            if b == g + 1:
                cols = ahead
                for k in range(8):
                    xs = x[k] * recip[k]
                    for m in range(8):
                        cols[m] = cols[m] - x[k] * rows_of(xs, m)
            new = jnp.where(here, 0.0, a[b])
            for k in range(8):
                new = new - x[k] * tk[k]
            a[b] = new
        wide.append(jnp.where((lane >= c0 + 8) & (lane < 8 * (g // SPAN * SPAN + SPAN)), 0.0, r_))
        if (g + 1) % SPAN == 0 and near < n:
            hi, lo = split(jnp.concatenate(wide, axis=0))
            wide = []
            both = tn32(jnp.concatenate([hi, hi, lo], axis=0), jnp.concatenate([hi, lo, hi], axis=0))
            done = (lane >= c0 + 8 - 8 * SPAN) & (lane < c0 + 8)
            for b in range(near, n):
                a[b] = jnp.where(done, 0.0, a[b]) - both[8 * b : 8 * b + 8]
    return up, inv


def split(x):
    hi = x.astype(BF16)
    return hi, (x - hi.astype(F32)).astype(BF16)


def tn32(a, b):
    return lax.dot_general(a, b, TN, preferred_element_type=F32)


def tn(a, b):
    return tn32(a, b).astype(BF16)


def mm(a, b):
    return jnp.dot(a, b, preferred_element_type=F32)


def mm3(a, b):
    return mm(jnp.concatenate([a[0], a[0], a[1]], axis=1), jnp.concatenate([b[0], b[1], b[0]], axis=0))


def unfold(work, take):
    for r in range(NBLK):
        n = min(5, NBLK - r)
        rows = slice(r * BLK, (r + 1) * BLK)
        work[rows, r * BLK : (r + n) * BLK] = take(r, slice(0, n * BLK))
        for c in range(r + 5, NBLK):
            o = (NBLK - (c - r)) * BLK
            work[rows, c * BLK : (c + 1) * BLK] = take(c, slice(o, o + BLK)).T


def cholesky_blocks(work, lb, mh, ml, inv_s):
    def body(k, _):
        off = pl.multiple_of(k * BLK, BLK)
        rows = [work[pl.ds(pl.multiple_of(off + 8 * i, 8), 8), pl.ds(off, BLK)] for i in range(16)]
        up, inv = factor_block(rows)
        for i in range(16):
            inv_s[8 * i : 8 * i + 8, :] = inv[i]
        work[pl.ds(off, BLK), pl.ds(off, BLK)] = jnp.concatenate(up, axis=0).T
        hi, lo = split(inv_s[...])
        mh[pl.ds(off, BLK), :] = hi
        ml[pl.ds(off, BLK), :] = lo
        for kk in range(NBLK - 1):

            @pl.when(k == kk)
            def _():
                o = BLK * kk
                e = o + BLK
                upper = mm3((hi, lo), split(work[o:e, e:]))
                parts = split(upper)
                for ib in range(kk + 1, NBLK):
                    i0 = BLK * ib
                    c = i0 - e
                    low = upper[:, c : c + BLK].T
                    lows = split(low)
                    lb[i0 : i0 + BLK, o:e] = lows[0]
                    work[i0 : i0 + BLK, o:e] = low
                    work[i0 : i0 + BLK, i0:] = work[i0 : i0 + BLK, i0:] - mm3(
                        lows, (parts[0][:, c:], parts[1][:, c:])
                    )

        return 0

    lax.fori_loop(0, NBLK, body, 0)


def write_rows(place, work, lrow):
    start = pl.multiple_of(64 * (2 * place[0] + place[1]), 64)
    r = lax.broadcasted_iota(jnp.int32, (64, NB), 0) + start
    c = lax.broadcasted_iota(jnp.int32, (64, NB), 1)
    lrow[...] = jnp.where(c <= r, work[pl.ds(start, 64), :], 0.0)


def fetch(pairs, sems):
    copies = [pltpu.make_async_copy(src, dst, sems.at[n]) for n, (src, dst) in enumerate(pairs)]
    for one in copies:
        one.start()
    return copies


def first_kernel(place, raw_h, lrow, lb, mh, ml, raw, work, inv_s, sems):
    for one in fetch([(raw_h, raw)], sems):
        one.wait()
    unfold(work, lambda r, cols: raw[r * BLK : (r + 1) * BLK, cols])
    cholesky_blocks(work, lb, mh, ml, inv_s)
    write_rows(place, work, lrow)


def solve_step(k, w, lb, mh, ml, p):
    o = BLK * k
    e = o + BLK
    x = mm3((mh[o:e, :], ml[o:e, :]), split(w[o:e, :]))
    p[o:e, :] = x.astype(BF16)
    if e < NB:
        w[e:, :] = w[e:, :] - mm(lb[e:, o:e], p[o:e, :])


def second_kernel(
    place, tile_h, lb0_h, mh0_h, ml0_h, lrow, lb, mh, ml, p10, tile, lb0, mh0, ml0, work, w, inv_s, sems
):
    diag, factors = pl.ds(0, 2 * BAND), pl.ds(2 * BAND, 4 * RANK)
    copies = fetch(
        [
            (tile_h.at[:, factors], tile.at[:, factors]),
            (mh0_h, mh0),
            (ml0_h, ml0),
            (lb0_h, lb0),
            (tile_h.at[:, diag], tile.at[:, diag]),
        ],
        sems,
    )
    for one in copies[:4]:
        one.wait()
    w[:, :RANK] = tile[:, 2 * BAND + RANK : TILE1].astype(F32)
    w[:, RANK:] = tile[:, TILE1 + RANK : TILE1 + 2 * RANK].astype(F32)
    for k in range(NBLK):
        solve_step(k, w, lb0, mh0, ml0, p10)
    solved = p10[:, :RANK]
    inner = lax.dot_general(solved, solved, TN, preferred_element_type=F32).astype(BF16)
    u = tile[:, 2 * BAND : 2 * BAND + RANK]
    corr = split(mm(u, inner))

    def take(r, cols):
        rows = slice(r * BLK, (r + 1) * BLK)
        return tile[rows, cols].astype(F32) + tile[rows, cols.start + BAND : cols.stop + BAND].astype(F32)

    copies[4].wait()
    unfold(work, take)
    for r in range(NBLK):
        o = r * BLK
        right = u[o:, :]
        work[o : o + BLK, o:] = work[o : o + BLK, o:] - (
            lax.dot_general(corr[0][o : o + BLK], right, NT, preferred_element_type=F32)
            + lax.dot_general(corr[1][o : o + BLK], right, NT, preferred_element_type=F32)
        )
    cholesky_blocks(work, lb, mh, ml, inv_s)
    write_rows(place, work, lrow)


def last_kernel(place, *refs):
    parts, (tile_h, p10i_h, diag_h, lrow0_h, lrow1_h) = refs[:4], refs[4:9]
    lb0_h, mh0_h, ml0_h, lb1_h, mh1_h, ml1_h, new, upd = refs[9:17]
    (cols, rows, u10, p10i, diag, lrow0, lrow1, lb0, mh0, ml0, lb1, mh1, ml1, w0, w1, pj, p1, sems) = refs[17:]
    j = 2 * place[0] + place[1]
    i = place[2]
    x, y = i // 4, lax.rem(i, 4)
    def tile_part(n):
        return tile_h.at[:, pl.ds(TILE1 + n * RANK, RANK)], rows.at[:, pl.ds(n * RANK, RANK)]

    pairs = [tile_part(3), (tile_h.at[:, 2 * BAND : 2 * BAND + RANK], u10)]
    for b in range(4):
        for a in range(4):
            k = 4 * lax.rem(x + 4 - a, 4) + lax.rem(y + 4 - b, 4)
            pairs.append((parts[b].at[pl.ds(64 * a, 64)], cols.at[pl.ds(pl.multiple_of(64 * k, 64), 64)]))
    head = len(pairs)
    pairs += [(mh0_h, mh0), (ml0_h, ml0), (mh1_h, mh1), (ml1_h, ml1), (lb0_h, lb0), (lb1_h, lb1)]
    body = len(pairs)
    pairs += [tile_part(0), tile_part(2), (p10i_h, p10i), (diag_h, diag), (lrow0_h, lrow0), (lrow1_h, lrow1)]
    copies = fetch(pairs, sems)
    for one in copies[:head]:
        one.wait()
    w0[...] = cols[:, :RANK].astype(F32)
    w1[:, :RANK] = rows[:, 3 * RANK :].astype(F32)
    w1[:, RANK : 2 * RANK] = u10[...].astype(F32)
    w1[:, 2 * RANK :] = cols[:, RANK:].astype(F32)
    for one in copies[head:body]:
        one.wait()
    for k in range(NBLK):
        solve_step(k, w0, lb0, mh0, ml0, pj)
        solve_step(k, w1, lb1, mh1, ml1, p1)
    for one in copies[body:]:
        one.wait()
    zero = jnp.zeros((), BF16)
    pi = jnp.where(i > 0, p10i[:, RANK:], zero)
    ui = rows[:, :RANK]
    start = pl.multiple_of(64 * j, 64)
    ui_part = rows[pl.ds(start, 64), :RANK]
    inner01 = tn(pi, p10i[:, :RANK])
    c0 = mm(ui, tn(pi, pj[...])).astype(BF16)
    c01 = mm(ui, inner01).astype(BF16)
    c0_part = mm(ui_part, tn(pi, pi)).astype(BF16)
    d = diag[...] - lax.dot_general(c0_part, ui, NT, preferred_element_type=F32)
    upd[:, :RANK] = jnp.where(j == 0, pi, jnp.where((i > j) & (j > 0), c0, zero))
    q = jnp.where(i > 1, p1[...], zero)
    q_i = q[:, : 2 * RANK]
    square = tn(q_i, q_i)
    inner = jnp.concatenate([tn(q_i, q[:, 2 * RANK :]), square[:, RANK:]], axis=1)
    up = jnp.concatenate([rows[:, 2 * RANK : 3 * RANK], -c01], axis=1)
    c1 = mm(up, inner).astype(BF16)
    up_part = jnp.concatenate(
        [rows[pl.ds(start, 64), 2 * RANK : 3 * RANK], -mm(ui_part, inner01).astype(BF16)], axis=1
    )
    c1_part = mm(up_part, square).astype(BF16)
    d = d - lax.dot_general(c1_part, up, NT, preferred_element_type=F32)
    new[...] = jnp.where(i == 0, lrow0[...], jnp.where(i == 1, lrow1[...], d))
    upd[:, RANK:] = jnp.where(j == 1, q_i, jnp.where((i > j) & (j > 1), c1, zero))


def shape(rows, cols, dtype):
    return jax.ShapeDtypeStruct((rows, cols), dtype)


FACTOR = [shape(64, NB, F32), shape(NB, NB, BF16), shape(NB, BLK, BF16), shape(NB, BLK, BF16)]


def swap_core(x):
    return lax.ppermute(x, "col", [(c, c ^ 1) for c in range(16)])


def after(x, *tokens):
    return lax.optimization_barrier((x, *tokens))[0]


def at(row, col):
    return 16 * row + col


def pick(cases, default):
    for hit, x in cases:
        default = jnp.where(hit, x, default)
    return default


def spread_x(x, row_at, rows):
    got = [lax.ppermute(x, "row", [(y, 4 * k + y) for y in rows]) for k in (1, 2, 3)]
    return pick([(row_at // 4 == k, got[k - 1]) for k in (1, 2, 3)], x)


def spread_y(x, row_at, rows):
    got = [lax.ppermute(x, "row", [(4 * a + y, 4 * a + (y + s) % 4) for a in range(4) for y in rows]) for s in (1, 2, 3)]
    return [pick([(row_at % 4 == (y + s) % 4, got[s - 1]) for s in (1, 2, 3)], x) for y in rows]


def halve(x, z, gap):
    half = x.shape[0] // 2
    pairs = [(at(r, 2 * a + c), at(r, 2 * (a + gap) + c)) for r in BELOW for a in range(0, 8, 2 * gap) for c in (0, 1)]
    got = lax.ppermute(x[half:], ("row", "col"), pairs)
    return jnp.where((z // gap) % 2 == 1, got, x[:half])


def deal(cur, z, core, tokens):
    first = core == 0

    def chunk(q0, q1):
        return jnp.where(first, cur[64 * q0 : 64 * q0 + 64], cur[64 * q1 : 64 * q1 + 64])

    def send(x, step, flip):
        pairs = [(2 * a + c, 2 * (a + step) + (c ^ flip)) for a in range(0, 8, 2) for c in (0, 1)]
        return lax.ppermute(after(x, *tokens), "col", pairs)

    odd = z % 2 == 1
    same = jnp.where(odd, send(chunk(2, 3), 1, 0), chunk(0, 1))
    cross = jnp.where(odd, send(chunk(3, 2), 1, 1), send(chunk(1, 0), 0, 1))
    return jnp.where(first, same, cross), jnp.where(first, cross, same)


def shards(diag_tiles, left_factors, right_factors, ranks):
    row_at = lax.axis_index("row")
    col_at = lax.axis_index("col")
    z, core = col_at // 2, col_at % 2
    place = jnp.stack([z, core, row_at]).astype(jnp.int32)
    mine = diag_tiles[0, 0]
    keep = jnp.arange(RANK)[None, :] < ranks[0, 0, 0, 0]
    zero = jnp.zeros((), BF16)
    both = jnp.concatenate(
        [jnp.where(keep, left_factors[0, 0, 0, 0], zero), jnp.where(keep, right_factors[0, 0, 0, 0], zero)], axis=1
    )

    band = lax.dynamic_slice(jnp.concatenate([mine, mine[:, :BAND]], axis=1), (0, BLK * z), (64, BAND))
    half = halve(both, z, 4)
    band0, band1 = spread_y(spread_x(band, row_at, (0, 1)), row_at, (0, 1))
    band0, half = lax.optimization_barrier((band0, half))
    raw0 = lax.all_gather(band0, "col", tiled=True)

    part0, part1 = deal(halve(half, z, 2), z, core, ())
    (first,) = spread_y(spread_x(part0, row_at, (1,)), row_at, (1,))
    hi, lo = split(band1)
    tile = lax.all_gather(jnp.concatenate([hi, lo, first, part0, part1], axis=1), "col", tiled=True)
    flip = lax.ppermute(
        after(jnp.concatenate([part0[:, RANK:], part1[:, RANK:]], axis=1), first),
        ("row", "col"),
        [(at(r, c), at(c, r)) for r in range(16) for c in range(16)],
    )

    lrow0, lb0, mh0, ml0 = pl.pallas_call(
        first_kernel,
        out_shape=FACTOR,
        in_specs=[SMEM, ANY],
        out_specs=[VMEM] * 4,
        scratch_shapes=[
            pltpu.VMEM((NB, BAND), F32),
            pltpu.VMEM((NB, NB), F32),
            pltpu.VMEM((BLK, BLK), F32),
            pltpu.SemaphoreType.DMA((1,)),
        ],
        compiler_params=grant(56),
        name="factor_first",
    )(place, raw0)

    flip = after(flip, mh0)
    over_x = [
        lax.ppermute(flip, "row", [(4 * a + b, 4 * ((a + s) % 4) + b) for a in range(4) for b in range(4)])
        for s in (1, 2, 3)
    ]
    parts = [jnp.concatenate([flip, *over_x], axis=0)]
    for s in (1, 2, 3):
        parts.append(
            lax.ppermute(parts[0], "row", [(4 * a + b, 4 * a + (b + s) % 4) for a in range(4) for b in range(4)])
        )

    lrow1, lb1, mh1, ml1, p10i = pl.pallas_call(
        second_kernel,
        out_shape=FACTOR + [shape(NB, 2 * RANK, BF16)],
        in_specs=[SMEM] + [ANY] * 4,
        out_specs=[VMEM] * 5,
        scratch_shapes=[
            pltpu.VMEM((NB, TILE1 + 2 * RANK), BF16),
            pltpu.VMEM((NB, NB), BF16),
            pltpu.VMEM((NB, BLK), BF16),
            pltpu.VMEM((NB, BLK), BF16),
            pltpu.VMEM((NB, NB), F32),
            pltpu.VMEM((NB, 2 * RANK), F32),
            pltpu.VMEM((BLK, BLK), F32),
            pltpu.SemaphoreType.DMA((5,)),
        ],
        compiler_params=grant(56),
        name="factor_second",
    )(place, tile, lb0, mh0, ml0)
    new, upd = pl.pallas_call(
        last_kernel,
        out_shape=[shape(64, NB, F32), shape(NB, 3 * RANK, BF16)],
        in_specs=[SMEM] + [ANY] * 15,
        out_specs=[VMEM] * 2,
        scratch_shapes=[
            pltpu.VMEM((NB, 2 * RANK), BF16),
            pltpu.VMEM((NB, 4 * RANK), BF16),
            pltpu.VMEM((NB, RANK), BF16),
            pltpu.VMEM((NB, 2 * RANK), BF16),
            pltpu.VMEM((64, NB), F32),
            pltpu.VMEM((64, NB), F32),
            pltpu.VMEM((64, NB), F32),
            pltpu.VMEM((NB, NB), BF16),
            pltpu.VMEM((NB, BLK), BF16),
            pltpu.VMEM((NB, BLK), BF16),
            pltpu.VMEM((NB, NB), BF16),
            pltpu.VMEM((NB, BLK), BF16),
            pltpu.VMEM((NB, BLK), BF16),
            pltpu.VMEM((NB, RANK), F32),
            pltpu.VMEM((NB, 3 * RANK), F32),
            pltpu.VMEM((NB, RANK), BF16),
            pltpu.VMEM((NB, 3 * RANK), BF16),
            pltpu.SemaphoreType.DMA((30,)),
        ],
        compiler_params=grant(56),
        name="finish",
    )(place, *parts, tile, p10i, mine, lrow0, lrow1, lb0, mh0, ml0, lb1, mh1, ml1)
    return new[None, None], upd[None, None, None, None]


def solution(mesh):
    in_specs = (
        P(None, "row", "col", None),
        P(None, "row", None, "col", None, None),
        P(None, "row", None, "col", None, None),
        P(None, "row", None, "col"),
    )
    out_specs = (P(None, "row", "col", None), P(None, "row", None, "col", None, None))
    return jax.shard_map(shards, mesh=mesh, in_specs=in_specs, out_specs=out_specs, check_vma=False)
```
